32 devices in a mesh: parts: 2 (over x), leaf: 16 (over z, y, core).
Axes of the slice: x: 2, y: 2, z: 4, core: 2. Of those that a mesh axis runs over, the one named last changes fastest.
Arguments:
- samples: bfloat16 [64, 8, 8192], P(None, None, ('parts', 'leaf')), parts along dimension 2, may hold values from -6 to 6
- interp_in: bfloat16 [32, 64, 8192], P(None, None, ('parts', 'leaf')), parts along dimension 2, may hold values from -0.75 to 0.75
- top_blocks: bfloat16 [4, 32, 64, 8192], P(None, None, None, ('parts', 'leaf')), parts along dimension 3, may hold values from -0.875 to 0.875
- top_pattern: int32 [4, 2, 8192], P(None, None, ('parts', 'leaf')), parts along dimension 2, may hold values 0 or 1
- bottom_blocks: bfloat16 [4, 32, 64, 8192], P(None, None, None, ('parts', 'leaf')), parts along dimension 3, may hold values from -0.875 to 0.875
- bottom_pattern: int32 [4, 2, 8192], P(None, None, ('parts', 'leaf')), parts along dimension 2, may hold values 0 or 1
- interp_out: bfloat16 [64, 32, 8192], P(None, None, ('parts', 'leaf')), parts along dimension 2, may hold values from -1 to 1
Outputs:
- image: bfloat16 [64, 8, 8192], P(None, None, ('parts', 'leaf')), parts along dimension 2
The draws below stay inside these ranges and needn't reach their ends.
There are 2 independent parts, one for each index of `parts`. The reference program is written for one: setup_inputs(seed, part) draws one part's arguments, and reference() takes and returns one part's arrays. A program takes and returns all parts, laid end to end along the dimension named above; each array names one. Nothing has to cross between parts.
All inputs are finite; a program needn't handle non-finite values. No bound on the sum of `top_pattern` or of `bottom_pattern` on one device may be relied on, other than what follows from the above.
Results may differ from the reference program's by a relative error of at most 0.0094.
Values may be sent and summed in bfloat16 or wider, within the bound.
No kernel may reach another device: no remote copies, remote signals or barrier semaphores. Data moves between devices by JAX's collectives and lax.ppermute only.
A program may use at most 64 MiB of HBM per device.

```python
import jax
import jax.numpy as jnp

K = 32
R = 8
P_SIZE = 64
Q = 64
SW = 4
BOX_DEV = 256
NBOX = 4096
LEAF_BITS = 4
N_LEAF = 16


def touch_ends(values, stream_key, least, top_value):
    longest = values.shape.index(max(values.shape))
    spots = []
    for shift in (0, 1):
        where = [jax.random.randint(jax.random.fold_in(stream_key, axis), (), 0, length) for axis, length in enumerate(values.shape)]
        where[longest] = (where[longest] + shift) % values.shape[longest]
        spots.append(tuple(where))
    return values.at[spots[0]].set(least).at[spots[1]].set(top_value)


def level_of(stream_key, shape, pieces, least, top_value):
    gain, own = 1.0, jax.random.fold_in(stream_key, 6)
    for dim, blocks in pieces:
        heights = jnp.exp(jax.random.uniform(jax.random.fold_in(own, dim), (blocks,), jnp.float32, least / len(pieces), top_value / len(pieces)))
        gain = gain * jnp.repeat(heights, shape[dim] // blocks).reshape([-1 if axis == dim else 1 for axis in range(len(shape))])
    return gain


def centred(key, extent, scale, reach, shards=(), kind=jnp.bfloat16):
    factor_of = level_of(key, extent, shards, -0.22, 0.18) if shards else 1.0
    drawn = jax.random.normal(key, extent, jnp.float32) * scale * factor_of
    return jnp.minimum(jnp.maximum(drawn, -reach), reach).astype(kind)


def setup_inputs(seed: int = 0, part: int = 0) -> dict:
    key_list = jax.random.split(jax.random.key(seed), 8)
    own_keys = jax.random.split(jax.random.fold_in(key_list[7], part), 8)
    samples = centred(own_keys[0], (P_SIZE, R, NBOX), 1.0, 6.0, ((2, 16),))
    interp_in = centred(own_keys[1], (K, P_SIZE, NBOX), P_SIZE ** -0.5, 0.75, ((2, 16),))
    top_blocks = centred(own_keys[2], (SW, K, 2 * K, NBOX), (3 * K // 2) ** -0.5, 0.875, ((3, 16),))
    top_pattern = touch_ends((jax.random.randint(own_keys[3], (SW, 2, NBOX), 0, 4) < 3).astype(jnp.int32), jax.random.fold_in(own_keys[3], 1), 0, 1)
    bottom_blocks = centred(own_keys[4], (SW, K, 2 * K, NBOX), (3 * K // 2) ** -0.5, 0.875, ((3, 16),))
    bottom_pattern = touch_ends((jax.random.randint(own_keys[5], (SW, 2, NBOX), 0, 4) < 3).astype(jnp.int32), jax.random.fold_in(own_keys[5], 1), 0, 1)
    interp_out = centred(own_keys[6], (Q, K, NBOX), K ** -0.5, 1.0, ((2, 16),))
    return {"samples": samples, "interp_in": interp_in, "top_blocks": top_blocks, "top_pattern": top_pattern, "bottom_blocks": bottom_blocks, "bottom_pattern": bottom_pattern, "interp_out": interp_out}


def apply_pattern(blocks, pattern):
    rank_size = blocks.shape[0]
    present = jnp.repeat(pattern, rank_size, axis=0).astype(jnp.float32)
    return blocks.astype(jnp.float32) * present[None]


def pair_level(current, weights, stride):
    rank_size, rhs_count, box_count = current.shape
    groups = box_count // (2 * stride)
    grouped = current.astype(jnp.float32).reshape(rank_size, rhs_count, groups, 2, stride)
    paired = jnp.concatenate([grouped[:, :, :, 0], grouped[:, :, :, 1]], axis=0)
    folded = weights.reshape(rank_size, 2 * rank_size, groups, 2, stride)
    result = jnp.einsum('ijgch,jrgh->irgch', folded, paired)
    return result.reshape(rank_size, rhs_count, box_count).astype(jnp.bfloat16)


def reference(samples, interp_in, top_blocks, top_pattern, bottom_blocks, bottom_pattern, interp_out):
    current = jnp.einsum('kpb,prb->krb', interp_in.astype(jnp.float32), samples.astype(jnp.float32)).astype(jnp.bfloat16)
    for level in range(SW):
        weights = apply_pattern(top_blocks[level], top_pattern[level])
        current = pair_level(current, weights, BOX_DEV * 2 ** (LEAF_BITS - 1 - level))
    slot_width = BOX_DEV // N_LEAF
    current = current.reshape(K, R, N_LEAF, N_LEAF, slot_width).transpose(0, 1, 3, 2, 4).reshape(K, R, NBOX)
    for level in range(SW):
        weights = apply_pattern(bottom_blocks[level], bottom_pattern[level])
        current = pair_level(current, weights, BOX_DEV * 2 ** level)
    result = jnp.einsum('qkb,krb->qrb', interp_out.astype(jnp.float32), current.astype(jnp.float32))
    return result.astype(jnp.bfloat16)
```

```python
import functools

import jax
import jax.numpy as jnp
from jax import lax
from jax.experimental import pallas as pl
from jax.experimental.pallas import tpu as pltpu
from jax.sharding import PartitionSpec as P

CHUNKS = 2


def swapped(value, axis, apart):
    mask = 2**apart
    pairs = [(source, source ^ mask) for source in range(lax.axis_size(axis))]
    return lax.ppermute(value, axis, pairs)


def contract(weights, state):
    product = weights[:, :, None].astype(jnp.float32) * state[None].astype(jnp.float32)
    return jnp.sum(product, axis=1)


def half_of(blocks, pattern, half, box_slice):
    rank_size = blocks.shape[0]
    part = lax.dynamic_slice_in_dim(blocks, half * rank_size, rank_size, axis=1)
    present = lax.dynamic_index_in_dim(pattern, half, axis=0, keepdims=False)
    return part[:, :, box_slice], present[box_slice].astype(jnp.float32)


def level_step(states, blocks, pattern, bit, leaf_place):
    own = leaf_place // 2**bit % 2
    chunk = states[0].shape[2]
    partners = [swapped(state, "leaf", bit) for state in states]
    out = []
    for place, (state, partner) in enumerate(zip(states, partners)):
        boxes = slice(place * chunk, (place + 1) * chunk)
        own_blocks, own_present = half_of(blocks, pattern, own, boxes)
        far_blocks, far_present = half_of(blocks, pattern, 1 - own, boxes)
        near = contract(own_blocks, state) * own_present
        far = contract(far_blocks, partner) * far_present
        out.append((near + far).astype(jnp.bfloat16))
    return out


def exchange_groups(tile, slot, fold):
    lane_group = lax.broadcasted_iota(jnp.int32, tile.shape[1:], 2) // slot
    pieces = [tile[index] for index in range(fold)]
    width = tile.shape[-1]
    step = 1
    while step < fold:
        low = (lane_group // step) % 2 == 0
        fresh = list(pieces)
        for index in range(fold):
            if index & step:
                continue
            first, second = pieces[index], pieces[index + step]
            fresh[index] = jnp.where(low, first, pltpu.roll(second, step * slot, 2))
            fresh[index + step] = jnp.where(low, pltpu.roll(first, width - step * slot, 2), second)
        pieces = fresh
        step *= 2
    return pieces


def pack_kernel(slot, fold, *refs):
    count = len(refs) // 2
    for source, target in zip(refs[:count], refs[count:]):
        rank_size, rhs_count, width = source.shape
        tile = source[...].astype(jnp.float32).reshape(fold, rank_size // fold, rhs_count, width)
        for index, piece in enumerate(exchange_groups(tile, slot, fold)):
            target[index] = piece.astype(jnp.bfloat16)


def unpack_kernel(slot, fold, *refs):
    count = len(refs) // 2
    for source, target in zip(refs[:count], refs[count:]):
        rank_size, rhs_count, width = target.shape
        tile = source[...].astype(jnp.float32)
        rows = rank_size // fold
        for index, piece in enumerate(exchange_groups(tile, slot, fold)):
            target[index * rows:(index + 1) * rows] = piece.astype(jnp.bfloat16)


def switch_boxes(states, leaf_count):
    rank_size, rhs_count, chunk = states[0].shape
    slot = len(states) * chunk // leaf_count
    fold = chunk // slot
    rows = rank_size // fold
    whole = pl.BlockSpec(memory_space=pltpu.VMEM)
    packed = pl.pallas_call(
        functools.partial(pack_kernel, slot, fold),
        out_shape=[jax.ShapeDtypeStruct((fold, rows, rhs_count, chunk), jnp.bfloat16)] * len(states),
        in_specs=[whole] * len(states),
        out_specs=[whole] * len(states),
    )(*states)
    joined = jnp.concatenate(packed, axis=0)
    moved = lax.all_to_all(joined, "leaf", split_axis=0, concat_axis=0, tiled=True)
    parts = jnp.split(moved, len(states), axis=0)
    return pl.pallas_call(
        functools.partial(unpack_kernel, slot, fold),
        out_shape=[jax.ShapeDtypeStruct((rank_size, rhs_count, chunk), jnp.bfloat16)] * len(states),
        in_specs=[whole] * len(states),
        out_specs=[whole] * len(states),
    )(*parts)


def plain_switch(states):
    joined = jnp.concatenate(states, axis=2)
    rank_size, rhs_count, box_count = joined.shape
    flat = joined.reshape(rank_size * rhs_count, box_count)
    moved = lax.all_to_all(flat, "leaf", split_axis=1, concat_axis=1, tiled=True)
    moved = moved.reshape(rank_size, rhs_count, box_count)
    return jnp.split(moved, len(states), axis=2)


def local(samples, interp_in, top_blocks, top_pattern, bottom_blocks, bottom_pattern, interp_out):
    level_count = top_blocks.shape[0]
    rank_size = interp_in.shape[0]
    box_count = samples.shape[2]
    leaf_count = lax.axis_size("leaf")
    bit_count = leaf_count.bit_length() - 1
    leaf_place = lax.axis_index("leaf")
    chunk = box_count // CHUNKS
    parts = [slice(place * chunk, (place + 1) * chunk) for place in range(CHUNKS)]
    states = [contract(interp_in[:, :, part], samples[:, :, part]).astype(jnp.bfloat16) for part in parts]
    for level in range(level_count):
        bit = bit_count - 1 - level
        states = level_step(states, top_blocks[level], top_pattern[level], bit, leaf_place)
    slot = box_count // leaf_count
    fold = chunk // slot
    if chunk == 128 and fold <= rank_size:
        states = switch_boxes(states, leaf_count)
    else:
        states = plain_switch(states)
    for level in range(level_count):
        states = level_step(states, bottom_blocks[level], bottom_pattern[level], level, leaf_place)
    images = [contract(interp_out[:, :, part], state) for part, state in zip(parts, states)]
    return jnp.concatenate(images, axis=2).astype(jnp.bfloat16)


def solution(mesh):
    boxes = ("parts", "leaf")
    return jax.shard_map(
        local,
        mesh=mesh,
        in_specs=(
            P(None, None, boxes),
            P(None, None, boxes),
            P(None, None, None, boxes),
            P(None, None, boxes),
            P(None, None, None, boxes),
            P(None, None, boxes),
            P(None, None, boxes),
        ),
        out_specs=P(None, None, boxes),
        check_vma=False,
    )
```

```python
import functools

import jax
import jax.numpy as jnp
from jax import lax
from jax.experimental import pallas as pl
from jax.experimental.pallas import tpu as pltpu
from jax.sharding import PartitionSpec as P

LANES = 128
GROUP = 4


def digits():
    place = lax.axis_index("leaf")
    return lax.rem(place // 8, 2), lax.rem(place // 4, 2), lax.rem(place // 2, 2), lax.rem(place, 2)


def lanes_of(chunk):
    return pl.ds(pl.multiple_of(chunk * LANES, LANES), LANES)


def rows_of(half, rank):
    return pl.ds(pl.multiple_of(half * rank, rank), rank)


def spread(wide, load, row_count, rank):
    def body(step, carry):
        rows = load(step * GROUP).astype(jnp.float32)
        wide[pl.ds(step * GROUP * rank, GROUP * rank), :] = rows.reshape(GROUP * rank, LANES)
        return carry

    lax.fori_loop(0, row_count // GROUP, body, 0)


def multiply(wide, state, row_count, emit):
    rank = len(state)

    def body(step, carry):
        for inner in range(GROUP):
            sums = [None, None]
            for index in range(rank):
                weight = wide[pl.ds(step * GROUP * rank + inner * rank + index, 8, stride=0), :]
                term = weight * state[index]
                old = sums[index % 2]
                sums[index % 2] = term if old is None else old + term
            emit(step * GROUP + inner, sums[0] + sums[1])
        return carry

    lax.fori_loop(0, row_count // GROUP, body, 0)


def state_rows(ref, present=None):
    rows = [ref[index].astype(jnp.float32) for index in range(ref.shape[0])]
    return rows if present is None else [row * present for row in rows]


def level_load(blocks, level, half, chunk):
    rank = blocks.shape[1]
    return lambda row: blocks[level, pl.ds(row, GROUP), rows_of(half, rank), lanes_of(chunk)]


def present_of(pattern, level, half, chunk):
    pair = [pattern[level, place:place + 1, lanes_of(chunk)].astype(jnp.float32) for place in range(2)]
    return jnp.where(half == 0, pair[0], pair[1])


def coeff_kernel(flip, interp, samples, out, wide, total):
    rank, depth = interp.shape[0], interp.shape[1] // 2
    chunk = digits()[3] ^ flip
    for half in range(2):
        spread(wide, lambda row: interp[pl.ds(row, GROUP), pl.ds(half * depth, depth), lanes_of(chunk)], rank, depth)
        state = [samples[half * depth + index, :, lanes_of(chunk)].astype(jnp.float32) for index in range(depth)]

        def emit(row, value):
            if half == 0:
                total[row] = value
            else:
                out[row] = (total[row] + value).astype(jnp.bfloat16)

        multiply(wide, state, rank, emit)


def near_kernel(level, bit, flip, blocks, pattern, state, out, wide):
    places = digits()
    chunk, own = places[3] ^ flip, places[3 - bit]
    spread(wide, level_load(blocks, level, own, chunk), blocks.shape[1], blocks.shape[1])

    def emit(row, value):
        out[row] = value

    multiply(wide, state_rows(state, present_of(pattern, level, own, chunk)), blocks.shape[1], emit)


def far_kernel(level, bit, flip, blocks, pattern, partner, near, out, wide):
    places = digits()
    chunk, other = places[3] ^ flip, 1 - places[3 - bit]
    spread(wide, level_load(blocks, level, other, chunk), blocks.shape[1], blocks.shape[1])

    def emit(row, value):
        out[row] = (near[row] + value).astype(jnp.bfloat16)

    multiply(wide, state_rows(partner, present_of(pattern, level, other, chunk)), blocks.shape[1], emit)


def share_kernel(top_level, top_blocks, top_pattern, bottom_blocks, bottom_pattern, after, out):
    rank = top_blocks.shape[1]
    chunk = 1 - digits()[3]
    for place, (blocks, pattern, level) in enumerate(((top_blocks, top_pattern, top_level), (bottom_blocks, bottom_pattern, 0))):
        for half in range(2):
            present = present_of(pattern, level, half, chunk)[None]

            def body(row, carry):
                rows = blocks[level, pl.ds(row, 1), half * rank:(half + 1) * rank, lanes_of(chunk)]
                out[place, pl.ds(row, 1), half * rank:(half + 1) * rank, :] = (rows.astype(jnp.float32) * present).astype(jnp.bfloat16)
                return carry

            lax.fori_loop(0, rank, body, 0)


def swap_groups(tile, slot):
    lane_group = lax.broadcasted_iota(jnp.int32, tile[0].shape, 2) // slot
    step = 1
    while step < len(tile):
        low = (lane_group // step) % 2 == 0
        fresh = list(tile)
        for place in range(len(tile)):
            if place & step == 0:
                first, second = tile[place], tile[place + step]
                fresh[place] = jnp.where(low, first, pltpu.roll(second, step * slot, 2))
                fresh[place + step] = jnp.where(low, pltpu.roll(first, LANES - step * slot, 2), second)
        tile = fresh
        step *= 2
    return tile


def pair_near_kernel(level, blocks, pattern, shared, state, out, wide):
    rank = blocks.shape[1]
    core = digits()[3]
    rows = state_rows(state)
    present = present_of(pattern, level, core, core)
    for box in range(2):
        load = (
            level_load(blocks, level, core, core)
            if box == 0
            else lambda row: shared[0, pl.ds(row, GROUP), rows_of(core, rank), :]
        )
        spread(wide, load, rank, rank)

        def emit(row, value):
            out[box, row] = value

        multiply(wide, [row * present for row in rows] if box == 0 else rows, rank, emit)


def pair_far_kernel(level, slot, blocks, pattern, shared, partner, near, *rest):
    outs, (wide, total, packed) = rest[:4], rest[4:]
    rank = blocks.shape[1]
    _, mid, low, core = digits()
    rows = state_rows(partner)
    present = present_of(pattern, level, 1 - core, core)
    fold = LANES // slot
    for box in range(2):
        load = (
            level_load(blocks, level, 1 - core, core)
            if box == 0
            else lambda row: shared[0, pl.ds(row, GROUP), rows_of(1 - core, rank), :]
        )
        spread(wide, load, rank, rank)

        def emit(row, value):
            total[row] = near[box, row] + value

        multiply(wide, [row * present for row in rows] if box == 0 else rows, rank, emit)
        depth = rank // fold
        pieces = swap_groups([total[place * depth:(place + 1) * depth] for place in range(fold)], slot)
        for place, piece in enumerate(pieces):
            packed[core ^ box, place] = piece.astype(jnp.bfloat16)
    for turn, out in enumerate(outs):
        first = ((mid ^ (turn // 2)) * 2 + (low ^ (turn % 2))) * 2
        for box in range(2):
            for last in range(2):
                out[box, last] = packed[box, first + last]


def pair_box(level, wide, total, states, loads, presents, rank, out):
    for half in range(2):
        spread(wide, loads[half], rank, rank)
        present = presents[half]
        rows = [states[half, index].astype(jnp.float32) for index in range(rank)]
        if present is not None:
            rows = [row * present for row in rows]

        def emit(row, value):
            if half == 0:
                total[row] = value
            else:
                out[row] = (total[row] + value).astype(jnp.bfloat16)

        multiply(wide, rows, rank, emit)


def open_kernel(slot, blocks, pattern, *rest):
    pieces, (out, states, wide, total, packed) = rest[:4], rest[4:]
    rank = blocks.shape[1]
    _, mid, low, core = digits()
    fold = LANES // slot
    depth = rank // fold
    for turn, piece in enumerate(pieces):
        first = ((mid ^ (turn // 2)) * 2 + (low ^ (turn % 2))) * 2
        for box in range(2):
            for last in range(2):
                packed[last, first + box] = piece[box, last]
    for last in range(2):
        tile = swap_groups([packed[last, place].astype(jnp.float32) for place in range(fold)], slot)
        for place, rows in enumerate(tile):
            states[last, place * depth:(place + 1) * depth] = rows.astype(jnp.bfloat16)
    loads = [level_load(blocks, 0, half, core) for half in range(2)]
    presents = [present_of(pattern, 0, half, core) for half in range(2)]
    pair_box(0, wide, total, states, loads, presents, rank, out)


def other_kernel(shared, states, out, wide, total):
    rank = out.shape[0]
    loads = [
        functools.partial(lambda half, row: shared[1, pl.ds(row, GROUP), half * rank:(half + 1) * rank, :], half)
        for half in range(2)
    ]
    pair_box(0, wide, total, states, loads, (None, None), rank, out)


def last_kernel(level, bit, flip, joins, blocks, pattern, interp, partner, near, *rest):
    places = digits()
    chunk, other = places[3] ^ flip, 1 - places[3 - bit]
    rank = blocks.shape[1]
    if joins:
        ready, out, wide, total = rest
        for index in range(out.shape[0]):
            out[index, :, lanes_of(1 - chunk)] = ready[index]
    else:
        out, wide, total = rest
    spread(wide, level_load(blocks, level, other, chunk), rank, rank)

    def emit_state(row, value):
        total[row] = (near[row] + value).astype(jnp.bfloat16).astype(jnp.float32)

    multiply(wide, state_rows(partner, present_of(pattern, level, other, chunk)), rank, emit_state)
    spread(wide, lambda row: interp[pl.ds(row, GROUP), :, lanes_of(chunk)], out.shape[0], rank)

    def emit(row, value):
        if joins:
            out[row, :, lanes_of(chunk)] = value.astype(jnp.bfloat16)
        else:
            out[row] = value.astype(jnp.bfloat16)

    multiply(wide, [total[index] for index in range(rank)], out.shape[0], emit)


def run(kernel, outs, operands, scratch=(), products=1):
    whole = pl.BlockSpec(memory_space=pltpu.VMEM)
    single = not isinstance(outs, list)
    shapes = [outs] if single else outs
    result = pl.pallas_call(
        kernel,
        out_shape=shapes,
        in_specs=[whole] * len(operands),
        out_specs=[whole] * len(shapes),
        scratch_shapes=list(scratch),
        compiler_params=pltpu.CompilerParams(vmem_limit_bytes=16 * 2**20),
        cost_estimate=pl.CostEstimate(flops=products * 2**21, bytes_accessed=products * 2**19, transcendentals=0),
    )(*operands)
    return result[0] if single else result


def permuted(value, target_of):
    pairs = [(source, target_of(source)) for source in range(lax.axis_size("leaf"))]
    return lax.ppermute(value, "leaf", pairs)


def swapped(value, bit):
    return permuted(value, lambda source: source ^ 2**bit)


def crossed(source, turn):
    high, mid, low, core = source // 8 % 2, source // 4 % 2, source // 2 % 2, source % 2
    return ((core * 2 + (mid ^ (turn // 2))) * 2 + (low ^ (turn % 2))) * 2 + high


def fast_local(samples, interp_in, top_blocks, top_pattern, bottom_blocks, bottom_pattern, interp_out):
    rank, depth = interp_in.shape[:2]
    rhs_count, box_count = samples.shape[1:]
    out_depth = interp_out.shape[0]
    slot = box_count // lax.axis_size("leaf")
    fold = LANES // slot
    state = jax.ShapeDtypeStruct((rank, rhs_count, LANES), jnp.bfloat16)
    partial = jax.ShapeDtypeStruct((rank, rhs_count, LANES), jnp.float32)
    total = pltpu.VMEM((rank, rhs_count, LANES), jnp.float32)
    wide = pltpu.VMEM((rank * rank, LANES), jnp.float32)
    packed = pltpu.VMEM((2, fold, rank // fold, rhs_count, LANES), jnp.bfloat16)

    current = {}
    for flip in (1, 0):
        current[flip] = run(
            functools.partial(coeff_kernel, flip), state, (interp_in, samples),
            (pltpu.VMEM((rank * depth // 2, LANES), jnp.float32), total), 2,
        )
    after = current[0]
    for level in range(3):
        bit = 3 - level
        partner = {flip: swapped(current[flip], bit) for flip in (1, 0)}
        near = {
            flip: run(functools.partial(near_kernel, level, bit, flip), partial, (top_blocks, top_pattern, current[flip]), (wide,))
            for flip in (1, 0)
        }
        for flip in (1, 0):
            current[flip] = run(
                functools.partial(far_kernel, level, bit, flip), state,
                (top_blocks, top_pattern, partner[flip], near[flip]), (wide,),
            )
    shared = run(
        functools.partial(share_kernel, 3), jax.ShapeDtypeStruct((2, rank, 2 * rank, LANES), jnp.bfloat16),
        (top_blocks, top_pattern, bottom_blocks, bottom_pattern, after),
    )
    shared = swapped(shared, 0)

    far = swapped(current[1], 0)
    near = run(
        functools.partial(pair_near_kernel, 3), jax.ShapeDtypeStruct((2, rank, rhs_count, LANES), jnp.float32),
        (top_blocks, top_pattern, shared, current[0]), (wide,), 2,
    )
    piece = jax.ShapeDtypeStruct((2, 2, rank // fold, rhs_count, LANES), jnp.bfloat16)
    pieces = run(
        functools.partial(pair_far_kernel, 3, slot), [piece] * 4,
        (top_blocks, top_pattern, shared, far, near), (wide, total, packed), 2,
    )
    pieces = [permuted(value, functools.partial(crossed, turn=turn)) for turn, value in enumerate(pieces)]
    first, states = run(
        functools.partial(open_kernel, slot), [state, jax.ShapeDtypeStruct((2, rank, rhs_count, LANES), jnp.bfloat16)],
        (bottom_blocks, bottom_pattern, *pieces), (wide, total, packed), 2,
    )
    second = run(other_kernel, state, (shared, states), (wide, total), 2)
    current = {0: first, 1: swapped(second, 0)}

    for level in (1, 2, 3):
        partner = {flip: swapped(current[flip], level) for flip in (0, 1)}
        near = {
            flip: run(functools.partial(near_kernel, level, level, flip), partial, (bottom_blocks, bottom_pattern, current[flip]), (wide,))
            for flip in (0, 1)
        }
        if level < 3:
            for flip in (0, 1):
                current[flip] = run(
                    functools.partial(far_kernel, level, level, flip), state,
                    (bottom_blocks, bottom_pattern, partner[flip], near[flip]), (wide,),
                )
    broad = pltpu.VMEM((out_depth * rank, LANES), jnp.float32)
    ready = run(
        functools.partial(last_kernel, 3, 3, 0, False), jax.ShapeDtypeStruct((out_depth, rhs_count, LANES), jnp.bfloat16),
        (bottom_blocks, bottom_pattern, interp_out, partner[0], near[0]), (broad, total), 3,
    )
    return run(
        functools.partial(last_kernel, 3, 3, 1, True), jax.ShapeDtypeStruct((out_depth, rhs_count, box_count), jnp.bfloat16),
        (bottom_blocks, bottom_pattern, interp_out, partner[1], near[1], ready), (broad, total), 3,
    )


def contract(weights, state):
    product = weights[:, :, None].astype(jnp.float32) * state[None].astype(jnp.float32)
    return jnp.sum(product, axis=1)


def plain_level(current, blocks, pattern, bit):
    rank = blocks.shape[0]
    partner = swapped(current, bit)
    is_lower = lax.axis_index("leaf") // 2**bit % 2 == 0
    lower = jnp.where(is_lower, current, partner)
    upper = jnp.where(is_lower, partner, current)
    weights = blocks * jnp.repeat(pattern, rank, axis=0).astype(jnp.bfloat16)[None]
    return contract(weights, jnp.concatenate([lower, upper], axis=0)).astype(jnp.bfloat16)


def plain_local(samples, interp_in, top_blocks, top_pattern, bottom_blocks, bottom_pattern, interp_out):
    bit_count = lax.axis_size("leaf").bit_length() - 1
    current = contract(interp_in, samples).astype(jnp.bfloat16)
    for level in range(top_blocks.shape[0]):
        current = plain_level(current, top_blocks[level], top_pattern[level], bit_count - 1 - level)
    flat = current.reshape(-1, current.shape[2])
    current = lax.all_to_all(flat, "leaf", split_axis=1, concat_axis=1, tiled=True).reshape(current.shape)
    for level in range(bottom_blocks.shape[0]):
        current = plain_level(current, bottom_blocks[level], bottom_pattern[level], level)
    return contract(interp_out, current).astype(jnp.bfloat16)


def local(samples, interp_in, top_blocks, *rest):
    four_digits = lax.axis_size("leaf") == 16 and top_blocks.shape[0] == 4
    chosen = fast_local if four_digits and samples.shape[1:] == (8, 2 * LANES) else plain_local
    return chosen(samples, interp_in, top_blocks, *rest)


def solution(mesh):
    boxes = ("parts", "leaf")
    return jax.shard_map(
        local,
        mesh=mesh,
        in_specs=(
            P(None, None, boxes),
            P(None, None, boxes),
            P(None, None, None, boxes),
            P(None, None, boxes),
            P(None, None, None, boxes),
            P(None, None, boxes),
            P(None, None, boxes),
        ),
        out_specs=P(None, None, boxes),
        check_vma=False,
    )
```

```python
import functools

import jax
import jax.numpy as jnp
from jax import lax
from jax.experimental import pallas as pl
from jax.experimental.pallas import tpu as pltpu
from jax.sharding import PartitionSpec as P

LANES = 128
GROUP = 4


def digits():
    place = lax.axis_index("leaf")
    return lax.rem(place // 8, 2), lax.rem(place // 4, 2), lax.rem(place // 2, 2), lax.rem(place, 2)


def lanes_of(chunk):
    return pl.ds(pl.multiple_of(chunk * LANES, LANES), LANES)


def rows_of(half, rank):
    return pl.ds(pl.multiple_of(half * rank, rank), rank)


def spread(wide, load, row_count, rank):
    def body(step, carry):
        rows = load(step * GROUP).astype(jnp.float32)
        wide[pl.ds(step * GROUP * rank, GROUP * rank), :] = rows.reshape(GROUP * rank, LANES)
        return carry

    lax.fori_loop(0, row_count // GROUP, body, 0)


def multiply(wide, state, row_count, emit):
    rank = len(state)

    def body(step, carry):
        for inner in range(GROUP):
            sums = [None, None]
            for index in range(rank):
                weight = wide[pl.ds(step * GROUP * rank + inner * rank + index, 8, stride=0), :]
                term = weight * state[index]
                old = sums[index % 2]
                sums[index % 2] = term if old is None else old + term
            emit(step * GROUP + inner, sums[0] + sums[1])
        return carry

    lax.fori_loop(0, row_count // GROUP, body, 0)


def state_rows(ref, present=None):
    rows = [ref[index].astype(jnp.float32) for index in range(ref.shape[0])]
    return rows if present is None else [row * present for row in rows]


def level_load(blocks, level, half, chunk):
    rank = blocks.shape[1]
    return lambda row: blocks[level, pl.ds(row, GROUP), rows_of(half, rank), lanes_of(chunk)]


def present_of(pattern, level, half, chunk):
    pair = [pattern[level, place:place + 1, lanes_of(chunk)].astype(jnp.float32) for place in range(2)]
    return jnp.where(half == 0, pair[0], pair[1])


def coeff_kernel(flip, interp, samples, out, wide, total):
    rank, depth = interp.shape[0], interp.shape[1] // 2
    chunk = digits()[3] ^ flip
    for half in range(2):
        spread(wide, lambda row: interp[pl.ds(row, GROUP), pl.ds(half * depth, depth), lanes_of(chunk)], rank, depth)
        state = [samples[half * depth + index, :, lanes_of(chunk)].astype(jnp.float32) for index in range(depth)]

        def emit(row, value):
            if half == 0:
                total[row] = value
            else:
                out[row] = (total[row] + value).astype(jnp.bfloat16)

        multiply(wide, state, rank, emit)


def near_kernel(level, bit, flip, blocks, pattern, state, out, wide):
    places = digits()
    chunk, own = places[3] ^ flip, places[3 - bit]
    spread(wide, level_load(blocks, level, own, chunk), blocks.shape[1], blocks.shape[1])

    def emit(row, value):
        out[row] = value

    multiply(wide, state_rows(state, present_of(pattern, level, own, chunk)), blocks.shape[1], emit)


def far_kernel(level, bit, flip, blocks, pattern, partner, near, out, wide):
    places = digits()
    chunk, other = places[3] ^ flip, 1 - places[3 - bit]
    spread(wide, level_load(blocks, level, other, chunk), blocks.shape[1], blocks.shape[1])

    def emit(row, value):
        out[row] = (near[row] + value).astype(jnp.bfloat16)

    multiply(wide, state_rows(partner.at[other], present_of(pattern, level, other, chunk)), blocks.shape[1], emit)


def share_kernel(top_level, top_blocks, top_pattern, bottom_blocks, bottom_pattern, after, out):
    rank = top_blocks.shape[1]
    chunk = 1 - digits()[3]
    for place, (blocks, pattern, level) in enumerate(((top_blocks, top_pattern, top_level), (bottom_blocks, bottom_pattern, 0))):
        for half in range(2):
            present = present_of(pattern, level, half, chunk)[None]

            def body(row, carry):
                rows = blocks[level, pl.ds(row, 1), half * rank:(half + 1) * rank, lanes_of(chunk)]
                out[place, pl.ds(row, 1), half * rank:(half + 1) * rank, :] = (rows.astype(jnp.float32) * present).astype(jnp.bfloat16)
                return carry

            lax.fori_loop(0, rank, body, 0)


def swap_groups(tile, slot):
    lane_group = lax.broadcasted_iota(jnp.int32, tile[0].shape, 2) // slot
    step = 1
    while step < len(tile):
        low = (lane_group // step) % 2 == 0
        fresh = list(tile)
        for place in range(len(tile)):
            if place & step == 0:
                first, second = tile[place], tile[place + step]
                fresh[place] = jnp.where(low, first, pltpu.roll(second, step * slot, 2))
                fresh[place + step] = jnp.where(low, pltpu.roll(first, LANES - step * slot, 2), second)
        tile = fresh
        step *= 2
    return tile


def pair_near_kernel(level, blocks, pattern, shared, state, out, wide):
    rank = blocks.shape[1]
    core = digits()[3]
    rows = state_rows(state)
    present = present_of(pattern, level, core, core)
    for box in range(2):
        load = (
            level_load(blocks, level, core, core)
            if box == 0
            else lambda row: shared[0, pl.ds(row, GROUP), rows_of(core, rank), :]
        )
        spread(wide, load, rank, rank)

        def emit(row, value):
            out[box, row] = value

        multiply(wide, [row * present for row in rows] if box == 0 else rows, rank, emit)


def pair_far_kernel(level, slot, blocks, pattern, shared, partner, near, *rest):
    outs, (wide, total, packed) = rest[:4], rest[4:]
    rank = blocks.shape[1]
    _, mid, low, core = digits()
    rows = state_rows(partner)
    present = present_of(pattern, level, 1 - core, core)
    fold = LANES // slot
    for box in range(2):
        load = (
            level_load(blocks, level, 1 - core, core)
            if box == 0
            else lambda row: shared[0, pl.ds(row, GROUP), rows_of(1 - core, rank), :]
        )
        spread(wide, load, rank, rank)

        def emit(row, value):
            total[row] = near[box, row] + value

        multiply(wide, [row * present for row in rows] if box == 0 else rows, rank, emit)
        depth = rank // fold
        pieces = swap_groups([total[place * depth:(place + 1) * depth] for place in range(fold)], slot)
        for place, piece in enumerate(pieces):
            packed[core ^ box, place] = piece.astype(jnp.bfloat16)
    for turn, out in enumerate(outs):
        first = ((mid ^ (turn // 2)) * 2 + (low ^ (turn % 2))) * 2
        for box in range(2):
            for last in range(2):
                out[box, last] = packed[box, first + last]


def pair_box(level, wide, total, states, loads, presents, rank, out):
    for half in range(2):
        spread(wide, loads[half], rank, rank)
        present = presents[half]
        rows = [states[half, index].astype(jnp.float32) for index in range(rank)]
        if present is not None:
            rows = [row * present for row in rows]

        def emit(row, value):
            if half == 0:
                total[row] = value
            else:
                out[row] = (total[row] + value).astype(jnp.bfloat16)

        multiply(wide, rows, rank, emit)


def open_kernel(slot, blocks, pattern, *rest):
    pieces, (out, states, wide, total, packed) = rest[:4], rest[4:]
    rank = blocks.shape[1]
    _, mid, low, core = digits()
    fold = LANES // slot
    depth = rank // fold
    for turn, piece in enumerate(pieces):
        first = ((mid ^ (turn // 2)) * 2 + (low ^ (turn % 2))) * 2
        for box in range(2):
            for last in range(2):
                packed[last, first + box] = piece[box, last]
    for last in range(2):
        tile = swap_groups([packed[last, place].astype(jnp.float32) for place in range(fold)], slot)
        for place, rows in enumerate(tile):
            states[last, place * depth:(place + 1) * depth] = rows.astype(jnp.bfloat16)
    loads = [level_load(blocks, 0, half, core) for half in range(2)]
    presents = [present_of(pattern, 0, half, core) for half in range(2)]
    pair_box(0, wide, total, states, loads, presents, rank, out)


def other_kernel(shared, states, out, wide, total):
    rank = out.shape[0]
    loads = [
        functools.partial(lambda half, row: shared[1, pl.ds(row, GROUP), half * rank:(half + 1) * rank, :], half)
        for half in range(2)
    ]
    pair_box(0, wide, total, states, loads, (None, None), rank, out)


def last_kernel(level, bit, flip, joins, blocks, pattern, interp, partner, near, *rest):
    places = digits()
    chunk, other = places[3] ^ flip, 1 - places[3 - bit]
    rank = blocks.shape[1]
    if joins:
        ready, out, wide, total = rest
        for index in range(out.shape[0]):
            out[index, :, lanes_of(1 - chunk)] = ready[index]
    else:
        out, wide, total = rest
    spread(wide, level_load(blocks, level, other, chunk), rank, rank)

    def emit_state(row, value):
        total[row] = (near[row] + value).astype(jnp.bfloat16).astype(jnp.float32)

    multiply(wide, state_rows(partner.at[other], present_of(pattern, level, other, chunk)), rank, emit_state)
    spread(wide, lambda row: interp[pl.ds(row, GROUP), :, lanes_of(chunk)], out.shape[0], rank)

    def emit(row, value):
        if joins:
            out[row, :, lanes_of(chunk)] = value.astype(jnp.bfloat16)
        else:
            out[row] = value.astype(jnp.bfloat16)

    multiply(wide, [total[index] for index in range(rank)], out.shape[0], emit)


def run(kernel, outs, operands, scratch=(), products=1):
    whole = pl.BlockSpec(memory_space=pltpu.VMEM)
    single = not isinstance(outs, list)
    shapes = [outs] if single else outs
    result = pl.pallas_call(
        kernel,
        out_shape=shapes,
        in_specs=[whole] * len(operands),
        out_specs=[whole] * len(shapes),
        scratch_shapes=list(scratch),
        compiler_params=pltpu.CompilerParams(vmem_limit_bytes=16 * 2**20),
        cost_estimate=pl.CostEstimate(flops=products * 2**21, bytes_accessed=products * 2**19, transcendentals=0),
    )(*operands)
    return result[0] if single else result


def permuted(value, target_of):
    pairs = [(source, target_of(source)) for source in range(lax.axis_size("leaf"))]
    return lax.ppermute(value, "leaf", pairs)


def swapped(value, bit):
    return permuted(value, lambda source: source ^ 2**bit)


def gathered(value, bit):
    count = lax.axis_size("leaf")
    pairs = [[place, place + 2**bit] for place in range(count) if place // 2**bit % 2 == 0]
    return lax.all_gather(value, "leaf", axis_index_groups=pairs)


def crossed(source, turn):
    high, mid, low, core = source // 8 % 2, source // 4 % 2, source // 2 % 2, source % 2
    return ((core * 2 + (mid ^ (turn // 2))) * 2 + (low ^ (turn % 2))) * 2 + high


def fast_local(samples, interp_in, top_blocks, top_pattern, bottom_blocks, bottom_pattern, interp_out):
    rank, depth = interp_in.shape[:2]
    rhs_count, box_count = samples.shape[1:]
    out_depth = interp_out.shape[0]
    slot = box_count // lax.axis_size("leaf")
    fold = LANES // slot
    state = jax.ShapeDtypeStruct((rank, rhs_count, LANES), jnp.bfloat16)
    partial = jax.ShapeDtypeStruct((rank, rhs_count, LANES), jnp.float32)
    total = pltpu.VMEM((rank, rhs_count, LANES), jnp.float32)
    wide = pltpu.VMEM((rank * rank, LANES), jnp.float32)
    packed = pltpu.VMEM((2, fold, rank // fold, rhs_count, LANES), jnp.bfloat16)

    current = {}
    for flip in (1, 0):
        current[flip] = run(
            functools.partial(coeff_kernel, flip), state, (interp_in, samples),
            (pltpu.VMEM((rank * depth // 2, LANES), jnp.float32), total), 2,
        )
    for level in range(3):
        bit = 3 - level
        partner = {flip: gathered(current[flip], bit) for flip in (1, 0)}
        near = {
            flip: run(functools.partial(near_kernel, level, bit, flip), partial, (top_blocks, top_pattern, current[flip]), (wide,))
            for flip in (1, 0)
        }
        if level == 0:
            after = near[0]
        for flip in (1, 0):
            current[flip] = run(
                functools.partial(far_kernel, level, bit, flip), state,
                (top_blocks, top_pattern, partner[flip], near[flip]), (wide,),
            )
    shared = run(
        functools.partial(share_kernel, 3), jax.ShapeDtypeStruct((2, rank, 2 * rank, LANES), jnp.bfloat16),
        (top_blocks, top_pattern, bottom_blocks, bottom_pattern, after),
    )
    shared = swapped(shared, 0)

    far = swapped(current[1], 0)
    near = run(
        functools.partial(pair_near_kernel, 3), jax.ShapeDtypeStruct((2, rank, rhs_count, LANES), jnp.float32),
        (top_blocks, top_pattern, shared, current[0]), (wide,), 2,
    )
    piece = jax.ShapeDtypeStruct((2, 2, rank // fold, rhs_count, LANES), jnp.bfloat16)
    pieces = run(
        functools.partial(pair_far_kernel, 3, slot), [piece] * 4,
        (top_blocks, top_pattern, shared, far, near), (wide, total, packed), 2,
    )
    pieces = [permuted(value, functools.partial(crossed, turn=turn)) for turn, value in enumerate(pieces)]
    first, states = run(
        functools.partial(open_kernel, slot), [state, jax.ShapeDtypeStruct((2, rank, rhs_count, LANES), jnp.bfloat16)],
        (bottom_blocks, bottom_pattern, *pieces), (wide, total, packed), 2,
    )
    second = run(other_kernel, state, (shared, states), (wide, total), 2)
    current = {0: first, 1: swapped(second, 0)}

    for level in (1, 2, 3):
        partner = {flip: gathered(current[flip], level) for flip in (0, 1)}
        near = {
            flip: run(functools.partial(near_kernel, level, level, flip), partial, (bottom_blocks, bottom_pattern, current[flip]), (wide,))
            for flip in (0, 1)
        }
        if level < 3:
            for flip in (0, 1):
                current[flip] = run(
                    functools.partial(far_kernel, level, level, flip), state,
                    (bottom_blocks, bottom_pattern, partner[flip], near[flip]), (wide,),
                )
    broad = pltpu.VMEM((out_depth * rank, LANES), jnp.float32)
    ready = run(
        functools.partial(last_kernel, 3, 3, 0, False), jax.ShapeDtypeStruct((out_depth, rhs_count, LANES), jnp.bfloat16),
        (bottom_blocks, bottom_pattern, interp_out, partner[0], near[0]), (broad, total), 3,
    )
    return run(
        functools.partial(last_kernel, 3, 3, 1, True), jax.ShapeDtypeStruct((out_depth, rhs_count, box_count), jnp.bfloat16),
        (bottom_blocks, bottom_pattern, interp_out, partner[1], near[1], ready), (broad, total), 3,
    )


def contract(weights, state):
    product = weights[:, :, None].astype(jnp.float32) * state[None].astype(jnp.float32)
    return jnp.sum(product, axis=1)


def plain_level(current, blocks, pattern, bit):
    rank = blocks.shape[0]
    partner = swapped(current, bit)
    is_lower = lax.axis_index("leaf") // 2**bit % 2 == 0
    lower = jnp.where(is_lower, current, partner)
    upper = jnp.where(is_lower, partner, current)
    weights = blocks * jnp.repeat(pattern, rank, axis=0).astype(jnp.bfloat16)[None]
    return contract(weights, jnp.concatenate([lower, upper], axis=0)).astype(jnp.bfloat16)


def plain_local(samples, interp_in, top_blocks, top_pattern, bottom_blocks, bottom_pattern, interp_out):
    bit_count = lax.axis_size("leaf").bit_length() - 1
    current = contract(interp_in, samples).astype(jnp.bfloat16)
    for level in range(top_blocks.shape[0]):
        current = plain_level(current, top_blocks[level], top_pattern[level], bit_count - 1 - level)
    flat = current.reshape(-1, current.shape[2])
    current = lax.all_to_all(flat, "leaf", split_axis=1, concat_axis=1, tiled=True).reshape(current.shape)
    for level in range(bottom_blocks.shape[0]):
        current = plain_level(current, bottom_blocks[level], bottom_pattern[level], level)
    return contract(interp_out, current).astype(jnp.bfloat16)


def local(samples, interp_in, top_blocks, *rest):
    four_digits = lax.axis_size("leaf") == 16 and top_blocks.shape[0] == 4
    chosen = fast_local if four_digits and samples.shape[1:] == (8, 2 * LANES) else plain_local
    return chosen(samples, interp_in, top_blocks, *rest)


def solution(mesh):
    boxes = ("parts", "leaf")
    return jax.shard_map(
        local,
        mesh=mesh,
        in_specs=(
            P(None, None, boxes),
            P(None, None, boxes),
            P(None, None, None, boxes),
            P(None, None, boxes),
            P(None, None, None, boxes),
            P(None, None, boxes),
            P(None, None, boxes),
        ),
        out_specs=P(None, None, boxes),
        check_vma=False,
    )
```

```python
import functools

import jax
import jax.numpy as jnp
from jax import lax
from jax.experimental import pallas as pl
from jax.experimental.pallas import tpu as pltpu
from jax.sharding import PartitionSpec as P

LANES = 128
GROUP = 4
START_LIMIT = 62_700_000


def digits():
    place = lax.axis_index("leaf")
    return lax.rem(place // 8, 2), lax.rem(place // 4, 2), lax.rem(place // 2, 2), lax.rem(place, 2)


def lanes_of(chunk):
    return pl.ds(pl.multiple_of(chunk * LANES, LANES), LANES)


def rows_of(half, rank):
    return pl.ds(pl.multiple_of(half * rank, rank), rank)


def spread(wide, load, row_count, rank):
    def body(step, carry):
        rows = load(step * GROUP).astype(jnp.float32)
        wide[pl.ds(step * GROUP * rank, GROUP * rank), :] = rows.reshape(GROUP * rank, LANES)
        return carry

    lax.fori_loop(0, row_count // GROUP, body, 0)


def multiply(wide, state, row_count, emit):
    rank = len(state)

    def body(step, carry):
        for inner in range(GROUP):
            sums = [None, None]
            for index in range(rank):
                weight = wide[pl.ds(step * GROUP * rank + inner * rank + index, 8, stride=0), :]
                term = weight * state[index]
                old = sums[index % 2]
                sums[index % 2] = term if old is None else old + term
            emit(step * GROUP + inner, sums[0] + sums[1])
        return carry

    lax.fori_loop(0, row_count // GROUP, body, 0)


def state_rows(ref, present=None):
    rows = [ref[index].astype(jnp.float32) for index in range(ref.shape[0])]
    return rows if present is None else [row * present for row in rows]


def level_load(blocks, level, half, chunk):
    rank = blocks.shape[1]
    return lambda row: blocks[level, pl.ds(row, GROUP), rows_of(half, rank), lanes_of(chunk)]


def present_of(pattern, level, half, chunk):
    pair = [pattern[level, place:place + 1, lanes_of(chunk)].astype(jnp.float32) for place in range(2)]
    return jnp.where(half == 0, pair[0], pair[1])


def coeff_kernel(interp, samples, first, second, held_interp, held_samples, wide, total, sems):
    rank, depth = first.shape[0], held_samples.shape[1]
    core = digits()[3]
    pairs = []
    for turn, chunk in enumerate((1 - core, core)):
        for half in range(2):
            place, part = turn * 2 + half, pl.ds(half * depth, depth)
            pairs.append((
                pltpu.make_async_copy(samples.at[part, :, lanes_of(chunk)], held_samples.at[place], sems.at[2 * place]),
                pltpu.make_async_copy(interp.at[:, part, lanes_of(chunk)], held_interp.at[place], sems.at[2 * place + 1]),
            ))
    for pair in pairs:
        for copy in pair:
            copy.start()
    for place, pair in enumerate(pairs):
        for copy in pair:
            copy.wait()
        spread(wide, lambda row: held_interp[place, pl.ds(row, GROUP)], rank, depth)
        state = [held_samples[place, index].astype(jnp.float32) for index in range(depth)]
        out = (first, second)[place // 2]

        def emit(row, value):
            if place % 2 == 0:
                total[row] = value
            else:
                out[row] = (total[row] + value).astype(jnp.bfloat16)

        multiply(wide, state, rank, emit)


def near_kernel(level, bit, flip, blocks, pattern, state, *rest):
    out, far_wide, wide = rest[-3:]
    places = digits()
    chunk, own = places[3] ^ flip, places[3 - bit]
    spread(wide, level_load(blocks, level, own, chunk), blocks.shape[1], blocks.shape[1])
    spread(far_wide, level_load(blocks, level, 1 - own, chunk), blocks.shape[1], blocks.shape[1])

    def emit(row, value):
        out[row] = value

    multiply(wide, state_rows(state, present_of(pattern, level, own, chunk)), blocks.shape[1], emit)


def far_kernel(level, bit, flip, pattern, partner, near, wide, out):
    places = digits()
    chunk, other = places[3] ^ flip, 1 - places[3 - bit]

    def emit(row, value):
        out[row] = (near[row] + value).astype(jnp.bfloat16)

    multiply(wide, state_rows(partner, present_of(pattern, level, other, chunk)), out.shape[0], emit)


def share_kernel(top_level, top_blocks, top_pattern, bottom_blocks, bottom_pattern, out):
    rank = top_blocks.shape[1]
    chunk = 1 - digits()[3]
    for place, (blocks, pattern, level) in enumerate(((top_blocks, top_pattern, top_level), (bottom_blocks, bottom_pattern, 0))):
        for half in range(2):
            present = present_of(pattern, level, half, chunk)[None]

            def body(row, carry):
                rows = blocks[level, pl.ds(row, 1), half * rank:(half + 1) * rank, lanes_of(chunk)]
                out[place * rank + row, half * rank:(half + 1) * rank, :] = (rows.astype(jnp.float32) * present)[0].astype(jnp.bfloat16)
                return carry

            lax.fori_loop(0, rank, body, 0)


def shared_load(shared, place, half):
    rank = shared.shape[1] // 2
    return lambda row: shared[pl.ds(place * rank + row, GROUP), rows_of(half, rank), :]


def send_kernel(level, bit, flip, pattern, partner, near, wide, shared, out):
    rank, per = partner.shape[0], shared.shape[1] // partner.shape[1]
    places = digits()
    chunk, other = places[3] ^ flip, 1 - places[3 - bit]

    def emit(row, value):
        place = pl.ds(pl.multiple_of(lax.rem(row, per) * 8, 8), 8)
        out[2 * rank + row // per, place, :] = (near[row] + value).astype(jnp.bfloat16)

    multiply(wide, state_rows(partner, present_of(pattern, level, other, chunk)), rank, emit)


def sent_rows(shared):
    rank = shared.shape[1] // 2
    per = shared.shape[1] // 8
    return [
        shared[2 * rank + row // per, row % per * 8:(row % per + 1) * 8, :].astype(jnp.float32) for row in range(rank)
    ]


def swap_groups(tile, slot):
    lane_group = lax.broadcasted_iota(jnp.int32, tile[0].shape, 2) // slot
    step = 1
    while step < len(tile):
        low = (lane_group // step) % 2 == 0
        fresh = list(tile)
        for place in range(len(tile)):
            if place & step == 0:
                first, second = tile[place], tile[place + step]
                fresh[place] = jnp.where(low, first, pltpu.roll(second, step * slot, 2))
                fresh[place + step] = jnp.where(low, pltpu.roll(first, LANES - step * slot, 2), second)
        tile = fresh
        step *= 2
    return tile


def pair_near_kernel(level, blocks, pattern, shared, state, out, far_wide, wide):
    rank = blocks.shape[1]
    core = digits()[3]
    rows = state_rows(state)
    present = present_of(pattern, level, core, core)
    for box in range(2):
        for target, half in ((wide, core), (far_wide.at[box], 1 - core)):
            load = (
                level_load(blocks, level, half, core)
                if box == 0
                else shared_load(shared, 0, half)
            )
            spread(target, load, rank, rank)

        def emit(row, value):
            out[box, row] = value

        multiply(wide, [row * present for row in rows] if box == 0 else rows, rank, emit)


def pair_far_kernel(level, slot, pattern, wide, shared, near, *rest):
    outs, (total, packed) = rest[:4], rest[4:]
    rank = near.shape[1]
    _, mid, low, core = digits()
    rows = sent_rows(shared)
    present = present_of(pattern, level, 1 - core, core)
    fold = LANES // slot
    for box in range(2):
        def emit(row, value):
            total[row] = near[box, row] + value

        multiply(wide.at[box], [row * present for row in rows] if box == 0 else rows, rank, emit)
        depth = rank // fold
        pieces = swap_groups([total[place * depth:(place + 1) * depth] for place in range(fold)], slot)
        for place, piece in enumerate(pieces):
            packed[core ^ box, place] = piece.astype(jnp.bfloat16)
    for turn, out in enumerate(outs):
        first = ((mid ^ (turn // 2)) * 2 + (low ^ (turn % 2))) * 2
        for box in range(2):
            for last in range(2):
                out[box, last] = packed[box, first + last]


def wide_kernel(blocks, shared, own_wide, other_wide):
    rank = blocks.shape[1]
    core = digits()[3]
    for half in range(2):
        spread(own_wide.at[half], level_load(blocks, 0, half, core), rank, rank)
        spread(other_wide.at[half], shared_load(shared, 1, half), rank, rank)


def pair_box(wide, total, states, presents, out):
    for half in range(2):
        present = presents[half]
        rows = [states[half, index].astype(jnp.float32) for index in range(out.shape[0])]
        if present is not None:
            rows = [row * present for row in rows]

        def emit(row, value):
            if half == 0:
                total[row] = value
            else:
                out[row] = (total[row] + value).astype(jnp.bfloat16)

        multiply(wide.at[half], rows, out.shape[0], emit)


def open_kernel(slot, pattern, wide, *rest):
    pieces, (out, states, total, packed) = rest[:4], rest[4:]
    _, mid, low, core = digits()
    fold = LANES // slot
    depth = out.shape[0] // fold
    for turn, piece in enumerate(pieces):
        first = ((mid ^ (turn // 2)) * 2 + (low ^ (turn % 2))) * 2
        for box in range(2):
            for last in range(2):
                packed[last, first + box] = piece[box, last]
    for last in range(2):
        tile = swap_groups([packed[last, place].astype(jnp.float32) for place in range(fold)], slot)
        for place, rows in enumerate(tile):
            states[last, place * depth:(place + 1) * depth] = rows.astype(jnp.bfloat16)
    pair_box(wide, total, states, [present_of(pattern, 0, half, core) for half in range(2)], out)


def other_kernel(wide, states, after, out, total):
    pair_box(wide, total, states, (None, None), out)


def interp_kernel(interp, after, first_wide, second_wide):
    core = digits()[3]
    for wide, chunk in ((first_wide, core), (second_wide, 1 - core)):
        spread(wide, lambda row: interp[pl.ds(row, GROUP), :, lanes_of(chunk)], interp.shape[0], interp.shape[1])


def last_kernel(level, bit, flip, pattern, wide, image_wide, partner, near, *rest):
    image, held, total, sems = rest[-4:]
    places = digits()
    chunk, other = places[3] ^ flip, 1 - places[3 - bit]
    rank, depth = total.shape[0], held.shape[0]

    def emit_state(row, value):
        total[row] = (near[row] + value).astype(jnp.bfloat16).astype(jnp.float32)

    multiply(wide, state_rows(partner, present_of(pattern, level, other, chunk)), rank, emit_state)
    rows = [total[index] for index in range(rank)]
    parts = 4
    size = depth // parts
    copies = []
    for part in range(parts):

        def emit(row, value):
            held[part * size + row] = value.astype(jnp.bfloat16)

        multiply(image_wide.at[pl.ds(part * size * rank, size * rank), :], rows, size, emit)
        span = pl.ds(part * size, size)
        copies.append(pltpu.make_async_copy(held.at[span], image.at[span, :, lanes_of(chunk)], sems.at[part]))
        copies[-1].start()
    for copy in copies:
        copy.wait()


def run(kernel, outs, operands, scratch=(), products=1, in_specs=None, out_specs=None, aliases=None, limit=16 * 2**20):
    whole = pl.BlockSpec(memory_space=pltpu.VMEM)
    single = not isinstance(outs, list)
    shapes = [outs] if single else outs
    result = pl.pallas_call(
        kernel,
        out_shape=shapes,
        in_specs=in_specs or [whole] * len(operands),
        out_specs=out_specs or [whole] * len(shapes),
        scratch_shapes=list(scratch),
        input_output_aliases=aliases or {},
        compiler_params=pltpu.CompilerParams(vmem_limit_bytes=limit),
        cost_estimate=pl.CostEstimate(flops=products * 2**21, bytes_accessed=products * 2**19, transcendentals=0),
    )(*operands)
    return result[0] if single else result


def permuted(value, target_of):
    pairs = [(source, target_of(source)) for source in range(lax.axis_size("leaf"))]
    return lax.ppermute(value, "leaf", pairs)


def swapped(value, bit):
    return permuted(value, lambda source: source ^ 2**bit)


def crossed(source, turn):
    high, mid, low, core = source // 8 % 2, source // 4 % 2, source // 2 % 2, source % 2
    return ((core * 2 + (mid ^ (turn // 2))) * 2 + (low ^ (turn % 2))) * 2 + high


def fast_local(samples, interp_in, top_blocks, top_pattern, bottom_blocks, bottom_pattern, interp_out):
    rank, depth = interp_in.shape[:2]
    rhs_count, box_count = samples.shape[1:]
    out_depth = interp_out.shape[0]
    slot = box_count // lax.axis_size("leaf")
    fold = LANES // slot
    state = jax.ShapeDtypeStruct((rank, rhs_count, LANES), jnp.bfloat16)
    partial = jax.ShapeDtypeStruct((rank, rhs_count, LANES), jnp.float32)
    spread_out = jax.ShapeDtypeStruct((rank * rank, LANES), jnp.float32)
    pair_spread = jax.ShapeDtypeStruct((2, rank * rank, LANES), jnp.float32)
    total = pltpu.VMEM((rank, rhs_count, LANES), jnp.float32)
    wide = pltpu.VMEM((rank * rank, LANES), jnp.float32)
    packed = pltpu.VMEM((2, fold, rank // fold, rhs_count, LANES), jnp.bfloat16)
    whole, anywhere = pl.BlockSpec(memory_space=pltpu.VMEM), pl.BlockSpec(memory_space=pl.ANY)

    def level_nears(blocks, pattern, level, bit, order):
        return {
            flip: run(
                functools.partial(near_kernel, level, bit, flip), [partial, spread_out],
                (blocks, pattern, current[flip]) + ((current[1 - flip],) if place < len(order) - 1 else ()), (wide,),
            )
            for place, flip in enumerate(order)
        }

    def level_fars(pattern, level, bit, order):
        return {
            flip: run(
                functools.partial(far_kernel, level, bit, flip), state, (pattern, partner[flip], *near[flip]),
            )
            for flip in order
        }

    current = {}
    current[1], current[0] = run(
        coeff_kernel, [state, state], (interp_in, samples),
        (
            pltpu.VMEM((4, rank, depth // 2, LANES), jnp.bfloat16),
            pltpu.VMEM((4, depth // 2, rhs_count, LANES), jnp.bfloat16),
            pltpu.VMEM((rank * depth // 2, LANES), jnp.float32), total, pltpu.SemaphoreType.DMA((8,)),
        ),
        4, [anywhere] * 2, limit=START_LIMIT,
    )
    for level in range(3):
        bit = 3 - level
        partner = {flip: swapped(current[flip], bit) for flip in (1, 0)}
        near = level_nears(top_blocks, top_pattern, level, bit, (1, 0))
        if level < 2:
            current = level_fars(top_pattern, level, bit, (1, 0))

    share_rows = 2 * rank + rank * rhs_count // (2 * rank)
    shared_shape = jax.ShapeDtypeStruct((share_rows, 2 * rank, LANES), jnp.bfloat16)
    shared = run(functools.partial(share_kernel, 3), shared_shape, (top_blocks, top_pattern, bottom_blocks, bottom_pattern))
    shared = run(
        functools.partial(send_kernel, 2, 1, 1), shared_shape, (top_pattern, partner[1], *near[1], shared), aliases={4: 0},
    )
    shared = swapped(shared, 0)
    current = level_fars(top_pattern, 2, 1, (0,))

    pair_near = run(
        functools.partial(pair_near_kernel, 3),
        [jax.ShapeDtypeStruct((2, rank, rhs_count, LANES), jnp.float32), pair_spread],
        (top_blocks, top_pattern, shared, current[0]), (wide,), 2,
    )
    piece = jax.ShapeDtypeStruct((2, 2, rank // fold, rhs_count, LANES), jnp.bfloat16)
    pieces = run(
        functools.partial(pair_far_kernel, 3, slot), [piece] * 4,
        (top_pattern, pair_near[1], shared, pair_near[0]), (total, packed), 2,
    )
    pieces = [permuted(value, functools.partial(crossed, turn=turn)) for turn, value in enumerate(pieces)]
    own_wide, other_wide = run(wide_kernel, [pair_spread] * 2, (bottom_blocks, shared))
    first, states = run(
        functools.partial(open_kernel, slot), [state, jax.ShapeDtypeStruct((2, rank, rhs_count, LANES), jnp.bfloat16)],
        (bottom_pattern, own_wide, *pieces), (total, packed), 2,
    )
    current = {0: first}
    partner = {0: swapped(first, 1)}
    near = level_nears(bottom_blocks, bottom_pattern, 1, 1, (0,))
    current[1] = swapped(run(other_kernel, state, (other_wide, states, near[0][0]), (total,), 2), 0)
    partner[1] = swapped(current[1], 1)
    near.update(level_nears(bottom_blocks, bottom_pattern, 1, 1, (1,)))
    current = level_fars(bottom_pattern, 1, 1, (0, 1))
    for level in (2, 3):
        partner = {flip: swapped(current[flip], level) for flip in (0, 1)}
        near = level_nears(bottom_blocks, bottom_pattern, level, level, (0, 1))
        if level == 2:
            current = level_fars(bottom_pattern, level, level, (0, 1))

    image_spread = jax.ShapeDtypeStruct((out_depth * rank, LANES), jnp.float32)
    image_wide = run(interp_kernel, [image_spread] * 2, (interp_out, near[0][0]))
    image = jax.ShapeDtypeStruct((out_depth, rhs_count, box_count), jnp.bfloat16)
    out = ()
    for flip in (0, 1):
        operands = (bottom_pattern, near[flip][1], image_wide[flip], partner[flip], near[flip][0])
        out = (run(
            functools.partial(last_kernel, 3, 3, flip), image, operands + out,
            (pltpu.VMEM((out_depth, rhs_count, LANES), jnp.bfloat16), total, pltpu.SemaphoreType.DMA((4,))), 3,
            [whole] * 5 + [anywhere] * flip, [anywhere], {5: 0} if flip else None,
        ),)
    return out[0]


def contract(weights, state):
    product = weights[:, :, None].astype(jnp.float32) * state[None].astype(jnp.float32)
    return jnp.sum(product, axis=1)


def plain_level(current, blocks, pattern, bit):
    rank = blocks.shape[0]
    partner = swapped(current, bit)
    is_lower = lax.axis_index("leaf") // 2**bit % 2 == 0
    lower = jnp.where(is_lower, current, partner)
    upper = jnp.where(is_lower, partner, current)
    weights = blocks * jnp.repeat(pattern, rank, axis=0).astype(jnp.bfloat16)[None]
    return contract(weights, jnp.concatenate([lower, upper], axis=0)).astype(jnp.bfloat16)


def plain_local(samples, interp_in, top_blocks, top_pattern, bottom_blocks, bottom_pattern, interp_out):
    bit_count = lax.axis_size("leaf").bit_length() - 1
    current = contract(interp_in, samples).astype(jnp.bfloat16)
    for level in range(top_blocks.shape[0]):
        current = plain_level(current, top_blocks[level], top_pattern[level], bit_count - 1 - level)
    flat = current.reshape(-1, current.shape[2])
    current = lax.all_to_all(flat, "leaf", split_axis=1, concat_axis=1, tiled=True).reshape(current.shape)
    for level in range(bottom_blocks.shape[0]):
        current = plain_level(current, bottom_blocks[level], bottom_pattern[level], level)
    return contract(interp_out, current).astype(jnp.bfloat16)


def local(samples, interp_in, top_blocks, *rest):
    four_digits = lax.axis_size("leaf") == 16 and top_blocks.shape[0] == 4
    chosen = fast_local if four_digits and samples.shape[1:] == (8, 2 * LANES) else plain_local
    return chosen(samples, interp_in, top_blocks, *rest)


def solution(mesh):
    boxes = ("parts", "leaf")
    return jax.shard_map(
        local,
        mesh=mesh,
        in_specs=(
            P(None, None, boxes),
            P(None, None, boxes),
            P(None, None, None, boxes),
            P(None, None, boxes),
            P(None, None, None, boxes),
            P(None, None, boxes),
            P(None, None, boxes),
        ),
        out_specs=P(None, None, boxes),
        check_vma=False,
    )
```

```python
import functools

import jax
import jax.numpy as jnp
from jax import lax
from jax.experimental import pallas as pl
from jax.experimental.pallas import tpu as pltpu
from jax.sharding import PartitionSpec as P

LANES = 128
GROUP = 4
KERNEL_COST = 1024
START_COST = 2**22


def digits():
    place = lax.axis_index("leaf")
    return lax.rem(place // 8, 2), lax.rem(place // 4, 2), lax.rem(place // 2, 2), lax.rem(place, 2)


def lanes_of(chunk):
    return pl.ds(pl.multiple_of(chunk * LANES, LANES), LANES)


def pick(chunk, read):
    near, far = read(lanes_of(chunk)).astype(jnp.float32), read(lanes_of(1 - chunk)).astype(jnp.float32)
    return merge(chunk, near, far)


def merge(number, near, far):
    side = lax.broadcasted_iota(jnp.int32, near.shape, near.ndim - 1) // (LANES // 2)
    return jnp.where(side == number, near, pltpu.roll(far, LANES // 2, near.ndim - 1))


def rows_of(half, rank):
    return pl.ds(pl.multiple_of(half * rank, rank), rank)


def spread(wide, load, row_count, rank):
    def body(step, carry):
        rows = load(step * GROUP).astype(jnp.float32)
        wide[pl.ds(step * GROUP * rank, GROUP * rank), :] = rows.reshape(GROUP * rank, LANES)
        return carry

    lax.fori_loop(0, row_count // GROUP, body, 0)


def multiply(wide, state, row_count, emit):
    rank = len(state)

    def body(step, carry):
        for inner in range(GROUP):
            sums = [None, None]
            for index in range(rank):
                weight = wide[pl.ds(step * GROUP * rank + inner * rank + index, 8, stride=0), :]
                term = weight * state[index]
                old = sums[index % 2]
                sums[index % 2] = term if old is None else old + term
            emit(step * GROUP + inner, sums[0] + sums[1])
        return carry

    lax.fori_loop(0, row_count // GROUP, body, 0)


def state_rows(ref, present=None):
    rows = [ref[index].astype(jnp.float32) for index in range(ref.shape[0])]
    return rows if present is None else [row * present for row in rows]


def level_load(blocks, level, half, chunk):
    rank = blocks.shape[1]
    return lambda row: pick(chunk, lambda lanes: blocks[level, pl.ds(row, GROUP), rows_of(half, rank), lanes])


def present_of(pattern, level, half, chunk):
    def read(lanes):
        pair = [pattern[level, place:place + 1, lanes].astype(jnp.float32) for place in range(2)]
        return jnp.broadcast_to(jnp.where(half == 0, pair[0], pair[1]), (8, LANES))

    return pick(chunk, read)


def coeff_kernel(interp, samples, first, second, wide, total):
    rank, depth = first.shape[0], samples.shape[0] // 2
    core = digits()[3]
    for turn in range(2):
        lanes = slice(turn * LANES, (turn + 1) * LANES)
        for half in range(2):
            part = slice(half * depth, (half + 1) * depth)
            spread(wide, lambda row: interp[pl.ds(row, GROUP), part, lanes], rank, depth)
            state = [samples[half * depth + index, :, lanes].astype(jnp.float32) for index in range(depth)]

            def emit(row, value):
                total[turn, row] = value if half == 0 else total[turn, row] + value

            multiply(wide, state, rank, emit)
    for row in range(rank):
        for out, chunk in ((first, 1 - core), (second, core)):
            out[row] = merge(chunk, total[chunk, row], total[1 - chunk, row]).astype(jnp.bfloat16)


def near_kernel(level, bit, flip, blocks, pattern, state, *rest):
    out, far_wide, wide = rest[-3:]
    places = digits()
    chunk, own = places[3] ^ flip, places[3 - bit]
    spread(wide, level_load(blocks, level, own, chunk), blocks.shape[1], blocks.shape[1])
    spread(far_wide, level_load(blocks, level, 1 - own, chunk), blocks.shape[1], blocks.shape[1])

    def emit(row, value):
        out[row] = value

    multiply(wide, state_rows(state, present_of(pattern, level, own, chunk)), blocks.shape[1], emit)


def far_kernel(level, bit, flip, pattern, partner, near, wide, out):
    places = digits()
    chunk, other = places[3] ^ flip, 1 - places[3 - bit]

    def emit(row, value):
        out[row] = (near[row] + value).astype(jnp.bfloat16)

    multiply(wide, state_rows(partner, present_of(pattern, level, other, chunk)), out.shape[0], emit)


def share_kernel(top_level, top_blocks, top_pattern, bottom_blocks, bottom_pattern, out):
    rank = top_blocks.shape[1]
    chunk = 1 - digits()[3]
    for place, (blocks, pattern, level) in enumerate(((top_blocks, top_pattern, top_level), (bottom_blocks, bottom_pattern, 0))):
        for half in range(2):
            present = present_of(pattern, level, half, chunk)[:1][None]
            load = level_load(blocks, level, half, chunk)

            def body(step, carry):
                span = pl.ds(place * rank + step * GROUP, GROUP)
                out[span, half * rank:(half + 1) * rank, :] = (load(step * GROUP) * present).astype(jnp.bfloat16)
                return carry

            lax.fori_loop(0, rank // GROUP, body, 0)


def shared_load(shared, place, half):
    rank = shared.shape[1] // 2
    return lambda row: shared[pl.ds(place * rank + row, GROUP), rows_of(half, rank), :]


def send_kernel(level, bit, flip, pattern, partner, near, wide, shared, out):
    rank, per = partner.shape[0], shared.shape[1] // partner.shape[1]
    places = digits()
    chunk, other = places[3] ^ flip, 1 - places[3 - bit]

    def emit(row, value):
        place = pl.ds(pl.multiple_of(lax.rem(row, per) * 8, 8), 8)
        out[2 * rank + row // per, place, :] = (near[row] + value).astype(jnp.bfloat16)

    multiply(wide, state_rows(partner, present_of(pattern, level, other, chunk)), rank, emit)


def sent_rows(shared):
    rank = shared.shape[1] // 2
    per = shared.shape[1] // 8
    return [
        shared[2 * rank + row // per, row % per * 8:(row % per + 1) * 8, :].astype(jnp.float32) for row in range(rank)
    ]


def swap_groups(tile, slot):
    lane_group = lax.broadcasted_iota(jnp.int32, tile[0].shape, 2) // slot
    step = 1
    while step < len(tile):
        low = (lane_group // step) % 2 == 0
        fresh = list(tile)
        for place in range(len(tile)):
            if place & step == 0:
                first, second = tile[place], tile[place + step]
                fresh[place] = jnp.where(low, first, pltpu.roll(second, step * slot, 2))
                fresh[place + step] = jnp.where(low, pltpu.roll(first, LANES - step * slot, 2), second)
        tile = fresh
        step *= 2
    return tile


def pair_near_kernel(level, blocks, pattern, shared, state, out, far_wide, wide):
    rank = blocks.shape[1]
    core = digits()[3]
    rows = state_rows(state)
    present = present_of(pattern, level, core, core)
    for box in range(2):
        for target, half in ((wide, core), (far_wide.at[box], 1 - core)):
            load = (
                level_load(blocks, level, half, core)
                if box == 0
                else shared_load(shared, 0, half)
            )
            spread(target, load, rank, rank)

        def emit(row, value):
            out[box, row] = value

        multiply(wide, [row * present for row in rows] if box == 0 else rows, rank, emit)


def pair_far_kernel(level, slot, pattern, wide, shared, near, *rest):
    outs, (total, packed) = rest[:4], rest[4:]
    rank = near.shape[1]
    high, _, low, core = digits()
    rows = sent_rows(shared)
    present = present_of(pattern, level, 1 - core, core)
    fold = LANES // slot
    for box in range(2):
        def emit(row, value):
            total[row] = near[box, row] + value

        multiply(wide.at[box], [row * present for row in rows] if box == 0 else rows, rank, emit)
        depth = rank // fold
        pieces = swap_groups([total[place * depth:(place + 1) * depth] for place in range(fold)], slot)
        for place, piece in enumerate(pieces):
            packed[core ^ box, place] = piece.astype(jnp.bfloat16)
    for turn, out in enumerate(outs):
        first = ((high ^ (turn // 2)) * 2 + (low ^ (turn % 2))) * 2
        for box in range(2):
            for last in range(2):
                out[box, last] = packed[box, first + last]


def wide_kernel(blocks, shared, own_wide, other_wide):
    rank = blocks.shape[1]
    core = digits()[3]
    for half in range(2):
        spread(own_wide.at[half], level_load(blocks, 0, half, core), rank, rank)
        spread(other_wide.at[half], shared_load(shared, 1, half), rank, rank)


def pair_box(wide, total, states, presents, out):
    for half in range(2):
        present = presents[half]
        rows = [states[half, index].astype(jnp.float32) for index in range(out.shape[0])]
        if present is not None:
            rows = [row * present for row in rows]

        def emit(row, value):
            if half == 0:
                total[row] = value
            else:
                out[row] = (total[row] + value).astype(jnp.bfloat16)

        multiply(wide.at[half], rows, out.shape[0], emit)


def open_kernel(slot, pattern, wide, *rest):
    pieces, (out, states, total, packed) = rest[:4], rest[4:]
    high, _, low, core = digits()
    fold = LANES // slot
    depth = out.shape[0] // fold
    for turn, piece in enumerate(pieces):
        first = ((high ^ (turn // 2)) * 2 + (low ^ (turn % 2))) * 2
        for box in range(2):
            for last in range(2):
                packed[last, first + box] = piece[box, last]
    for last in range(2):
        tile = swap_groups([packed[last, place].astype(jnp.float32) for place in range(fold)], slot)
        for place, rows in enumerate(tile):
            states[last, place * depth:(place + 1) * depth] = rows.astype(jnp.bfloat16)
    pair_box(wide, total, states, [present_of(pattern, 0, half, core) for half in range(2)], out)


def other_kernel(wide, states, out, total):
    pair_box(wide, total, states, (None, None), out)


def interp_kernel(interp, first_wide, second_wide):
    core = digits()[3]
    for wide, chunk in ((first_wide, core), (second_wide, 1 - core)):
        spread(wide, lambda row: pick(chunk, lambda lanes: interp[pl.ds(row, GROUP), :, lanes]), interp.shape[0], interp.shape[1])


def image_rows(level, bit, flip, pattern, wide, partner, near, total):
    places = digits()
    chunk, other = places[3] ^ flip, 1 - places[3 - bit]

    def emit(row, value):
        total[row] = (near[row] + value).astype(jnp.bfloat16).astype(jnp.float32)

    multiply(wide, state_rows(partner, present_of(pattern, level, other, chunk)), total.shape[0], emit)
    return [total[index] for index in range(total.shape[0])]


def first_image_kernel(level, bit, pattern, wide, image_wide, partner, near, out, total):
    rows = image_rows(level, bit, 0, pattern, wide, partner, near, total)

    def emit(row, value):
        out[row] = value

    multiply(image_wide, rows, out.shape[0], emit)


def last_kernel(level, bit, pattern, wide, image_wide, partner, near, ready, image, held, total, sems):
    core = digits()[3]
    rows = image_rows(level, bit, 1, pattern, wide, partner, near, total)
    rank, parts = total.shape[0], sems.shape[0]
    size = held.shape[0] // parts
    copies = []
    for part in range(parts):

        def emit(row, value):
            place = part * size + row
            first = ready[place]
            held[place, :, lanes_of(core)] = merge(core, first, value).astype(jnp.bfloat16)
            held[place, :, lanes_of(1 - core)] = merge(1 - core, value, first).astype(jnp.bfloat16)

        multiply(image_wide.at[pl.ds(part * size * rank, size * rank), :], rows, size, emit)
        span = pl.ds(part * size, size)
        copies.append(pltpu.make_async_copy(held.at[span], image.at[span], sems.at[part]))
        copies[-1].start()
    for copy in copies:
        copy.wait()


def run(kernel, outs, operands, scratch=(), products=1, in_specs=None, out_specs=None, aliases=None, limit=16 * 2**20, cost=KERNEL_COST):
    whole = pl.BlockSpec(memory_space=pltpu.VMEM)
    single = not isinstance(outs, list)
    shapes = [outs] if single else outs
    result = pl.pallas_call(
        kernel,
        out_shape=shapes,
        in_specs=in_specs or [whole] * len(operands),
        out_specs=out_specs or [whole] * len(shapes),
        scratch_shapes=list(scratch),
        input_output_aliases=aliases or {},
        compiler_params=pltpu.CompilerParams(vmem_limit_bytes=limit),
        cost_estimate=pl.CostEstimate(flops=products * cost, bytes_accessed=products * cost, transcendentals=0),
    )(*operands)
    return result[0] if single else result


def permuted(value, target_of):
    pairs = [(source, target_of(source)) for source in range(lax.axis_size("leaf"))]
    return lax.ppermute(value, "leaf", pairs)


def swapped(value, bit):
    return permuted(value, lambda source: source ^ 2**bit)


def crossed(source, turn):
    high, mid, low, core = source // 8 % 2, source // 4 % 2, source // 2 % 2, source % 2
    return (((high ^ (turn // 2)) * 2 + core) * 2 + (low ^ (turn % 2))) * 2 + mid


def fast_local(samples, interp_in, top_blocks, top_pattern, bottom_blocks, bottom_pattern, interp_out):
    rank, depth = interp_in.shape[:2]
    rhs_count, box_count = samples.shape[1:]
    out_depth = interp_out.shape[0]
    slot = box_count // lax.axis_size("leaf")
    fold = LANES // slot
    state = jax.ShapeDtypeStruct((rank, rhs_count, LANES), jnp.bfloat16)
    partial = jax.ShapeDtypeStruct((rank, rhs_count, LANES), jnp.float32)
    spread_out = jax.ShapeDtypeStruct((rank * rank, LANES), jnp.float32)
    pair_spread = jax.ShapeDtypeStruct((2, rank * rank, LANES), jnp.float32)
    total = pltpu.VMEM((rank, rhs_count, LANES), jnp.float32)
    wide = pltpu.VMEM((rank * rank, LANES), jnp.float32)
    packed = pltpu.VMEM((2, fold, rank // fold, rhs_count, LANES), jnp.bfloat16)

    def level_nears(blocks, pattern, level, bit, order, extra=()):
        return {
            flip: run(
                functools.partial(near_kernel, level, bit, flip), [partial, spread_out],
                (blocks, pattern, current[flip]) + ((current[1 - flip], *extra) if place < len(order) - 1 else ()), (wide,),
            )
            for place, flip in enumerate(order)
        }

    def level_fars(pattern, level, bit, order):
        return {
            flip: run(
                functools.partial(far_kernel, level, bit, flip), state, (pattern, partner[flip], *near[flip]),
            )
            for flip in order
        }

    current = {}
    current[1], current[0] = run(
        coeff_kernel, [state, state], (interp_in, samples),
        (pltpu.VMEM((rank * depth // 2, LANES), jnp.float32), pltpu.VMEM((2, rank, rhs_count, LANES), jnp.float32)),
        4, cost=START_COST,
    )
    share_rows = 2 * rank + rank * rhs_count // (2 * rank)
    shared_shape = jax.ShapeDtypeStruct((share_rows, 2 * rank, LANES), jnp.bfloat16)
    shared = run(functools.partial(share_kernel, 3), shared_shape, (top_blocks, top_pattern, bottom_blocks, bottom_pattern))
    for level in range(3):
        bit = 3 - level
        partner = {flip: swapped(current[flip], bit) for flip in (1, 0)}
        near = level_nears(top_blocks, top_pattern, level, bit, (1, 0), (shared,) if level == 1 else ())
        if level < 2:
            current = level_fars(top_pattern, level, bit, (1, 0))

    shared = run(
        functools.partial(send_kernel, 2, 1, 1), shared_shape, (top_pattern, partner[1], *near[1], shared), aliases={4: 0},
    )
    shared = swapped(shared, 0)
    current = level_fars(top_pattern, 2, 1, (0,))

    pair_near = run(
        functools.partial(pair_near_kernel, 3),
        [jax.ShapeDtypeStruct((2, rank, rhs_count, LANES), jnp.float32), pair_spread],
        (top_blocks, top_pattern, shared, current[0]), (wide,), 2,
    )
    piece = jax.ShapeDtypeStruct((2, 2, rank // fold, rhs_count, LANES), jnp.bfloat16)
    pieces = run(
        functools.partial(pair_far_kernel, 3, slot), [piece] * 4,
        (top_pattern, pair_near[1], shared, pair_near[0]), (total, packed), 2,
    )
    pieces = [permuted(value, functools.partial(crossed, turn=turn)) for turn, value in enumerate(pieces)]
    own_wide, other_wide = run(wide_kernel, [pair_spread] * 2, (bottom_blocks, shared))
    first, states = run(
        functools.partial(open_kernel, slot), [state, jax.ShapeDtypeStruct((2, rank, rhs_count, LANES), jnp.bfloat16)],
        (bottom_pattern, own_wide, *pieces), (total, packed), 2,
    )
    current = {0: first}
    partner = {0: swapped(first, 1)}
    near = level_nears(bottom_blocks, bottom_pattern, 1, 1, (0,))
    current[1] = swapped(run(other_kernel, state, (other_wide, states), (total,), 2), 0)
    partner[1] = swapped(current[1], 1)
    near.update(level_nears(bottom_blocks, bottom_pattern, 1, 1, (1,)))
    current = level_fars(bottom_pattern, 1, 1, (0, 1))
    image_spread = jax.ShapeDtypeStruct((out_depth * rank, LANES), jnp.float32)
    image_wide = run(interp_kernel, [image_spread] * 2, (interp_out,))
    for level in (2, 3):
        partner = {flip: swapped(current[flip], level) for flip in (0, 1)}
        near = level_nears(bottom_blocks, bottom_pattern, level, level, (0, 1), image_wide)
        if level == 2:
            current = level_fars(bottom_pattern, level, level, (0, 1))

    ready = run(
        functools.partial(first_image_kernel, 3, 3), jax.ShapeDtypeStruct((out_depth, rhs_count, LANES), jnp.float32),
        (bottom_pattern, near[0][1], image_wide[0], partner[0], near[0][0]), (total,), 3,
    )
    return run(
        functools.partial(last_kernel, 3, 3), jax.ShapeDtypeStruct((out_depth, rhs_count, box_count), jnp.bfloat16),
        (bottom_pattern, near[1][1], image_wide[1], partner[1], near[1][0], ready),
        (pltpu.VMEM((out_depth, rhs_count, box_count), jnp.bfloat16), total, pltpu.SemaphoreType.DMA((4,))), 3,
        out_specs=[pl.BlockSpec(memory_space=pl.ANY)],
    )


def contract(weights, state):
    product = weights[:, :, None].astype(jnp.float32) * state[None].astype(jnp.float32)
    return jnp.sum(product, axis=1)


def plain_level(current, blocks, pattern, bit):
    rank = blocks.shape[0]
    partner = swapped(current, bit)
    is_lower = lax.axis_index("leaf") // 2**bit % 2 == 0
    lower = jnp.where(is_lower, current, partner)
    upper = jnp.where(is_lower, partner, current)
    weights = blocks * jnp.repeat(pattern, rank, axis=0).astype(jnp.bfloat16)[None]
    return contract(weights, jnp.concatenate([lower, upper], axis=0)).astype(jnp.bfloat16)


def plain_local(samples, interp_in, top_blocks, top_pattern, bottom_blocks, bottom_pattern, interp_out):
    bit_count = lax.axis_size("leaf").bit_length() - 1
    current = contract(interp_in, samples).astype(jnp.bfloat16)
    for level in range(top_blocks.shape[0]):
        current = plain_level(current, top_blocks[level], top_pattern[level], bit_count - 1 - level)
    flat = current.reshape(-1, current.shape[2])
    current = lax.all_to_all(flat, "leaf", split_axis=1, concat_axis=1, tiled=True).reshape(current.shape)
    for level in range(bottom_blocks.shape[0]):
        current = plain_level(current, bottom_blocks[level], bottom_pattern[level], level)
    return contract(interp_out, current).astype(jnp.bfloat16)


def local(samples, interp_in, top_blocks, *rest):
    four_digits = lax.axis_size("leaf") == 16 and top_blocks.shape[0] == 4
    chosen = fast_local if four_digits and samples.shape[1:] == (8, 2 * LANES) else plain_local
    return chosen(samples, interp_in, top_blocks, *rest)


def solution(mesh):
    boxes = ("parts", "leaf")
    return jax.shard_map(
        local,
        mesh=mesh,
        in_specs=(
            P(None, None, boxes),
            P(None, None, boxes),
            P(None, None, None, boxes),
            P(None, None, boxes),
            P(None, None, None, boxes),
            P(None, None, boxes),
            P(None, None, boxes),
        ),
        out_specs=P(None, None, boxes),
        check_vma=False,
    )
```

```python
import functools

import jax
import jax.numpy as jnp
from jax import lax
from jax.experimental import pallas as pl
from jax.experimental.pallas import tpu as pltpu
from jax.sharding import PartitionSpec as P

LANES = 128
GROUP = 4
KERNEL_COST = 1024
KERNEL_LIMIT = 16 * 2**20
FETCH_LIMIT = 53_000_000


def digits():
    place = lax.axis_index("leaf")
    return lax.rem(place // 8, 2), lax.rem(place // 4, 2), lax.rem(place // 2, 2), lax.rem(place, 2)


def lanes_of(chunk):
    return pl.ds(pl.multiple_of(chunk * LANES, LANES), LANES)


def rows_of(half, rank):
    return pl.ds(pl.multiple_of(half * rank, rank), rank)


def spread(wide, load, row_count, rank):
    def body(step, carry):
        rows = load(step * GROUP).astype(jnp.float32)
        wide[pl.ds(step * GROUP * rank, GROUP * rank), :] = rows.reshape(GROUP * rank, LANES)
        return carry

    lax.fori_loop(0, row_count // GROUP, body, 0)


def multiply(wide, state, row_count, emit):
    rank = len(state)

    def body(step, carry):
        for inner in range(GROUP):
            sums = [None, None]
            for index in range(rank):
                weight = wide[pl.ds(step * GROUP * rank + inner * rank + index, 8, stride=0), :]
                term = weight * state[index]
                old = sums[index % 2]
                sums[index % 2] = term if old is None else old + term
            emit(step * GROUP + inner, sums[0] + sums[1])
        return carry

    lax.fori_loop(0, row_count // GROUP, body, 0)


def state_rows(ref, present=None):
    rows = [ref[index].astype(jnp.float32) for index in range(ref.shape[0])]
    return rows if present is None else [row * present for row in rows]


def level_load(blocks, level, half, chunk):
    rank = blocks.shape[1]
    return lambda row: blocks[level, pl.ds(row, GROUP), rows_of(half, rank), lanes_of(chunk)]


def present_of(pattern, level, half, chunk):
    pair = [pattern[level, place:place + 1, lanes_of(chunk)].astype(jnp.float32) for place in range(2)]
    return jnp.where(half == 0, pair[0], pair[1])


def coeff_kernel(flip, interp, samples, out, wide, total):
    rank, depth = interp.shape[0], interp.shape[1] // 2
    lanes = lanes_of(digits()[3] ^ flip)
    for half in range(2):
        part = slice(half * depth, (half + 1) * depth)
        spread(wide, lambda row: interp[pl.ds(row, GROUP), part, lanes], rank, depth)
        state = [samples[half * depth + index, :, lanes].astype(jnp.float32) for index in range(depth)]

        def emit(row, value):
            if half == 0:
                total[row] = value
            else:
                out[row] = (total[row] + value).astype(jnp.bfloat16)

        multiply(wide, state, rank, emit)


def fetch_kernel(level, bit, blocks, after, *rest):
    held, sem = rest[-2:]
    copy = pltpu.make_async_copy(blocks.at[pl.ds(level, 1)], held, sem)
    copy.start()
    copy.wait()
    ahead_kernel(0, bit, held, *rest[:-2])


def ahead_kernel(level, bit, blocks, *rest):
    near_wides, far_wides = rest[-4:-2], rest[-2:]
    rank = blocks.shape[1]
    places = digits()
    own = places[3 - bit]
    for flip in range(2):
        chunk = places[3] ^ flip
        spread(near_wides[flip], level_load(blocks, level, own, chunk), rank, rank)
        spread(far_wides[flip], level_load(blocks, level, 1 - own, chunk), rank, rank)


def near_kernel(level, bit, flip, pattern, state, wide, *rest):
    out = rest[-1]
    places = digits()
    chunk, own = places[3] ^ flip, places[3 - bit]

    def emit(row, value):
        out[row] = value

    multiply(wide, state_rows(state, present_of(pattern, level, own, chunk)), out.shape[0], emit)


def far_kernel(level, bit, flip, pattern, partner, near, wide, out):
    places = digits()
    chunk, other = places[3] ^ flip, 1 - places[3 - bit]

    def emit(row, value):
        out[row] = (near[row] + value).astype(jnp.bfloat16)

    multiply(wide, state_rows(partner, present_of(pattern, level, other, chunk)), out.shape[0], emit)


def share_kernel(top_level, top_blocks, top_pattern, bottom_blocks, bottom_pattern, out):
    rank = top_blocks.shape[1]
    chunk = 1 - digits()[3]
    for place, (blocks, pattern, level) in enumerate(((top_blocks, top_pattern, top_level), (bottom_blocks, bottom_pattern, 0))):
        for half in range(2):
            present = present_of(pattern, level, half, chunk)[None]

            def body(row, carry):
                rows = blocks[level, pl.ds(row, 1), half * rank:(half + 1) * rank, lanes_of(chunk)]
                out[place * rank + row, half * rank:(half + 1) * rank, :] = (rows.astype(jnp.float32) * present)[0].astype(jnp.bfloat16)
                return carry

            lax.fori_loop(0, rank, body, 0)


def shared_load(shared, place, half):
    rank = shared.shape[1] // 2
    return lambda row: shared[pl.ds(place * rank + row, GROUP), rows_of(half, rank), :]


def send_kernel(level, bit, flip, pattern, partner, near, wide, shared, out):
    rank, per = partner.shape[0], shared.shape[1] // partner.shape[1]
    places = digits()
    chunk, other = places[3] ^ flip, 1 - places[3 - bit]

    def emit(row, value):
        place = pl.ds(pl.multiple_of(lax.rem(row, per) * 8, 8), 8)
        out[2 * rank + row // per, place, :] = (near[row] + value).astype(jnp.bfloat16)

    multiply(wide, state_rows(partner, present_of(pattern, level, other, chunk)), rank, emit)


def sent_rows(shared):
    rank = shared.shape[1] // 2
    per = shared.shape[1] // 8
    return [
        shared[2 * rank + row // per, row % per * 8:(row % per + 1) * 8, :].astype(jnp.float32) for row in range(rank)
    ]


def swap_groups(tile, slot):
    lane_group = lax.broadcasted_iota(jnp.int32, tile[0].shape, 2) // slot
    step = 1
    while step < len(tile):
        low = (lane_group // step) % 2 == 0
        fresh = list(tile)
        for place in range(len(tile)):
            if place & step == 0:
                first, second = tile[place], tile[place + step]
                fresh[place] = jnp.where(low, first, pltpu.roll(second, step * slot, 2))
                fresh[place + step] = jnp.where(low, pltpu.roll(first, LANES - step * slot, 2), second)
        tile = fresh
        step *= 2
    return tile


def pair_near_kernel(level, blocks, pattern, shared, state, out, far_wide, wide):
    rank = blocks.shape[1]
    core = digits()[3]
    rows = state_rows(state)
    present = present_of(pattern, level, core, core)
    for box in range(2):
        for target, half in ((wide, core), (far_wide.at[box], 1 - core)):
            load = (
                level_load(blocks, level, half, core)
                if box == 0
                else shared_load(shared, 0, half)
            )
            spread(target, load, rank, rank)

        def emit(row, value):
            out[box, row] = value

        multiply(wide, [row * present for row in rows] if box == 0 else rows, rank, emit)


def pair_far_kernel(level, slot, pattern, wide, shared, near, *rest):
    outs, (total, packed) = rest[:4], rest[4:]
    rank = near.shape[1]
    _, mid, low, core = digits()
    rows = sent_rows(shared)
    present = present_of(pattern, level, 1 - core, core)
    fold = LANES // slot
    for box in range(2):
        def emit(row, value):
            total[row] = near[box, row] + value

        multiply(wide.at[box], [row * present for row in rows] if box == 0 else rows, rank, emit)
        depth = rank // fold
        pieces = swap_groups([total[place * depth:(place + 1) * depth] for place in range(fold)], slot)
        for place, piece in enumerate(pieces):
            packed[core ^ box, place] = piece.astype(jnp.bfloat16)
    for turn, out in enumerate(outs):
        first = ((mid ^ (turn // 2)) * 2 + (low ^ (turn % 2))) * 2
        for box in range(2):
            for last in range(2):
                out[box, last] = packed[box, first + last]


def wide_kernel(blocks, shared, own_wide, other_wide):
    rank = blocks.shape[1]
    core = digits()[3]
    for half in range(2):
        spread(own_wide.at[half], level_load(blocks, 0, half, core), rank, rank)
        spread(other_wide.at[half], shared_load(shared, 1, half), rank, rank)


def pair_box(wide, total, states, presents, out):
    for half in range(2):
        present = presents[half]
        rows = [states[half, index].astype(jnp.float32) for index in range(out.shape[0])]
        if present is not None:
            rows = [row * present for row in rows]

        def emit(row, value):
            if half == 0:
                total[row] = value
            else:
                out[row] = (total[row] + value).astype(jnp.bfloat16)

        multiply(wide.at[half], rows, out.shape[0], emit)


def open_kernel(slot, pattern, wide, *rest):
    pieces, (out, states, total, packed) = rest[:4], rest[-4:]
    _, mid, low, core = digits()
    fold = LANES // slot
    depth = out.shape[0] // fold
    for turn, piece in enumerate(pieces):
        first = ((mid ^ (turn // 2)) * 2 + (low ^ (turn % 2))) * 2
        for box in range(2):
            for last in range(2):
                packed[last, first + box] = piece[box, last]
    for last in range(2):
        tile = swap_groups([packed[last, place].astype(jnp.float32) for place in range(fold)], slot)
        for place, rows in enumerate(tile):
            states[last, place * depth:(place + 1) * depth] = rows.astype(jnp.bfloat16)
    pair_box(wide, total, states, [present_of(pattern, 0, half, core) for half in range(2)], out)


def other_kernel(wide, states, out, total):
    pair_box(wide, total, states, (None, None), out)


def interp_kernel(interp, first_wide, second_wide):
    core = digits()[3]
    for wide, chunk in ((first_wide, core), (second_wide, 1 - core)):
        spread(wide, lambda row: interp[pl.ds(row, GROUP), :, lanes_of(chunk)], interp.shape[0], interp.shape[1])


def image_rows(level, bit, flip, pattern, wide, partner, near, total):
    places = digits()
    chunk, other = places[3] ^ flip, 1 - places[3 - bit]

    def emit(row, value):
        total[row] = (near[row] + value).astype(jnp.bfloat16).astype(jnp.float32)

    multiply(wide, state_rows(partner, present_of(pattern, level, other, chunk)), total.shape[0], emit)
    return [total[index] for index in range(total.shape[0])]


def first_image_kernel(level, bit, pattern, wide, image_wide, partner, near, out, total):
    rows = image_rows(level, bit, 0, pattern, wide, partner, near, total)

    def emit(row, value):
        out[row] = value.astype(jnp.bfloat16)

    multiply(image_wide, rows, out.shape[0], emit)


def last_kernel(level, bit, pattern, wide, image_wide, partner, near, ready, image, held, total, sems):
    core = digits()[3]
    copies = [pltpu.make_async_copy(ready, image.at[:, :, lanes_of(core)], sems.at[0])]
    copies[0].start()
    rows = image_rows(level, bit, 1, pattern, wide, partner, near, total)
    rank, parts = total.shape[0], sems.shape[0] - 1
    size = held.shape[0] // parts
    for part in range(parts):

        def emit(row, value):
            held[part * size + row] = value.astype(jnp.bfloat16)

        multiply(image_wide.at[pl.ds(part * size * rank, size * rank), :], rows, size, emit)
        span = pl.ds(part * size, size)
        copies.append(pltpu.make_async_copy(held.at[span], image.at[span, :, lanes_of(1 - core)], sems.at[part + 1]))
        copies[-1].start()
    for copy in copies:
        copy.wait()


def run(kernel, outs, operands, scratch=(), products=1, in_specs=None, out_specs=None, aliases=None, limit=KERNEL_LIMIT):
    whole = pl.BlockSpec(memory_space=pltpu.VMEM)
    single = not isinstance(outs, list)
    shapes = [outs] if single else outs
    result = pl.pallas_call(
        kernel,
        out_shape=shapes,
        in_specs=in_specs or [whole] * len(operands),
        out_specs=out_specs or [whole] * len(shapes),
        scratch_shapes=list(scratch),
        input_output_aliases=aliases or {},
        compiler_params=pltpu.CompilerParams(vmem_limit_bytes=limit),
        cost_estimate=pl.CostEstimate(flops=products * KERNEL_COST, bytes_accessed=products * KERNEL_COST, transcendentals=0),
    )(*operands)
    return result[0] if single else result


def permuted(value, target_of):
    pairs = [(source, target_of(source)) for source in range(lax.axis_size("leaf"))]
    return lax.ppermute(value, "leaf", pairs)


def swapped(value, bit):
    return permuted(value, lambda source: source ^ 2**bit)


def crossed(source, turn):
    high, mid, low, core = source // 8 % 2, source // 4 % 2, source // 2 % 2, source % 2
    return ((core * 2 + (mid ^ (turn // 2))) * 2 + (low ^ (turn % 2))) * 2 + high


def fast_local(samples, interp_in, top_blocks, top_pattern, bottom_blocks, bottom_pattern, interp_out):
    rank, depth = interp_in.shape[:2]
    rhs_count, box_count = samples.shape[1:]
    out_depth = interp_out.shape[0]
    slot = box_count // lax.axis_size("leaf")
    fold = LANES // slot
    state = jax.ShapeDtypeStruct((rank, rhs_count, LANES), jnp.bfloat16)
    partial = jax.ShapeDtypeStruct((rank, rhs_count, LANES), jnp.float32)
    spread_out = jax.ShapeDtypeStruct((rank * rank, LANES), jnp.float32)
    pair_spread = jax.ShapeDtypeStruct((2, rank * rank, LANES), jnp.float32)
    total = pltpu.VMEM((rank, rhs_count, LANES), jnp.float32)
    wide = pltpu.VMEM((rank * rank, LANES), jnp.float32)
    packed = pltpu.VMEM((2, fold, rank // fold, rhs_count, LANES), jnp.bfloat16)

    def level_wides(blocks, level, bit, *after):
        wides = run(functools.partial(ahead_kernel, level, bit), [spread_out] * 4, (blocks, *after), products=4)
        return wides[:2], wides[2:]

    def level_nears(pattern, level, bit, order, wides, extra=()):
        return {
            flip: run(
                functools.partial(near_kernel, level, bit, flip), partial,
                (pattern, current[flip], wides[0][flip]) + ((current[1 - flip], *extra) if place < len(order) - 1 else ()),
            )
            for place, flip in enumerate(order)
        }

    def level_fars(pattern, level, bit, order, wides):
        return {
            flip: run(
                functools.partial(far_kernel, level, bit, flip), state,
                (pattern, partner[flip], near[flip], wides[1][flip]),
            )
            for flip in order
        }

    current = {
        flip: run(
            functools.partial(coeff_kernel, flip), state, (interp_in, samples),
            (pltpu.VMEM((rank * depth // 2, LANES), jnp.float32), total), 2,
        )
        for flip in (1, 0)
    }
    share_rows = 2 * rank + rank * rhs_count // (2 * rank)
    shared_shape = jax.ShapeDtypeStruct((share_rows, 2 * rank, LANES), jnp.bfloat16)
    for level in range(3):
        bit = 3 - level
        partner = {flip: swapped(current[flip], bit) for flip in (1, 0)}
        if level == 0:
            wides = run(
                functools.partial(fetch_kernel, 0, 3), [spread_out] * 4, (top_blocks, current[0]),
                (pltpu.VMEM((1, *top_blocks.shape[1:]), jnp.bfloat16), pltpu.SemaphoreType.DMA), 4,
                in_specs=[pl.BlockSpec(memory_space=pl.ANY), pl.BlockSpec(memory_space=pltpu.VMEM)], limit=FETCH_LIMIT,
            )
            wides = wides[:2], wides[2:]
        else:
            wides = later_wides[level]
        near = level_nears(top_pattern, level, bit, (1, 0), wides)
        if level == 0:
            later_wides = {later: level_wides(top_blocks, later, 3 - later, near[0]) for later in (1, 2)}
            shared = run(
                functools.partial(share_kernel, 3), shared_shape,
                (top_blocks, top_pattern, bottom_blocks, bottom_pattern),
            )
        if level < 2:
            current = level_fars(top_pattern, level, bit, (1, 0), wides)

    shared = run(
        functools.partial(send_kernel, 2, 1, 1), shared_shape, (top_pattern, partner[1], near[1], wides[1][1], shared), aliases={4: 0},
    )
    shared = swapped(shared, 0)
    current = level_fars(top_pattern, 2, 1, (0,), wides)

    pair_near = run(
        functools.partial(pair_near_kernel, 3),
        [jax.ShapeDtypeStruct((2, rank, rhs_count, LANES), jnp.float32), pair_spread],
        (top_blocks, top_pattern, shared, current[0]), (wide,), 2,
    )
    piece = jax.ShapeDtypeStruct((2, 2, rank // fold, rhs_count, LANES), jnp.bfloat16)
    pieces = run(
        functools.partial(pair_far_kernel, 3, slot), [piece] * 4,
        (top_pattern, pair_near[1], shared, pair_near[0]), (total, packed), 2,
    )
    pieces = [permuted(value, functools.partial(crossed, turn=turn)) for turn, value in enumerate(pieces)]
    own_wide, other_wide = run(wide_kernel, [pair_spread] * 2, (bottom_blocks, shared))
    wides = {level: level_wides(bottom_blocks, level, level, pair_near[0]) for level in (1, 2, 3)}
    image_spread = jax.ShapeDtypeStruct((out_depth * rank, LANES), jnp.float32)
    image_wide = run(interp_kernel, [image_spread] * 2, (interp_out,))
    spreads = [wide for level in (1, 2, 3) for group in wides[level] for wide in group]
    first, states = run(
        functools.partial(open_kernel, slot), [state, jax.ShapeDtypeStruct((2, rank, rhs_count, LANES), jnp.bfloat16)],
        (bottom_pattern, own_wide, *pieces, *spreads, *image_wide), (total, packed), 2,
    )
    current = {0: first}
    partner = {0: swapped(first, 1)}
    current[1] = swapped(run(other_kernel, state, (other_wide, states), (total,), 2), 0)
    partner[1] = swapped(current[1], 1)
    for level in (1, 2, 3):
        if level > 1:
            partner = {flip: swapped(current[flip], level) for flip in (0, 1)}
        near = level_nears(bottom_pattern, level, level, (0, 1), wides[level])
        if level < 3:
            current = level_fars(bottom_pattern, level, level, (0, 1), wides[level])

    ready = run(
        functools.partial(first_image_kernel, 3, 3), jax.ShapeDtypeStruct((out_depth, rhs_count, LANES), jnp.bfloat16),
        (bottom_pattern, wides[3][1][0], image_wide[0], partner[0], near[0]), (total,), 3,
    )
    return run(
        functools.partial(last_kernel, 3, 3), jax.ShapeDtypeStruct((out_depth, rhs_count, box_count), jnp.bfloat16),
        (bottom_pattern, wides[3][1][1], image_wide[1], partner[1], near[1], ready),
        (pltpu.VMEM((out_depth, rhs_count, LANES), jnp.bfloat16), total, pltpu.SemaphoreType.DMA((5,))), 3,
        out_specs=[pl.BlockSpec(memory_space=pl.ANY)],
    )


def contract(weights, state):
    product = weights[:, :, None].astype(jnp.float32) * state[None].astype(jnp.float32)
    return jnp.sum(product, axis=1)


def plain_level(current, blocks, pattern, bit):
    rank = blocks.shape[0]
    partner = swapped(current, bit)
    is_lower = lax.axis_index("leaf") // 2**bit % 2 == 0
    lower = jnp.where(is_lower, current, partner)
    upper = jnp.where(is_lower, partner, current)
    weights = blocks * jnp.repeat(pattern, rank, axis=0).astype(jnp.bfloat16)[None]
    return contract(weights, jnp.concatenate([lower, upper], axis=0)).astype(jnp.bfloat16)


def plain_local(samples, interp_in, top_blocks, top_pattern, bottom_blocks, bottom_pattern, interp_out):
    bit_count = lax.axis_size("leaf").bit_length() - 1
    current = contract(interp_in, samples).astype(jnp.bfloat16)
    for level in range(top_blocks.shape[0]):
        current = plain_level(current, top_blocks[level], top_pattern[level], bit_count - 1 - level)
    flat = current.reshape(-1, current.shape[2])
    current = lax.all_to_all(flat, "leaf", split_axis=1, concat_axis=1, tiled=True).reshape(current.shape)
    for level in range(bottom_blocks.shape[0]):
        current = plain_level(current, bottom_blocks[level], bottom_pattern[level], level)
    return contract(interp_out, current).astype(jnp.bfloat16)


def local(samples, interp_in, top_blocks, *rest):
    four_digits = lax.axis_size("leaf") == 16 and top_blocks.shape[0] == 4
    chosen = fast_local if four_digits and samples.shape[1:] == (8, 2 * LANES) else plain_local
    return chosen(samples, interp_in, top_blocks, *rest)


def solution(mesh):
    boxes = ("parts", "leaf")
    return jax.shard_map(
        local,
        mesh=mesh,
        in_specs=(
            P(None, None, boxes),
            P(None, None, boxes),
            P(None, None, None, boxes),
            P(None, None, boxes),
            P(None, None, None, boxes),
            P(None, None, boxes),
            P(None, None, boxes),
        ),
        out_specs=P(None, None, boxes),
        check_vma=False,
    )
```

```python
import functools

import jax
import jax.numpy as jnp
from jax import lax
from jax.experimental import pallas as pl
from jax.experimental.pallas import tpu as pltpu
from jax.sharding import PartitionSpec as P

LANES = 128
GROUP = 4
KERNEL_COST = 1024
KERNEL_LIMIT = 16 * 2**20
FETCH_LIMIT = 53_000_000


def digits():
    place = lax.axis_index("leaf")
    return lax.rem(place // 8, 2), lax.rem(place // 4, 2), lax.rem(place // 2, 2), lax.rem(place, 2)


def lanes_of(chunk):
    return pl.ds(pl.multiple_of(chunk * LANES, LANES), LANES)


def order_matrix(slot, width, start, back=False):
    lie = lax.broadcasted_iota(jnp.int32, (2 * LANES, width), 1 if back else 0)
    new = lax.broadcasted_iota(jnp.int32, (2 * LANES, width), 0 if back else 1) + start
    half, group, place = new // LANES, new % LANES // (slot // 2), new % (slot // 2)
    return (lie == group * slot + half * (slot // 2) + place).astype(jnp.float32).astype(jnp.bfloat16)


def reorder(rows, matrix):
    return jnp.dot(rows, matrix, preferred_element_type=jnp.float32)


def multiply(wide, state, row_count, emit):
    rank = len(state)

    def body(step, carry):
        for inner in range(GROUP):
            sums = [None, None]
            for index in range(rank):
                weight = wide[pl.ds(step * GROUP * rank + inner * rank + index, 8, stride=0), :]
                term = weight * state[index]
                old = sums[index % 2]
                sums[index % 2] = term if old is None else old + term
            emit(step * GROUP + inner, sums[0] + sums[1])
        return carry

    lax.fori_loop(0, row_count // GROUP, body, 0)


def state_rows(ref, present=None):
    rows = [ref[index].astype(jnp.float32) for index in range(ref.shape[0])]
    return rows if present is None else [row * present for row in rows]


def coeff_kernel(flip, slot, interp, samples, out, wide, held, total):
    rank, depth = interp.shape[0], interp.shape[1] // 2
    rhs_count = samples.shape[1]
    chunk = digits()[3] ^ flip
    matrix = order_matrix(slot, LANES, chunk * LANES)
    held[...] = reorder(samples[...].reshape(2 * depth * rhs_count, 2 * LANES), matrix)
    for half in range(2):
        part = slice(half * depth, (half + 1) * depth)

        def body(step, carry):
            rows = interp[pl.ds(step * 8, 8), part, :].reshape(8 * depth, 2 * LANES)
            wide[pl.ds(step * 8 * depth, 8 * depth), :] = reorder(rows, matrix)
            return carry

        lax.fori_loop(0, rank // 8, body, 0)
        state = [held[(half * depth + index) * rhs_count:(half * depth + index + 1) * rhs_count, :] for index in range(depth)]

        def emit(row, value):
            if half == 0:
                total[row] = value
            else:
                out[row] = (total[row] + value).astype(jnp.bfloat16)

        multiply(wide, state, rank, emit)


def spread(wide, rows_at, row_count, matrix):
    def body(step, carry):
        rows = rows_at(step * 8)
        span = pl.ds(pl.multiple_of(step * rows.shape[0], 8), rows.shape[0])
        both = reorder(rows, matrix)
        wide[0, span, :] = both[:, :LANES]
        wide[1, span, :] = both[:, LANES:]
        return carry

    lax.fori_loop(0, row_count // 8, body, 0)


def spread_level(blocks, level, matrix, wide):
    rank = blocks.shape[1]
    for half in range(2):
        columns = slice(half * rank, (half + 1) * rank)
        spread(
            wide.at[half],
            lambda row: blocks[level, pl.ds(row, 8), columns, :].reshape(8 * rank, 2 * LANES),
            rank, matrix,
        )


def fetch_kernel(slot, blocks, top_pattern, bottom_pattern, after, wide, matrix, back, top_present, bottom_present, held, sem):
    copy = pltpu.make_async_copy(blocks.at[pl.ds(0, 1)], held, sem)
    copy.start()
    matrix[...] = order_matrix(slot, 2 * LANES, 0)
    back[...] = order_matrix(slot, 2 * LANES, 0, True)
    for pattern, present in ((top_pattern, top_present), (bottom_pattern, bottom_present)):
        for level in range(pattern.shape[0]):
            for half in range(2):
                row = pattern[level, half:half + 1, :].astype(jnp.float32)
                both = reorder(jnp.broadcast_to(row, (16, 2 * LANES)).astype(jnp.bfloat16), matrix[...])
                present[0, level, half] = both[:8, :LANES]
                present[1, level, half] = both[:8, LANES:]
    copy.wait()
    spread_level(held, 0, matrix[...], wide)


def ahead_kernel(level, blocks, matrix, *rest):
    spread_level(blocks, level, matrix[...], rest[-1])


def near_kernel(level, bit, flip, present, state, wide, *rest):
    out = rest[-1]
    places = digits()
    chunk, own = places[3] ^ flip, places[3 - bit]

    def emit(row, value):
        out[row] = value

    multiply(wide.at[own, chunk], state_rows(state, present[chunk, level, own]), out.shape[0], emit)


def far_kernel(level, bit, flip, present, partner, near, wide, out):
    places = digits()
    chunk, other = places[3] ^ flip, 1 - places[3 - bit]

    def emit(row, value):
        out[row] = (near[row] + value).astype(jnp.bfloat16)

    multiply(wide.at[other, chunk], state_rows(partner, present[chunk, level, other]), out.shape[0], emit)


def share_kernel(top_level, top_wide, top_present, bottom_wide, bottom_present, *rest):
    out = rest[-1]
    rank = out.shape[1] // 2
    chunk = 1 - digits()[3]
    for place, (wide, present, level) in enumerate(((top_wide, top_present, top_level), (bottom_wide, bottom_present, 0))):
        for half in range(2):
            mask = present[chunk, level, half][:1]

            def body(step, carry):
                rows = wide[half, chunk, pl.ds(pl.multiple_of(step * GROUP * rank, 8), GROUP * rank), :] * mask
                span = pl.ds(place * rank + step * GROUP, GROUP)
                out[span, half * rank:(half + 1) * rank, :] = rows.reshape(GROUP, rank, LANES).astype(jnp.bfloat16)
                return carry

            lax.fori_loop(0, rank // GROUP, body, 0)


def widen_shared(shared, place, half, wide):
    rank = shared.shape[1] // 2

    def body(step, carry):
        rows = shared[pl.ds(place * rank + step * GROUP, GROUP), half * rank:(half + 1) * rank, :].astype(jnp.float32)
        wide[pl.ds(pl.multiple_of(step * GROUP * rank, 8), GROUP * rank), :] = rows.reshape(GROUP * rank, LANES)
        return carry

    lax.fori_loop(0, rank // GROUP, body, 0)


def send_kernel(level, bit, flip, present, partner, near, wide, shared, out):
    rank, per = partner.shape[0], shared.shape[1] // partner.shape[1]
    places = digits()
    chunk, other = places[3] ^ flip, 1 - places[3 - bit]

    def emit(row, value):
        place = pl.ds(pl.multiple_of(lax.rem(row, per) * 8, 8), 8)
        out[2 * rank + row // per, place, :] = (near[row] + value).astype(jnp.bfloat16)

    multiply(wide.at[other, chunk], state_rows(partner, present[chunk, level, other]), rank, emit)


def sent_rows(shared):
    rank = shared.shape[1] // 2
    per = shared.shape[1] // 8
    return [
        shared[2 * rank + row // per, row % per * 8:(row % per + 1) * 8, :].astype(jnp.float32) for row in range(rank)
    ]


def swap_groups(tile, size):
    lane_group = lax.broadcasted_iota(jnp.int32, tile[0].shape, 2) // size
    step = 1
    while step < len(tile):
        low = (lane_group // step) % 2 == 0
        fresh = list(tile)
        for place in range(len(tile)):
            if place & step == 0:
                first, second = tile[place], tile[place + step]
                fresh[place] = jnp.where(low, first, pltpu.roll(second, step * size, 2))
                fresh[place + step] = jnp.where(low, pltpu.roll(first, LANES - step * size, 2), second)
        tile = fresh
        step *= 2
    return tile


def pair_near_kernel(level, present, wide, shared, state, out, far_wide):
    rank = state.shape[0]
    core = digits()[3]
    rows = state_rows(state)
    mask = present[core, level, core]

    for half in range(2):
        widen_shared(shared, 0, half, far_wide.at[half])
    for box in range(2):

        def emit(row, value):
            out[box, row] = value

        if box == 0:
            multiply(wide.at[core, core], [row * mask for row in rows], rank, emit)
        else:
            multiply(far_wide.at[core], rows, rank, emit)


def pair_far_kernel(level, size, present, wide, far_wide, shared, near, out, total):
    rank = near.shape[1]
    core = digits()[3]
    rows = sent_rows(shared)
    mask = present[core, level, 1 - core]
    fold = LANES // size
    depth = rank // fold
    for box in range(2):

        def emit(row, value):
            total[row] = near[box, row] + value

        if box == 0:
            multiply(wide.at[1 - core, core], [row * mask for row in rows], rank, emit)
        else:
            multiply(far_wide.at[1 - core], rows, rank, emit)
        pieces = swap_groups([total[place * depth:(place + 1) * depth] for place in range(fold)], size)
        for place, piece in enumerate(pieces):
            out[place // 2, core ^ box, place % 2] = piece.astype(jnp.bfloat16)


def widen_kernel(shared, wide):
    for half in range(2):
        widen_shared(shared, 1, half, wide.at[half])


def pair_box(wides, total, states, presents, out):
    for half in range(2):
        present = presents[half]
        rows = [states[half, index].astype(jnp.float32) for index in range(out.shape[0])]
        if present is not None:
            rows = [row * present for row in rows]

        def emit(row, value):
            if half == 0:
                total[row] = value
            else:
                out[row] = (total[row] + value).astype(jnp.bfloat16)

        multiply(wides[half], rows, out.shape[0], emit)


def open_kernel(size, present, wide, moved, *rest):
    out, states, total = rest[-3:]
    core = digits()[3]
    fold = LANES // size
    depth = out.shape[0] // fold
    for last in range(2):
        tile = swap_groups([moved[place // 2, place % 2, last].astype(jnp.float32) for place in range(fold)], size)
        for place, rows in enumerate(tile):
            states[last, place * depth:(place + 1) * depth] = rows.astype(jnp.bfloat16)
    pair_box(
        [wide.at[half, core] for half in range(2)], total, states, [present[core, 0, half] for half in range(2)], out,
    )


def other_kernel(wide, states, out, total):
    pair_box([wide.at[half] for half in range(2)], total, states, (None, None), out)


def interp_kernel(interp, matrix, wide):
    rank = interp.shape[1]
    spread(wide, lambda row: interp[pl.ds(row, 8)].reshape(8 * rank, 2 * LANES), interp.shape[0], matrix[...])


def image_rows(level, bit, flip, present, wide, partner, near, total):
    places = digits()
    chunk, other = places[3] ^ flip, 1 - places[3 - bit]

    def emit(row, value):
        total[row] = (near[row] + value).astype(jnp.bfloat16).astype(jnp.float32)

    multiply(wide.at[other, chunk], state_rows(partner, present[chunk, level, other]), total.shape[0], emit)
    return [total[index] for index in range(total.shape[0])]


def first_image_kernel(level, bit, present, wide, image_wide, partner, near, out, total):
    rows = image_rows(level, bit, 0, present, wide, partner, near, total)

    def emit(row, value):
        out[row] = value.astype(jnp.bfloat16)

    multiply(image_wide.at[digits()[3]], rows, out.shape[0], emit)


def last_kernel(level, bit, present, wide, image_wide, partner, near, ready, back, image, both, held, total, sems):
    core = digits()[3]
    for row in range(ready.shape[0]):
        both[row, :, lanes_of(core)] = ready[row]
    rows = image_rows(level, bit, 1, present, wide, partner, near, total)
    rank, parts = total.shape[0], sems.shape[0]
    size, rhs_count = held.shape[0] // parts, held.shape[1]
    copies = []
    for part in range(parts):

        def emit(row, value):
            both[part * size + row, :, lanes_of(1 - core)] = value.astype(jnp.bfloat16)

        multiply(image_wide.at[1 - core, pl.ds(part * size * rank, size * rank), :], rows, size, emit)
        span = pl.ds(part * size, size)
        natural = reorder(both[span].reshape(size * rhs_count, 2 * LANES), back[...])
        held[span] = natural.astype(jnp.bfloat16).reshape(size, rhs_count, 2 * LANES)
        copies.append(pltpu.make_async_copy(held.at[span], image.at[span], sems.at[part]))
        copies[-1].start()
    for copy in copies:
        copy.wait()


def run(kernel, outs, operands, scratch=(), products=1, in_specs=None, out_specs=None, aliases=None, limit=KERNEL_LIMIT):
    whole = pl.BlockSpec(memory_space=pltpu.VMEM)
    single = not isinstance(outs, list)
    shapes = [outs] if single else outs
    result = pl.pallas_call(
        kernel,
        out_shape=shapes,
        in_specs=in_specs or [whole] * len(operands),
        out_specs=out_specs or [whole] * len(shapes),
        scratch_shapes=list(scratch),
        input_output_aliases=aliases or {},
        compiler_params=pltpu.CompilerParams(vmem_limit_bytes=limit),
        cost_estimate=pl.CostEstimate(flops=products * KERNEL_COST, bytes_accessed=products * KERNEL_COST, transcendentals=0),
    )(*operands)
    return result[0] if single else result


def permuted(value, target_of):
    pairs = [(source, target_of(source)) for source in range(lax.axis_size("leaf"))]
    return lax.ppermute(value, "leaf", pairs)


def swapped(value, bit):
    return permuted(value, lambda source: source ^ 2**bit)


def fast_local(samples, interp_in, top_blocks, top_pattern, bottom_blocks, bottom_pattern, interp_out):
    rank, depth = interp_in.shape[:2]
    rhs_count, box_count = samples.shape[1:]
    out_depth = interp_out.shape[0]
    leaf_count = lax.axis_size("leaf")
    slot = box_count // leaf_count
    size = slot // 2
    fold = LANES // size
    bf16, f32 = jnp.bfloat16, jnp.float32
    state = jax.ShapeDtypeStruct((rank, rhs_count, LANES), bf16)
    partial = jax.ShapeDtypeStruct((rank, rhs_count, LANES), f32)
    level_wide = jax.ShapeDtypeStruct((2, 2, rank * rank, LANES), f32)
    pair_wide = jax.ShapeDtypeStruct((2, rank * rank, LANES), f32)
    order = jax.ShapeDtypeStruct((box_count, box_count), bf16)
    presence = jax.ShapeDtypeStruct((2, 4, 2, 8, LANES), f32)
    total = pltpu.VMEM((rank, rhs_count, LANES), f32)
    whole, anywhere = pl.BlockSpec(memory_space=pltpu.VMEM), pl.BlockSpec(memory_space=pl.ANY)

    def ahead(blocks, level, *after):
        return run(functools.partial(ahead_kernel, level), level_wide, (blocks, matrix, *after), products=4)

    def level_nears(present, level, bit, order, wide, extra=()):
        return {
            flip: run(
                functools.partial(near_kernel, level, bit, flip), partial,
                (present, current[flip], wide) + ((current[1 - flip], *extra) if place < len(order) - 1 else ()),
            )
            for place, flip in enumerate(order)
        }

    def level_fars(present, level, bit, order, wide):
        return {
            flip: run(functools.partial(far_kernel, level, bit, flip), state, (present, partner[flip], near[flip], wide))
            for flip in order
        }

    current = {
        flip: run(
            functools.partial(coeff_kernel, flip, slot), state, (interp_in, samples),
            (
                pltpu.VMEM((rank * depth // 2, LANES), f32), pltpu.VMEM((depth * rhs_count, LANES), f32), total,
            ), 2,
        )
        for flip in (1, 0)
    }
    wide, matrix, back, top_present, bottom_present = run(
        functools.partial(fetch_kernel, slot), [level_wide, order, order, presence, presence],
        (top_blocks, top_pattern, bottom_pattern, current[0]),
        (pltpu.VMEM((1, *top_blocks.shape[1:]), bf16), pltpu.SemaphoreType.DMA), 4,
        in_specs=[anywhere, whole, whole, whole], limit=FETCH_LIMIT,
    )
    for level in range(3):
        bit = 3 - level
        partner = {flip: swapped(current[flip], bit) for flip in (1, 0)}
        if level > 0:
            wide = later[level]
        near = level_nears(top_present, level, bit, (1, 0), wide)
        if level == 0:
            later = {number: ahead(top_blocks, number, near[0]) for number in (1, 2, 3)}
            first_wide = ahead(bottom_blocks, 0, near[0])
        if level < 2:
            current = level_fars(top_present, level, bit, (1, 0), wide)

    share_rows = 2 * rank + rank * rhs_count // (2 * rank)
    shared_shape = jax.ShapeDtypeStruct((share_rows, 2 * rank, LANES), bf16)
    shared = run(
        functools.partial(share_kernel, 3), shared_shape, (later[3], top_present, first_wide, bottom_present),
    )
    shared = run(
        functools.partial(send_kernel, 2, 1, 1), shared_shape, (top_present, partner[1], near[1], wide, shared), aliases={4: 0},
    )
    shared = swapped(shared, 0)
    current = level_fars(top_present, 2, 1, (0,), wide)

    pair_near, far_wide = run(
        functools.partial(pair_near_kernel, 3),
        [jax.ShapeDtypeStruct((2, rank, rhs_count, LANES), f32), pair_wide],
        (top_present, later[3], shared, current[0]), products=2,
    )
    piece = jax.ShapeDtypeStruct((leaf_count // 2, 2, 2, rank // fold, rhs_count, LANES), bf16)
    pieces = run(
        functools.partial(pair_far_kernel, 3, size), piece,
        (top_present, later[3], far_wide, shared, pair_near), (total,), 2,
    )
    groups = [[place * 2 + core for place in range(leaf_count // 2)] for core in range(2)]
    moved = lax.all_to_all(pieces, "leaf", split_axis=0, concat_axis=0, axis_index_groups=groups, tiled=True)
    other_wide = run(widen_kernel, pair_wide, (shared,))
    wides = {level: ahead(bottom_blocks, level, pieces) for level in (1, 2, 3)}
    image_wide = run(interp_kernel, jax.ShapeDtypeStruct((2, out_depth * rank, LANES), f32), (interp_out, matrix))
    first, states = run(
        functools.partial(open_kernel, size), [state, jax.ShapeDtypeStruct((2, rank, rhs_count, LANES), bf16)],
        (bottom_present, first_wide, moved, *wides.values(), image_wide, other_wide), (total,), 2,
    )
    current = {0: first}
    partner = {0: swapped(first, 1)}
    current[1] = swapped(run(other_kernel, state, (other_wide, states), (total,), 2), 0)
    partner[1] = swapped(current[1], 1)
    for level in (1, 2, 3):
        if level > 1:
            partner = {flip: swapped(current[flip], level) for flip in (0, 1)}
        near = level_nears(bottom_present, level, level, (0, 1), wides[level])
        if level < 3:
            current = level_fars(bottom_present, level, level, (0, 1), wides[level])

    ready = run(
        functools.partial(first_image_kernel, 3, 3), jax.ShapeDtypeStruct((out_depth, rhs_count, LANES), bf16),
        (bottom_present, wides[3], image_wide, partner[0], near[0]), (total,), 3,
    )
    held = pltpu.VMEM((out_depth, rhs_count, box_count), bf16)
    return run(
        functools.partial(last_kernel, 3, 3), jax.ShapeDtypeStruct((out_depth, rhs_count, box_count), bf16),
        (bottom_present, wides[3], image_wide, partner[1], near[1], ready, back),
        (held, held, total, pltpu.SemaphoreType.DMA((4,))), 3, out_specs=[anywhere],
    )


def contract(weights, state):
    product = weights[:, :, None].astype(jnp.float32) * state[None].astype(jnp.float32)
    return jnp.sum(product, axis=1)


def plain_level(current, blocks, pattern, bit):
    rank = blocks.shape[0]
    partner = swapped(current, bit)
    is_lower = lax.axis_index("leaf") // 2**bit % 2 == 0
    lower = jnp.where(is_lower, current, partner)
    upper = jnp.where(is_lower, partner, current)
    weights = blocks * jnp.repeat(pattern, rank, axis=0).astype(jnp.bfloat16)[None]
    return contract(weights, jnp.concatenate([lower, upper], axis=0)).astype(jnp.bfloat16)


def plain_local(samples, interp_in, top_blocks, top_pattern, bottom_blocks, bottom_pattern, interp_out):
    bit_count = lax.axis_size("leaf").bit_length() - 1
    current = contract(interp_in, samples).astype(jnp.bfloat16)
    for level in range(top_blocks.shape[0]):
        current = plain_level(current, top_blocks[level], top_pattern[level], bit_count - 1 - level)
    flat = current.reshape(-1, current.shape[2])
    current = lax.all_to_all(flat, "leaf", split_axis=1, concat_axis=1, tiled=True).reshape(current.shape)
    for level in range(bottom_blocks.shape[0]):
        current = plain_level(current, bottom_blocks[level], bottom_pattern[level], level)
    return contract(interp_out, current).astype(jnp.bfloat16)


def local(samples, interp_in, top_blocks, *rest):
    four_digits = lax.axis_size("leaf") == 16 and top_blocks.shape[0] == 4
    chosen = fast_local if four_digits and samples.shape[1:] == (8, 2 * LANES) else plain_local
    return chosen(samples, interp_in, top_blocks, *rest)


def solution(mesh):
    boxes = ("parts", "leaf")
    return jax.shard_map(
        local,
        mesh=mesh,
        in_specs=(
            P(None, None, boxes),
            P(None, None, boxes),
            P(None, None, None, boxes),
            P(None, None, boxes),
            P(None, None, None, boxes),
            P(None, None, boxes),
            P(None, None, boxes),
        ),
        out_specs=P(None, None, boxes),
        check_vma=False,
    )
```

```python
import functools

import jax
import jax.numpy as jnp
from jax import lax
from jax.experimental import pallas as pl
from jax.experimental.pallas import tpu as pltpu
from jax.sharding import PartitionSpec as P

LANES = 128
GROUP = 4
KERNEL_COST = 1024
KERNEL_LIMIT = 16 * 2**20
FETCH_LIMIT = 53_000_000
START_LIMIT = 56_250_000


def digits():
    place = lax.axis_index("leaf")
    return lax.rem(place // 8, 2), lax.rem(place // 4, 2), lax.rem(place // 2, 2), lax.rem(place, 2)


def lanes_of(chunk):
    return pl.ds(pl.multiple_of(chunk * LANES, LANES), LANES)


def rows_of(half, rank):
    return pl.ds(pl.multiple_of(half * rank, rank), rank)


def spread(wide, load, row_count, rank):
    def body(step, carry):
        rows = load(step * GROUP).astype(jnp.float32)
        wide[pl.ds(step * GROUP * rank, GROUP * rank), :] = rows.reshape(GROUP * rank, LANES)
        return carry

    lax.fori_loop(0, row_count // GROUP, body, 0)


def multiply(wide, state, row_count, emit):
    rank = len(state)

    def body(step, carry):
        for inner in range(GROUP):
            sums = [None, None]
            for index in range(rank):
                weight = wide[pl.ds(step * GROUP * rank + inner * rank + index, 8, stride=0), :]
                term = weight * state[index]
                old = sums[index % 2]
                sums[index % 2] = term if old is None else old + term
            emit(step * GROUP + inner, sums[0] + sums[1])
        return carry

    lax.fori_loop(0, row_count // GROUP, body, 0)


def state_rows(ref, present=None):
    rows = [ref[index].astype(jnp.float32) for index in range(ref.shape[0])]
    return rows if present is None else [row * present for row in rows]


def level_load(blocks, level, half, chunk):
    rank = blocks.shape[1]
    return lambda row: blocks[level, pl.ds(row, GROUP), rows_of(half, rank), lanes_of(chunk)]


def present_of(pattern, level, half, chunk):
    pair = [pattern[level, place:place + 1, lanes_of(chunk)].astype(jnp.float32) for place in range(2)]
    return jnp.where(half == 0, pair[0], pair[1])


def coeff_kernel(flip, interp, samples, *rest):
    out, held_interp, held_samples, wide, total, sems = rest[-6:]
    rank, depth = interp.shape[0], interp.shape[1] // 2
    lanes = lanes_of(digits()[3] ^ flip)
    copies = []
    for half in range(2):
        part = pl.ds(half * depth, depth)
        copies.append(pltpu.make_async_copy(interp.at[:, part, lanes], held_interp.at[half], sems.at[half]))
        copies.append(pltpu.make_async_copy(samples.at[part, :, lanes], held_samples.at[half], sems.at[half + 2]))
    for copy in copies:
        copy.start()
    for half in range(2):
        copies[2 * half].wait()
        copies[2 * half + 1].wait()
        spread(wide, lambda row: held_interp[half, pl.ds(row, GROUP)], rank, depth)
        state = [held_samples[half, index].astype(jnp.float32) for index in range(depth)]

        def emit(row, value):
            if half == 0:
                total[row] = value
            else:
                out[row] = (total[row] + value).astype(jnp.bfloat16)

        multiply(wide, state, rank, emit)


def fetch_kernel(level, bit, blocks, after, *rest):
    held, sem = rest[-2:]
    copy = pltpu.make_async_copy(blocks.at[pl.ds(level, 1)], held, sem)
    copy.start()
    copy.wait()
    ahead_kernel(0, bit, held, *rest[:-2])


def ahead_kernel(level, bit, blocks, *rest):
    near_wides, far_wides = rest[-4:-2], rest[-2:]
    rank = blocks.shape[1]
    places = digits()
    own = places[3 - bit]
    for flip in range(2):
        chunk = places[3] ^ flip
        spread(near_wides[flip], level_load(blocks, level, own, chunk), rank, rank)
        spread(far_wides[flip], level_load(blocks, level, 1 - own, chunk), rank, rank)


def near_kernel(level, bit, flip, pattern, state, wide, *rest):
    out = rest[-1]
    places = digits()
    chunk, own = places[3] ^ flip, places[3 - bit]

    def emit(row, value):
        out[row] = value

    multiply(wide, state_rows(state, present_of(pattern, level, own, chunk)), out.shape[0], emit)


def far_kernel(level, bit, flip, pattern, partner, near, wide, *rest):
    out = rest[-1]
    places = digits()
    chunk, other = places[3] ^ flip, 1 - places[3 - bit]

    def emit(row, value):
        out[row] = (near[row] + value).astype(jnp.bfloat16)

    multiply(wide, state_rows(partner, present_of(pattern, level, other, chunk)), out.shape[0], emit)


def share_kernel(top_level, top_blocks, top_pattern, bottom_blocks, bottom_pattern, out):
    rank = top_blocks.shape[1]
    chunk = 1 - digits()[3]
    for place, (blocks, pattern, level) in enumerate(((top_blocks, top_pattern, top_level), (bottom_blocks, bottom_pattern, 0))):
        for half in range(2):
            present = present_of(pattern, level, half, chunk)[None]

            def body(step, carry):
                rows = blocks[level, pl.ds(step * 8, 8), half * rank:(half + 1) * rank, lanes_of(chunk)]
                span = pl.ds(place * rank + step * 8, 8)
                out[span, half * rank:(half + 1) * rank, :] = (rows.astype(jnp.float32) * present).astype(jnp.bfloat16)
                return carry

            lax.fori_loop(0, rank // 8, body, 0)


def shared_load(shared, place, half):
    rank = shared.shape[1] // 2
    return lambda row: shared[pl.ds(place * rank + row, GROUP), rows_of(half, rank), :]


def send_kernel(level, bit, flip, pattern, partner, near, wide, shared, out):
    rank, per = partner.shape[0], shared.shape[1] // partner.shape[1]
    places = digits()
    chunk, other = places[3] ^ flip, 1 - places[3 - bit]

    def emit(row, value):
        place = pl.ds(pl.multiple_of(lax.rem(row, per) * 8, 8), 8)
        out[2 * rank + row // per, place, :] = (near[row] + value).astype(jnp.bfloat16)

    multiply(wide, state_rows(partner, present_of(pattern, level, other, chunk)), rank, emit)


def sent_rows(shared):
    rank = shared.shape[1] // 2
    per = shared.shape[1] // 8
    return [
        shared[2 * rank + row // per, row % per * 8:(row % per + 1) * 8, :].astype(jnp.float32) for row in range(rank)
    ]


def swap_groups(tile, slot):
    lane_group = lax.broadcasted_iota(jnp.int32, tile[0].shape, 2) // slot
    step = 1
    while step < len(tile):
        low = (lane_group // step) % 2 == 0
        fresh = list(tile)
        for place in range(len(tile)):
            if place & step == 0:
                first, second = tile[place], tile[place + step]
                fresh[place] = jnp.where(low, first, pltpu.roll(second, step * slot, 2))
                fresh[place + step] = jnp.where(low, pltpu.roll(first, LANES - step * slot, 2), second)
        tile = fresh
        step *= 2
    return tile


def pair_far_kernel(level, blocks, pattern, shared, out, near_wide, wide):
    rank = blocks.shape[1]
    core = digits()[3]
    rows = sent_rows(shared)
    present = present_of(pattern, level, 1 - core, core)
    for box in range(2):
        for target, half in ((wide, 1 - core), (near_wide.at[box], core)):
            spread(target, level_load(blocks, level, half, core) if box == 0 else shared_load(shared, 0, half), rank, rank)

        def emit(row, value):
            out[box, row] = value

        multiply(wide, [row * present for row in rows] if box == 0 else rows, rank, emit)


def pair_near_kernel(level, slot, pattern, wide, state, far, *rest):
    outs, (total, packed) = rest[:4], rest[4:]
    rank = state.shape[0]
    _, mid, low, core = digits()
    rows = state_rows(state)
    present = present_of(pattern, level, core, core)
    fold = LANES // slot
    for box in range(2):

        def emit(row, value):
            total[row] = far[box, row] + value

        multiply(wide.at[box], [row * present for row in rows] if box == 0 else rows, rank, emit)
        depth = rank // fold
        pieces = swap_groups([total[place * depth:(place + 1) * depth] for place in range(fold)], slot)
        for place, piece in enumerate(pieces):
            packed[core ^ box, place] = piece.astype(jnp.bfloat16)
    for turn, out in enumerate(outs):
        first = ((mid ^ (turn // 2)) * 2 + (low ^ (turn % 2))) * 2
        for box in range(2):
            for last in range(2):
                out[box, last] = packed[box, first + last]


def wide_kernel(blocks, shared, own_wide, other_wide):
    rank = blocks.shape[1]
    core = digits()[3]
    for half in range(2):
        spread(own_wide.at[half], level_load(blocks, 0, half, core), rank, rank)
        spread(other_wide.at[half], shared_load(shared, 1, half), rank, rank)


def pair_box(wide, total, states, presents, out):
    for half in range(2):
        present = presents[half]
        rows = [states[half, index].astype(jnp.float32) for index in range(out.shape[0])]
        if present is not None:
            rows = [row * present for row in rows]

        def emit(row, value):
            if half == 0:
                total[row] = value
            else:
                out[row] = (total[row] + value).astype(jnp.bfloat16)

        multiply(wide.at[half], rows, out.shape[0], emit)


def open_kernel(slot, wide, kept, *rest):
    pieces, (out, states, total, packed) = rest[:4], rest[-4:]
    high, mid, low, core = digits()
    fold = LANES // slot
    depth = out.shape[0] // fold
    for turn, piece in enumerate(pieces):
        first = ((mid ^ (turn // 2)) * 2 + (low ^ (turn % 2))) * 2
        for box in range(2):
            for last in range(2):
                value = piece[box, last]
                if turn == 0:
                    value = jnp.where(high == core, kept[box, last], value)
                packed[last, first + box] = value
    for last in range(2):
        tile = swap_groups([packed[last, place].astype(jnp.float32) for place in range(fold)], slot)
        for place, rows in enumerate(tile):
            states[last, place * depth:(place + 1) * depth] = rows.astype(jnp.bfloat16)
    pair_box(wide, total, states, (None, None), out)


def own_kernel(pattern, wide, states, out, total):
    core = digits()[3]
    pair_box(wide, total, states, [present_of(pattern, 0, half, core) for half in range(2)], out)


def interp_kernel(interp, first_wide, second_wide):
    core = digits()[3]
    for wide, chunk in ((first_wide, core), (second_wide, 1 - core)):
        spread(wide, lambda row: interp[pl.ds(row, GROUP), :, lanes_of(chunk)], interp.shape[0], interp.shape[1])


def image_rows(level, bit, flip, pattern, wide, partner, near, total):
    places = digits()
    chunk, other = places[3] ^ flip, 1 - places[3 - bit]

    def emit(row, value):
        total[row] = (near[row] + value).astype(jnp.bfloat16).astype(jnp.float32)

    multiply(wide, state_rows(partner, present_of(pattern, level, other, chunk)), total.shape[0], emit)
    return [total[index] for index in range(total.shape[0])]


def first_image_kernel(level, bit, pattern, wide, image_wide, partner, near, out, total):
    rows = image_rows(level, bit, 0, pattern, wide, partner, near, total)

    def emit(row, value):
        out[row] = value.astype(jnp.bfloat16)

    multiply(image_wide, rows, out.shape[0], emit)


def last_kernel(level, bit, pattern, wide, image_wide, partner, near, ready, image, held, total, sems):
    core = digits()[3]
    copies = [pltpu.make_async_copy(ready, image.at[:, :, lanes_of(core)], sems.at[0])]
    copies[0].start()
    rows = image_rows(level, bit, 1, pattern, wide, partner, near, total)
    rank, parts = total.shape[0], sems.shape[0] - 1
    size = held.shape[0] // parts
    for part in range(parts):

        def emit(row, value):
            held[part * size + row] = value.astype(jnp.bfloat16)

        multiply(image_wide.at[pl.ds(part * size * rank, size * rank), :], rows, size, emit)
        span = pl.ds(part * size, size)
        copies.append(pltpu.make_async_copy(held.at[span], image.at[span, :, lanes_of(1 - core)], sems.at[part + 1]))
        copies[-1].start()
    for copy in copies:
        copy.wait()


def run(kernel, outs, operands, scratch=(), products=1, in_specs=None, out_specs=None, aliases=None, limit=KERNEL_LIMIT):
    whole = pl.BlockSpec(memory_space=pltpu.VMEM)
    single = not isinstance(outs, list)
    shapes = [outs] if single else outs
    result = pl.pallas_call(
        kernel,
        out_shape=shapes,
        in_specs=in_specs or [whole] * len(operands),
        out_specs=out_specs or [whole] * len(shapes),
        scratch_shapes=list(scratch),
        input_output_aliases=aliases or {},
        compiler_params=pltpu.CompilerParams(vmem_limit_bytes=limit),
        cost_estimate=pl.CostEstimate(flops=products * KERNEL_COST, bytes_accessed=products * KERNEL_COST, transcendentals=0),
    )(*operands)
    return result[0] if single else result


def permuted(value, target_of):
    pairs = [(source, target_of(source)) for source in range(lax.axis_size("leaf"))]
    pairs = [pair for pair in pairs if pair[0] != pair[1]]
    return lax.ppermute(value, "leaf", pairs)


def swapped(value, bit):
    return permuted(value, lambda source: source ^ 2**bit)


def crossed(source, turn):
    high, mid, low, core = source // 8 % 2, source // 4 % 2, source // 2 % 2, source % 2
    return ((core * 2 + (mid ^ (turn // 2))) * 2 + (low ^ (turn % 2))) * 2 + high


def fast_local(samples, interp_in, top_blocks, top_pattern, bottom_blocks, bottom_pattern, interp_out):
    rank, depth = interp_in.shape[:2]
    rhs_count, box_count = samples.shape[1:]
    out_depth = interp_out.shape[0]
    slot = box_count // lax.axis_size("leaf")
    fold = LANES // slot
    state = jax.ShapeDtypeStruct((rank, rhs_count, LANES), jnp.bfloat16)
    partial = jax.ShapeDtypeStruct((rank, rhs_count, LANES), jnp.float32)
    spread_out = jax.ShapeDtypeStruct((rank * rank, LANES), jnp.float32)
    pair_spread = jax.ShapeDtypeStruct((2, rank * rank, LANES), jnp.float32)
    total = pltpu.VMEM((rank, rhs_count, LANES), jnp.float32)
    wide = pltpu.VMEM((rank * rank, LANES), jnp.float32)
    packed = pltpu.VMEM((2, fold, rank // fold, rhs_count, LANES), jnp.bfloat16)

    def level_wides(blocks, level, bit, *after):
        wides = run(functools.partial(ahead_kernel, level, bit), [spread_out] * 4, (blocks, *after), products=4)
        return wides[:2], wides[2:]

    def level_nears(pattern, level, bit, order, wides, extra=()):
        return {
            flip: run(
                functools.partial(near_kernel, level, bit, flip), partial,
                (pattern, current[flip], wides[0][flip]) + ((current[1 - flip], *extra) if place < len(order) - 1 else ()),
            )
            for place, flip in enumerate(order)
        }

    def level_fars(pattern, level, bit, order, wides, extra=()):
        return {
            flip: run(
                functools.partial(far_kernel, level, bit, flip), state,
                (pattern, partner[flip], near[flip], wides[1][flip], *extra),
            )
            for flip in order
        }

    current = {}
    for flip in (1, 0):
        current[flip] = run(
            functools.partial(coeff_kernel, flip), state, (interp_in, samples, *current.values()),
            (
                pltpu.VMEM((2, rank, depth // 2, LANES), jnp.bfloat16),
                pltpu.VMEM((2, depth // 2, rhs_count, LANES), jnp.bfloat16),
                pltpu.VMEM((rank * depth // 2, LANES), jnp.float32), total, pltpu.SemaphoreType.DMA((4,)),
            ), 2, in_specs=[pl.BlockSpec(memory_space=pl.ANY)] * (2 + len(current)), limit=START_LIMIT,
        )
    share_rows = 2 * rank + rank * rhs_count // (2 * rank)
    shared_shape = jax.ShapeDtypeStruct((share_rows, 2 * rank, LANES), jnp.bfloat16)
    for level in range(3):
        bit = 3 - level
        partner = {flip: swapped(current[flip], bit) for flip in (1, 0)}
        if level == 0:
            wides = run(
                functools.partial(fetch_kernel, 0, 3), [spread_out] * 4, (top_blocks, current[0]),
                (pltpu.VMEM((1, *top_blocks.shape[1:]), jnp.bfloat16), pltpu.SemaphoreType.DMA), 4,
                in_specs=[pl.BlockSpec(memory_space=pl.ANY), pl.BlockSpec(memory_space=pltpu.VMEM)], limit=FETCH_LIMIT,
            )
            wides = wides[:2], wides[2:]
        else:
            wides = later_wides[level]
        near = level_nears(top_pattern, level, bit, (1, 0), wides)
        if level == 0:
            later_wides = {later: level_wides(top_blocks, later, 3 - later, near[0]) for later in (1, 2)}
            shared = run(
                functools.partial(share_kernel, 3), shared_shape,
                (top_blocks, top_pattern, bottom_blocks, bottom_pattern),
            )
        if level < 2:
            current = level_fars(top_pattern, level, bit, (1, 0), wides)

    shared = run(
        functools.partial(send_kernel, 2, 1, 1), shared_shape, (top_pattern, partner[1], near[1], wides[1][1], shared), aliases={4: 0},
    )
    shared = swapped(shared, 0)
    pair_far, near_wide = run(
        functools.partial(pair_far_kernel, 3),
        [jax.ShapeDtypeStruct((2, rank, rhs_count, LANES), jnp.float32), pair_spread],
        (top_blocks, top_pattern, shared), (wide,), 2,
    )
    current = level_fars(top_pattern, 2, 1, (0,), wides, (pair_far,))

    piece = jax.ShapeDtypeStruct((2, 2, rank // fold, rhs_count, LANES), jnp.bfloat16)
    pieces = run(
        functools.partial(pair_near_kernel, 3, slot), [piece] * 4,
        (top_pattern, near_wide, current[0], pair_far), (total, packed), 2,
    )
    kept = pieces[0]
    pieces = [permuted(value, functools.partial(crossed, turn=turn)) for turn, value in enumerate(pieces)]
    own_wide, other_wide = run(wide_kernel, [pair_spread] * 2, (bottom_blocks, shared))
    wides = {level: level_wides(bottom_blocks, level, level, kept) for level in (1, 2, 3)}
    image_spread = jax.ShapeDtypeStruct((out_depth * rank, LANES), jnp.float32)
    image_wide = run(interp_kernel, [image_spread] * 2, (interp_out,))
    spreads = [wide for level in (1, 2, 3) for group in wides[level] for wide in group]
    second, states = run(
        functools.partial(open_kernel, slot), [state, jax.ShapeDtypeStruct((2, rank, rhs_count, LANES), jnp.bfloat16)],
        (other_wide, kept, *pieces, *spreads, *image_wide), (total, packed), 2,
    )
    current = {1: swapped(second, 0), 0: run(own_kernel, state, (bottom_pattern, own_wide, states), (total,), 2)}
    partner = {0: swapped(current[0], 1)}
    partner[1] = swapped(current[1], 1)
    for level in (1, 2, 3):
        if level > 1:
            partner = {flip: swapped(current[flip], level) for flip in (0, 1)}
        near = level_nears(bottom_pattern, level, level, (0, 1), wides[level])
        if level < 3:
            current = level_fars(bottom_pattern, level, level, (0, 1), wides[level])

    ready = run(
        functools.partial(first_image_kernel, 3, 3), jax.ShapeDtypeStruct((out_depth, rhs_count, LANES), jnp.bfloat16),
        (bottom_pattern, wides[3][1][0], image_wide[0], partner[0], near[0]), (total,), 3,
    )
    return run(
        functools.partial(last_kernel, 3, 3), jax.ShapeDtypeStruct((out_depth, rhs_count, box_count), jnp.bfloat16),
        (bottom_pattern, wides[3][1][1], image_wide[1], partner[1], near[1], ready),
        (pltpu.VMEM((out_depth, rhs_count, LANES), jnp.bfloat16), total, pltpu.SemaphoreType.DMA((5,))), 3,
        out_specs=[pl.BlockSpec(memory_space=pl.ANY)],
    )


def contract(weights, state):
    product = weights[:, :, None].astype(jnp.float32) * state[None].astype(jnp.float32)
    return jnp.sum(product, axis=1)


def plain_level(current, blocks, pattern, bit):
    rank = blocks.shape[0]
    partner = swapped(current, bit)
    is_lower = lax.axis_index("leaf") // 2**bit % 2 == 0
    lower = jnp.where(is_lower, current, partner)
    upper = jnp.where(is_lower, partner, current)
    weights = blocks * jnp.repeat(pattern, rank, axis=0).astype(jnp.bfloat16)[None]
    return contract(weights, jnp.concatenate([lower, upper], axis=0)).astype(jnp.bfloat16)


def plain_local(samples, interp_in, top_blocks, top_pattern, bottom_blocks, bottom_pattern, interp_out):
    bit_count = lax.axis_size("leaf").bit_length() - 1
    current = contract(interp_in, samples).astype(jnp.bfloat16)
    for level in range(top_blocks.shape[0]):
        current = plain_level(current, top_blocks[level], top_pattern[level], bit_count - 1 - level)
    flat = current.reshape(-1, current.shape[2])
    current = lax.all_to_all(flat, "leaf", split_axis=1, concat_axis=1, tiled=True).reshape(current.shape)
    for level in range(bottom_blocks.shape[0]):
        current = plain_level(current, bottom_blocks[level], bottom_pattern[level], level)
    return contract(interp_out, current).astype(jnp.bfloat16)


def local(samples, interp_in, top_blocks, *rest):
    four_digits = lax.axis_size("leaf") == 16 and top_blocks.shape[0] == 4
    chosen = fast_local if four_digits and samples.shape[1:] == (8, 2 * LANES) else plain_local
    return chosen(samples, interp_in, top_blocks, *rest)


def solution(mesh):
    boxes = ("parts", "leaf")
    return jax.shard_map(
        local,
        mesh=mesh,
        in_specs=(
            P(None, None, boxes),
            P(None, None, boxes),
            P(None, None, None, boxes),
            P(None, None, boxes),
            P(None, None, None, boxes),
            P(None, None, boxes),
            P(None, None, boxes),
        ),
        out_specs=P(None, None, boxes),
        check_vma=False,
    )
```

```python
import functools

import jax
import jax.numpy as jnp
from jax import lax
from jax.experimental import pallas as pl
from jax.experimental.pallas import tpu as pltpu
from jax.sharding import PartitionSpec as P

LANES = 128
GROUP = 4
KERNEL_COST = 1024
KERNEL_LIMIT = 16 * 2**20
FETCH_LIMIT = 53_000_000
START_LIMIT = 56_250_000


def digits():
    place = lax.axis_index("leaf")
    return lax.rem(place // 8, 2), lax.rem(place // 4, 2), lax.rem(place // 2, 2), lax.rem(place, 2)


def lanes_of(chunk):
    return pl.ds(pl.multiple_of(chunk * LANES, LANES), LANES)


def rows_of(half, rank):
    return pl.ds(pl.multiple_of(half * rank, rank), rank)


def spread(wide, load, row_count, rank):
    def body(step, carry):
        rows = load(step * GROUP).astype(jnp.float32)
        wide[pl.ds(step * GROUP * rank, GROUP * rank), :] = rows.reshape(GROUP * rank, LANES)
        return carry

    lax.fori_loop(0, row_count // GROUP, body, 0)


def multiply(wide, state, row_count, emit):
    rank = len(state)

    def body(step, carry):
        for inner in range(GROUP):
            sums = [None, None]
            for index in range(rank):
                weight = wide[pl.ds(step * GROUP * rank + inner * rank + index, 8, stride=0), :]
                term = weight * state[index]
                old = sums[index % 2]
                sums[index % 2] = term if old is None else old + term
            emit(step * GROUP + inner, sums[0] + sums[1])
        return carry

    lax.fori_loop(0, row_count // GROUP, body, 0)


def state_rows(ref, present=None):
    rows = [ref[index].astype(jnp.float32) for index in range(ref.shape[0])]
    return rows if present is None else [row * present for row in rows]


def level_load(blocks, level, half, chunk):
    rank = blocks.shape[1]
    return lambda row: blocks[level, pl.ds(row, GROUP), rows_of(half, rank), lanes_of(chunk)]


def present_of(pattern, level, half, chunk):
    pair = [pattern[level, place:place + 1, lanes_of(chunk)].astype(jnp.float32) for place in range(2)]
    return jnp.where(half == 0, pair[0], pair[1])


def coeff_kernel(flip, interp, samples, *rest):
    out, held_interp, held_samples, wide, total, sems = rest[-6:]
    rank, depth = interp.shape[0], interp.shape[1] // 2
    lanes = lanes_of(digits()[3] ^ flip)
    copies = []
    for half in range(2):
        part = pl.ds(half * depth, depth)
        copies.append(pltpu.make_async_copy(interp.at[:, part, lanes], held_interp.at[half], sems.at[half]))
        copies.append(pltpu.make_async_copy(samples.at[part, :, lanes], held_samples.at[half], sems.at[half + 2]))
    for copy in copies:
        copy.start()
    for half in range(2):
        copies[2 * half].wait()
        copies[2 * half + 1].wait()
        spread(wide, lambda row: held_interp[half, pl.ds(row, GROUP)], rank, depth)
        state = [held_samples[half, index].astype(jnp.float32) for index in range(depth)]

        def emit(row, value):
            if half == 0:
                total[row] = value
            else:
                out[row] = (total[row] + value).astype(jnp.bfloat16)

        multiply(wide, state, rank, emit)


def fetch_kernel(level, bit, blocks, after, *rest):
    held, sem = rest[-2:]
    copy = pltpu.make_async_copy(blocks.at[pl.ds(level, 1)], held, sem)
    copy.start()
    copy.wait()
    ahead_kernel(0, bit, held, *rest[:-2])


def ahead_kernel(level, bit, blocks, *rest):
    near_wides, far_wides = rest[-4:-2], rest[-2:]
    rank = blocks.shape[1]
    places = digits()
    own = places[3 - bit]
    for flip in range(2):
        chunk = places[3] ^ flip
        spread(near_wides[flip], level_load(blocks, level, own, chunk), rank, rank)
        spread(far_wides[flip], level_load(blocks, level, 1 - own, chunk), rank, rank)


def near_kernel(level, bit, flip, pattern, state, wide, *rest):
    out = rest[-1]
    places = digits()
    chunk, own = places[3] ^ flip, places[3 - bit]

    def emit(row, value):
        out[row] = value

    multiply(wide, state_rows(state, present_of(pattern, level, own, chunk)), out.shape[0], emit)


def far_kernel(level, bit, flip, pattern, partner, near, wide, *rest):
    out = rest[-1]
    places = digits()
    chunk, other = places[3] ^ flip, 1 - places[3 - bit]

    def emit(row, value):
        out[row] = (near[row] + value).astype(jnp.bfloat16)

    multiply(wide, state_rows(partner, present_of(pattern, level, other, chunk)), out.shape[0], emit)


def share_kernel(top_level, top_blocks, top_pattern, bottom_blocks, bottom_pattern, out):
    rank = top_blocks.shape[1]
    chunk = 1 - digits()[3]
    for place, (blocks, pattern, level) in enumerate(((top_blocks, top_pattern, top_level), (bottom_blocks, bottom_pattern, 0))):
        for half in range(2):
            present = present_of(pattern, level, half, chunk)[None]

            def body(step, carry):
                rows = blocks[level, pl.ds(step * 8, 8), half * rank:(half + 1) * rank, lanes_of(chunk)]
                span = pl.ds(place * rank + step * 8, 8)
                out[span, half * rank:(half + 1) * rank, :] = (rows.astype(jnp.float32) * present).astype(jnp.bfloat16)
                return carry

            lax.fori_loop(0, rank // 8, body, 0)


def shared_load(shared, place, half):
    rank = shared.shape[1] // 2
    return lambda row: shared[pl.ds(place * rank + row, GROUP), rows_of(half, rank), :]


def send_kernel(level, bit, flip, pattern, partner, near, wide, shared, *rest):
    out = rest[-1]
    rank, per = partner.shape[0], shared.shape[1] // partner.shape[1]
    places = digits()
    chunk, other = places[3] ^ flip, 1 - places[3 - bit]

    def emit(row, value):
        place = pl.ds(pl.multiple_of(lax.rem(row, per) * 8, 8), 8)
        out[2 * rank + row // per, place, :] = (near[row] + value).astype(jnp.bfloat16)

    multiply(wide, state_rows(partner, present_of(pattern, level, other, chunk)), rank, emit)


def sent_rows(shared):
    rank = shared.shape[1] // 2
    per = shared.shape[1] // 8
    return [
        shared[2 * rank + row // per, row % per * 8:(row % per + 1) * 8, :].astype(jnp.float32) for row in range(rank)
    ]


def swap_groups(tile, slot):
    lane_group = lax.broadcasted_iota(jnp.int32, tile[0].shape, 2) // slot
    step = 1
    while step < len(tile):
        low = (lane_group // step) % 2 == 0
        fresh = list(tile)
        for place in range(len(tile)):
            if place & step == 0:
                first, second = tile[place], tile[place + step]
                fresh[place] = jnp.where(low, first, pltpu.roll(second, step * slot, 2))
                fresh[place + step] = jnp.where(low, pltpu.roll(first, LANES - step * slot, 2), second)
        tile = fresh
        step *= 2
    return tile


def pair_far_kernel(level, blocks, pattern, shared, out, near_wide, wide):
    rank = blocks.shape[1]
    core = digits()[3]
    rows = sent_rows(shared)
    present = present_of(pattern, level, 1 - core, core)
    for box in range(2):
        for target, half in ((wide, 1 - core), (near_wide.at[box], core)):
            spread(target, level_load(blocks, level, half, core) if box == 0 else shared_load(shared, 0, half), rank, rank)

        def emit(row, value):
            out[box, row] = value

        multiply(wide, [row * present for row in rows] if box == 0 else rows, rank, emit)


def pair_near_kernel(level, slot, pattern, wide, state, far, *rest):
    outs, (total, packed) = rest[:4], rest[4:]
    rank = state.shape[0]
    _, mid, low, core = digits()
    rows = state_rows(state)
    present = present_of(pattern, level, core, core)
    fold = LANES // slot
    for box in range(2):

        def emit(row, value):
            total[row] = far[box, row] + value

        multiply(wide.at[box], [row * present for row in rows] if box == 0 else rows, rank, emit)
        depth = rank // fold
        pieces = swap_groups([total[place * depth:(place + 1) * depth] for place in range(fold)], slot)
        for place, piece in enumerate(pieces):
            packed[core ^ box, place] = piece.astype(jnp.bfloat16)
    for turn, out in enumerate(outs):
        first = ((mid ^ (turn // 2)) * 2 + (low ^ (turn % 2))) * 2
        for box in range(2):
            for last in range(2):
                out[box, last] = packed[box, first + last]


def wide_kernel(blocks, shared, own_wide, other_wide):
    rank = blocks.shape[1]
    core = digits()[3]
    for half in range(2):
        spread(own_wide.at[half], level_load(blocks, 0, half, core), rank, rank)
        spread(other_wide.at[half], shared_load(shared, 1, half), rank, rank)


def pair_box(wide, total, states, presents, out):
    for half in range(2):
        present = presents[half]
        rows = [states[half, index].astype(jnp.float32) for index in range(out.shape[0])]
        if present is not None:
            rows = [row * present for row in rows]

        def emit(row, value):
            if half == 0:
                total[row] = value
            else:
                out[row] = (total[row] + value).astype(jnp.bfloat16)

        multiply(wide.at[half], rows, out.shape[0], emit)


def open_kernel(slot, wide, kept, *rest):
    pieces, (out, states, total, packed) = rest[:4], rest[-4:]
    high, mid, low, core = digits()
    fold = LANES // slot
    depth = out.shape[0] // fold
    for turn, piece in enumerate(pieces):
        first = ((mid ^ (turn // 2)) * 2 + (low ^ (turn % 2))) * 2
        for box in range(2):
            for last in range(2):
                value = piece[box, last]
                if turn == 0:
                    value = jnp.where(high == core, kept[box, last], value)
                packed[last, first + box] = value
    for last in range(2):
        tile = swap_groups([packed[last, place].astype(jnp.float32) for place in range(fold)], slot)
        for place, rows in enumerate(tile):
            states[last, place * depth:(place + 1) * depth] = rows.astype(jnp.bfloat16)
    pair_box(wide, total, states, (None, None), out)


def own_kernel(pattern, wide, states, out, total):
    core = digits()[3]
    pair_box(wide, total, states, [present_of(pattern, 0, half, core) for half in range(2)], out)


def interp_kernel(interp, first_wide, second_wide):
    core = digits()[3]
    for wide, chunk in ((first_wide, core), (second_wide, 1 - core)):
        spread(wide, lambda row: interp[pl.ds(row, GROUP), :, lanes_of(chunk)], interp.shape[0], interp.shape[1])


def image_rows(level, bit, flip, pattern, wide, partner, near, total):
    places = digits()
    chunk, other = places[3] ^ flip, 1 - places[3 - bit]

    def emit(row, value):
        total[row] = (near[row] + value).astype(jnp.bfloat16).astype(jnp.float32)

    multiply(wide, state_rows(partner, present_of(pattern, level, other, chunk)), total.shape[0], emit)
    return [total[index] for index in range(total.shape[0])]


def first_image_kernel(level, bit, pattern, wide, image_wide, partner, near, out, total):
    rows = image_rows(level, bit, 0, pattern, wide, partner, near, total)

    def emit(row, value):
        out[row] = value.astype(jnp.bfloat16)

    multiply(image_wide, rows, out.shape[0], emit)


def last_kernel(level, bit, pattern, wide, image_wide, partner, near, ready, image, held, total, sems):
    core = digits()[3]
    copies = [pltpu.make_async_copy(ready, image.at[:, :, lanes_of(core)], sems.at[0])]
    copies[0].start()
    rows = image_rows(level, bit, 1, pattern, wide, partner, near, total)
    rank, parts = total.shape[0], sems.shape[0] - 1
    size = held.shape[0] // parts
    for part in range(parts):

        def emit(row, value):
            held[part * size + row] = value.astype(jnp.bfloat16)

        multiply(image_wide.at[pl.ds(part * size * rank, size * rank), :], rows, size, emit)
        span = pl.ds(part * size, size)
        copies.append(pltpu.make_async_copy(held.at[span], image.at[span, :, lanes_of(1 - core)], sems.at[part + 1]))
        copies[-1].start()
    for copy in copies:
        copy.wait()


def run(kernel, outs, operands, scratch=(), products=1, in_specs=None, out_specs=None, aliases=None, limit=KERNEL_LIMIT):
    whole = pl.BlockSpec(memory_space=pltpu.VMEM)
    single = not isinstance(outs, list)
    shapes = [outs] if single else outs
    result = pl.pallas_call(
        kernel,
        out_shape=shapes,
        in_specs=in_specs or [whole] * len(operands),
        out_specs=out_specs or [whole] * len(shapes),
        scratch_shapes=list(scratch),
        input_output_aliases=aliases or {},
        compiler_params=pltpu.CompilerParams(vmem_limit_bytes=limit),
        cost_estimate=pl.CostEstimate(flops=products * KERNEL_COST, bytes_accessed=products * KERNEL_COST, transcendentals=0),
    )(*operands)
    return result[0] if single else result


def permuted(value, target_of):
    pairs = [(source, target_of(source)) for source in range(lax.axis_size("leaf"))]
    pairs = [pair for pair in pairs if pair[0] != pair[1]]
    return lax.ppermute(value, "leaf", pairs)


def swapped(value, bit):
    return permuted(value, lambda source: source ^ 2**bit)


def crossed(source, turn):
    high, mid, low, core = source // 8 % 2, source // 4 % 2, source // 2 % 2, source % 2
    return ((core * 2 + (mid ^ (turn // 2))) * 2 + (low ^ (turn % 2))) * 2 + high


def fast_local(samples, interp_in, top_blocks, top_pattern, bottom_blocks, bottom_pattern, interp_out):
    rank, depth = interp_in.shape[:2]
    rhs_count, box_count = samples.shape[1:]
    out_depth = interp_out.shape[0]
    slot = box_count // lax.axis_size("leaf")
    fold = LANES // slot
    state = jax.ShapeDtypeStruct((rank, rhs_count, LANES), jnp.bfloat16)
    partial = jax.ShapeDtypeStruct((rank, rhs_count, LANES), jnp.float32)
    spread_out = jax.ShapeDtypeStruct((rank * rank, LANES), jnp.float32)
    pair_spread = jax.ShapeDtypeStruct((2, rank * rank, LANES), jnp.float32)
    total = pltpu.VMEM((rank, rhs_count, LANES), jnp.float32)
    wide = pltpu.VMEM((rank * rank, LANES), jnp.float32)
    packed = pltpu.VMEM((2, fold, rank // fold, rhs_count, LANES), jnp.bfloat16)

    def level_wides(blocks, level, bit, *after):
        wides = run(functools.partial(ahead_kernel, level, bit), [spread_out] * 4, (blocks, *after), products=4)
        return wides[:2], wides[2:]

    def level_nears(pattern, level, bit, order, wides, extra=()):
        return {
            flip: run(
                functools.partial(near_kernel, level, bit, flip), partial,
                (pattern, current[flip], wides[0][flip]) + ((current[1 - flip], *extra) if place < len(order) - 1 else ()),
            )
            for place, flip in enumerate(order)
        }

    def level_fars(pattern, level, bit, order, wides, extra=()):
        return {
            flip: run(
                functools.partial(far_kernel, level, bit, flip), state,
                (pattern, partner[flip], near[flip], wides[1][flip], *extra),
            )
            for flip in order
        }

    def coefficients(flip, *after):
        return run(
            functools.partial(coeff_kernel, flip), state, (interp_in, samples, *after),
            (
                pltpu.VMEM((2, rank, depth // 2, LANES), jnp.bfloat16),
                pltpu.VMEM((2, depth // 2, rhs_count, LANES), jnp.bfloat16),
                pltpu.VMEM((rank * depth // 2, LANES), jnp.float32), total, pltpu.SemaphoreType.DMA((4,)),
            ), 2, in_specs=[pl.BlockSpec(memory_space=pl.ANY)] * (2 + len(after)), limit=START_LIMIT,
        )

    share_rows = 2 * rank + rank * rhs_count // (2 * rank)
    shared_shape = jax.ShapeDtypeStruct((share_rows, 2 * rank, LANES), jnp.bfloat16)
    current = {1: coefficients(1)}
    for level in range(3):
        bit = 3 - level
        if level == 0:
            partner = {1: swapped(current[1], bit)}
            wides = run(
                functools.partial(fetch_kernel, 0, 3), [spread_out] * 4, (top_blocks, current[1]),
                (pltpu.VMEM((1, *top_blocks.shape[1:]), jnp.bfloat16), pltpu.SemaphoreType.DMA), 4,
                in_specs=[pl.BlockSpec(memory_space=pl.ANY), pl.BlockSpec(memory_space=pltpu.VMEM)], limit=FETCH_LIMIT,
            )
            wides = wides[:2], wides[2:]
            near = level_nears(top_pattern, level, bit, (1,), wides)
            current[0] = coefficients(0, near[1])
            partner[0] = swapped(current[0], bit)
            near.update(level_nears(top_pattern, level, bit, (0,), wides))
            later_wides = {later: level_wides(top_blocks, later, 3 - later, near[0]) for later in (1, 2)}
            shared = run(
                functools.partial(share_kernel, 3), shared_shape,
                (top_blocks, top_pattern, bottom_blocks, bottom_pattern),
            )
        else:
            partner = {flip: swapped(current[flip], bit) for flip in (1, 0)}
            wides = later_wides[level]
            near = level_nears(top_pattern, level, bit, (1, 0), wides)
        if level < 2:
            current = level_fars(top_pattern, level, bit, (1, 0), wides)

    shared = run(
        functools.partial(send_kernel, 2, 1, 1), shared_shape, (top_pattern, partner[1], near[1], wides[1][1], shared), aliases={4: 0},
    )
    shared = swapped(shared, 0)
    pair_far, near_wide = run(
        functools.partial(pair_far_kernel, 3),
        [jax.ShapeDtypeStruct((2, rank, rhs_count, LANES), jnp.float32), pair_spread],
        (top_blocks, top_pattern, shared), (wide,), 2,
    )
    current = level_fars(top_pattern, 2, 1, (0,), wides, (pair_far,))

    piece = jax.ShapeDtypeStruct((2, 2, rank // fold, rhs_count, LANES), jnp.bfloat16)
    pieces = run(
        functools.partial(pair_near_kernel, 3, slot), [piece] * 4,
        (top_pattern, near_wide, current[0], pair_far), (total, packed), 2,
    )
    kept = pieces[0]
    pieces = [permuted(value, functools.partial(crossed, turn=turn)) for turn, value in enumerate(pieces)]
    own_wide, other_wide = run(wide_kernel, [pair_spread] * 2, (bottom_blocks, shared))
    wides = {level: level_wides(bottom_blocks, level, level, kept) for level in (1, 2, 3)}
    image_spread = jax.ShapeDtypeStruct((out_depth * rank, LANES), jnp.float32)
    image_wide = run(interp_kernel, [image_spread] * 2, (interp_out,))
    spreads = [wide for level in (1, 2, 3) for group in wides[level] for wide in group]
    second, states = run(
        functools.partial(open_kernel, slot), [state, jax.ShapeDtypeStruct((2, rank, rhs_count, LANES), jnp.bfloat16)],
        (other_wide, kept, *pieces, *spreads, *image_wide), (total, packed), 2,
    )
    current = {1: swapped(second, 0), 0: run(own_kernel, state, (bottom_pattern, own_wide, states), (total,), 2)}
    partner = {0: swapped(current[0], 1)}
    partner[1] = swapped(current[1], 1)
    for level in (1, 2, 3):
        if level > 1:
            partner = {flip: swapped(current[flip], level) for flip in (0, 1)}
        near = level_nears(bottom_pattern, level, level, (0, 1), wides[level])
        if level < 3:
            current = level_fars(bottom_pattern, level, level, (0, 1), wides[level])

    ready = run(
        functools.partial(first_image_kernel, 3, 3), jax.ShapeDtypeStruct((out_depth, rhs_count, LANES), jnp.bfloat16),
        (bottom_pattern, wides[3][1][0], image_wide[0], partner[0], near[0]), (total,), 3,
    )
    return run(
        functools.partial(last_kernel, 3, 3), jax.ShapeDtypeStruct((out_depth, rhs_count, box_count), jnp.bfloat16),
        (bottom_pattern, wides[3][1][1], image_wide[1], partner[1], near[1], ready),
        (pltpu.VMEM((out_depth, rhs_count, LANES), jnp.bfloat16), total, pltpu.SemaphoreType.DMA((5,))), 3,
        out_specs=[pl.BlockSpec(memory_space=pl.ANY)],
    )


def contract(weights, state):
    product = weights[:, :, None].astype(jnp.float32) * state[None].astype(jnp.float32)
    return jnp.sum(product, axis=1)


def plain_level(current, blocks, pattern, bit):
    rank = blocks.shape[0]
    partner = swapped(current, bit)
    is_lower = lax.axis_index("leaf") // 2**bit % 2 == 0
    lower = jnp.where(is_lower, current, partner)
    upper = jnp.where(is_lower, partner, current)
    weights = blocks * jnp.repeat(pattern, rank, axis=0).astype(jnp.bfloat16)[None]
    return contract(weights, jnp.concatenate([lower, upper], axis=0)).astype(jnp.bfloat16)


def plain_local(samples, interp_in, top_blocks, top_pattern, bottom_blocks, bottom_pattern, interp_out):
    bit_count = lax.axis_size("leaf").bit_length() - 1
    current = contract(interp_in, samples).astype(jnp.bfloat16)
    for level in range(top_blocks.shape[0]):
        current = plain_level(current, top_blocks[level], top_pattern[level], bit_count - 1 - level)
    flat = current.reshape(-1, current.shape[2])
    current = lax.all_to_all(flat, "leaf", split_axis=1, concat_axis=1, tiled=True).reshape(current.shape)
    for level in range(bottom_blocks.shape[0]):
        current = plain_level(current, bottom_blocks[level], bottom_pattern[level], level)
    return contract(interp_out, current).astype(jnp.bfloat16)


def local(samples, interp_in, top_blocks, *rest):
    four_digits = lax.axis_size("leaf") == 16 and top_blocks.shape[0] == 4
    chosen = fast_local if four_digits and samples.shape[1:] == (8, 2 * LANES) else plain_local
    return chosen(samples, interp_in, top_blocks, *rest)


def solution(mesh):
    boxes = ("parts", "leaf")
    return jax.shard_map(
        local,
        mesh=mesh,
        in_specs=(
            P(None, None, boxes),
            P(None, None, boxes),
            P(None, None, None, boxes),
            P(None, None, boxes),
            P(None, None, None, boxes),
            P(None, None, boxes),
            P(None, None, boxes),
        ),
        out_specs=P(None, None, boxes),
        check_vma=False,
    )
```

```python
import functools

import jax
import jax.numpy as jnp
from jax import lax
from jax.experimental import pallas as pl
from jax.experimental.pallas import tpu as pltpu
from jax.sharding import PartitionSpec as P

LANES = 128
GROUP = 4
KERNEL_COST = 1024
KERNEL_LIMIT = 16 * 2**20
FETCH_LIMIT = 53_850_000
START_LIMIT = 56_250_000


def digits():
    place = lax.axis_index("leaf")
    return lax.rem(place // 8, 2), lax.rem(place // 4, 2), lax.rem(place // 2, 2), lax.rem(place, 2)


def lanes_of(chunk):
    return pl.ds(pl.multiple_of(chunk * LANES, LANES), LANES)


def rows_of(half, rank):
    return pl.ds(pl.multiple_of(half * rank, rank), rank)


def spread(wide, load, row_count, rank):
    def body(step, carry):
        rows = load(step * GROUP).astype(jnp.float32)
        wide[pl.ds(step * GROUP * rank, GROUP * rank), :] = rows.reshape(GROUP * rank, LANES)
        return carry

    lax.fori_loop(0, row_count // GROUP, body, 0)


def multiply(wide, state, row_count, emit):
    rank = len(state)

    def body(step, carry):
        for inner in range(GROUP):
            sums = [None, None]
            for index in range(rank):
                weight = wide[pl.ds(step * GROUP * rank + inner * rank + index, 8, stride=0), :]
                term = weight * state[index]
                old = sums[index % 2]
                sums[index % 2] = term if old is None else old + term
            emit(step * GROUP + inner, sums[0] + sums[1])
        return carry

    lax.fori_loop(0, row_count // GROUP, body, 0)


def state_rows(ref, present=None):
    rows = [ref[index].astype(jnp.float32) for index in range(ref.shape[0])]
    return rows if present is None else [row * present for row in rows]


def level_load(blocks, level, half, chunk):
    rank = blocks.shape[1]
    return lambda row: blocks[level, pl.ds(row, GROUP), rows_of(half, rank), lanes_of(chunk)]


def present_of(pattern, level, half, chunk):
    pair = [pattern[level, place:place + 1, lanes_of(chunk)].astype(jnp.float32) for place in range(2)]
    return jnp.where(half == 0, pair[0], pair[1])


def coeff_kernel(flip, interp, samples, *rest):
    out, held_interp, held_samples, wide, total, sems = rest[-6:]
    rank, depth = interp.shape[0], interp.shape[1] // 2
    lanes = lanes_of(digits()[3] ^ flip)
    copies = []
    for half in range(2):
        part = pl.ds(half * depth, depth)
        copies.append(pltpu.make_async_copy(interp.at[:, part, lanes], held_interp.at[half], sems.at[half]))
        copies.append(pltpu.make_async_copy(samples.at[part, :, lanes], held_samples.at[half], sems.at[half + 2]))
    for copy in copies:
        copy.start()
    for half in range(2):
        copies[2 * half].wait()
        copies[2 * half + 1].wait()
        spread(wide, lambda row: held_interp[half, pl.ds(row, GROUP)], rank, depth)
        state = [held_samples[half, index].astype(jnp.float32) for index in range(depth)]

        def emit(row, value):
            if half == 0:
                total[row] = value
            else:
                out[row] = (total[row] + value).astype(jnp.bfloat16)

        multiply(wide, state, rank, emit)


def second_kernel(level, bit, flip, blocks, interp, samples, after, *rest):
    held, sem = rest[-2:]
    copy = pltpu.make_async_copy(blocks.at[pl.ds(level, 1)], held, sem)
    copy.start()
    coeff_kernel(flip, interp, samples, rest[0], *rest[5:-2])
    copy.wait()
    ahead_kernel(0, bit, held, *rest[1:5])


def ahead_kernel(level, bit, blocks, *rest):
    near_wides, far_wides = rest[-4:-2], rest[-2:]
    rank = blocks.shape[1]
    places = digits()
    own = places[3 - bit]
    for flip in range(2):
        chunk = places[3] ^ flip
        spread(near_wides[flip], level_load(blocks, level, own, chunk), rank, rank)
        spread(far_wides[flip], level_load(blocks, level, 1 - own, chunk), rank, rank)


def near_kernel(level, bit, flip, pattern, state, wide, *rest):
    out = rest[-1]
    places = digits()
    chunk, own = places[3] ^ flip, places[3 - bit]

    def emit(row, value):
        out[row] = value

    multiply(wide, state_rows(state, present_of(pattern, level, own, chunk)), out.shape[0], emit)


def far_kernel(level, bit, flip, pattern, partner, near, wide, *rest):
    out = rest[-1]
    places = digits()
    chunk, other = places[3] ^ flip, 1 - places[3 - bit]

    def emit(row, value):
        out[row] = (near[row] + value).astype(jnp.bfloat16)

    multiply(wide, state_rows(partner, present_of(pattern, level, other, chunk)), out.shape[0], emit)


def share_kernel(top_level, top_blocks, top_pattern, bottom_blocks, bottom_pattern, out):
    rank = top_blocks.shape[1]
    chunk = 1 - digits()[3]
    for place, (blocks, pattern, level) in enumerate(((top_blocks, top_pattern, top_level), (bottom_blocks, bottom_pattern, 0))):
        for half in range(2):
            present = present_of(pattern, level, half, chunk)[None]

            def body(step, carry):
                rows = blocks[level, pl.ds(step * 8, 8), half * rank:(half + 1) * rank, lanes_of(chunk)]
                span = pl.ds(place * rank + step * 8, 8)
                out[span, half * rank:(half + 1) * rank, :] = (rows.astype(jnp.float32) * present).astype(jnp.bfloat16)
                return carry

            lax.fori_loop(0, rank // 8, body, 0)


def shared_load(shared, place, half):
    rank = shared.shape[1] // 2
    return lambda row: shared[pl.ds(place * rank + row, GROUP), rows_of(half, rank), :]


def send_kernel(level, bit, flip, pattern, partner, near, wide, shared, *rest):
    out = rest[-1]
    rank, per = partner.shape[0], shared.shape[1] // partner.shape[1]
    places = digits()
    chunk, other = places[3] ^ flip, 1 - places[3 - bit]

    def emit(row, value):
        place = pl.ds(pl.multiple_of(lax.rem(row, per) * 8, 8), 8)
        out[2 * rank + row // per, place, :] = (near[row] + value).astype(jnp.bfloat16)

    multiply(wide, state_rows(partner, present_of(pattern, level, other, chunk)), rank, emit)


def sent_rows(shared):
    rank = shared.shape[1] // 2
    per = shared.shape[1] // 8
    return [
        shared[2 * rank + row // per, row % per * 8:(row % per + 1) * 8, :].astype(jnp.float32) for row in range(rank)
    ]


def swap_groups(tile, slot):
    lane_group = lax.broadcasted_iota(jnp.int32, tile[0].shape, 2) // slot
    step = 1
    while step < len(tile):
        low = (lane_group // step) % 2 == 0
        fresh = list(tile)
        for place in range(len(tile)):
            if place & step == 0:
                first, second = tile[place], tile[place + step]
                fresh[place] = jnp.where(low, first, pltpu.roll(second, step * slot, 2))
                fresh[place + step] = jnp.where(low, pltpu.roll(first, LANES - step * slot, 2), second)
        tile = fresh
        step *= 2
    return tile


def pair_far_kernel(level, blocks, pattern, shared, out, near_wide, wide):
    rank = blocks.shape[1]
    core = digits()[3]
    rows = sent_rows(shared)
    present = present_of(pattern, level, 1 - core, core)
    for box in range(2):
        for target, half in ((wide, 1 - core), (near_wide.at[box], core)):
            spread(target, level_load(blocks, level, half, core) if box == 0 else shared_load(shared, 0, half), rank, rank)

        def emit(row, value):
            out[box, row] = value

        multiply(wide, [row * present for row in rows] if box == 0 else rows, rank, emit)


def pair_near_kernel(level, slot, pattern, wide, state, far, *rest):
    outs, (total, packed) = rest[:4], rest[4:]
    rank = state.shape[0]
    _, mid, low, core = digits()
    rows = state_rows(state)
    present = present_of(pattern, level, core, core)
    fold = LANES // slot
    for box in range(2):

        def emit(row, value):
            total[row] = far[box, row] + value

        multiply(wide.at[box], [row * present for row in rows] if box == 0 else rows, rank, emit)
        depth = rank // fold
        pieces = swap_groups([total[place * depth:(place + 1) * depth] for place in range(fold)], slot)
        for place, piece in enumerate(pieces):
            packed[core ^ box, place] = piece.astype(jnp.bfloat16)
    for turn, out in enumerate(outs):
        first = ((mid ^ (turn // 2)) * 2 + (low ^ (turn % 2))) * 2
        for box in range(2):
            for last in range(2):
                out[box, last] = packed[box, first + last]


def wide_kernel(blocks, shared, own_wide, other_wide):
    rank = blocks.shape[1]
    core = digits()[3]
    for half in range(2):
        spread(own_wide.at[half], level_load(blocks, 0, half, core), rank, rank)
        spread(other_wide.at[half], shared_load(shared, 1, half), rank, rank)


def pair_box(wide, total, states, presents, out):
    for half in range(2):
        present = presents[half]
        rows = [states[half, index].astype(jnp.float32) for index in range(out.shape[0])]
        if present is not None:
            rows = [row * present for row in rows]

        def emit(row, value):
            if half == 0:
                total[row] = value
            else:
                out[row] = (total[row] + value).astype(jnp.bfloat16)

        multiply(wide.at[half], rows, out.shape[0], emit)


def open_kernel(slot, wide, kept, *rest):
    pieces, (out, states, total, packed) = rest[:4], rest[-4:]
    high, mid, low, core = digits()
    fold = LANES // slot
    depth = out.shape[0] // fold
    for turn, piece in enumerate(pieces):
        first = ((mid ^ (turn // 2)) * 2 + (low ^ (turn % 2))) * 2
        for box in range(2):
            for last in range(2):
                value = piece[box, last]
                if turn == 0:
                    value = jnp.where(high == core, kept[box, last], value)
                packed[last, first + box] = value
    for last in range(2):
        tile = swap_groups([packed[last, place].astype(jnp.float32) for place in range(fold)], slot)
        for place, rows in enumerate(tile):
            states[last, place * depth:(place + 1) * depth] = rows.astype(jnp.bfloat16)
    pair_box(wide, total, states, (None, None), out)


def own_kernel(pattern, wide, states, out, total):
    core = digits()[3]
    pair_box(wide, total, states, [present_of(pattern, 0, half, core) for half in range(2)], out)


def interp_kernel(interp, first_wide, second_wide):
    core = digits()[3]
    for wide, chunk in ((first_wide, core), (second_wide, 1 - core)):
        spread(wide, lambda row: interp[pl.ds(row, GROUP), :, lanes_of(chunk)], interp.shape[0], interp.shape[1])


def image_rows(level, bit, flip, pattern, wide, partner, near, total):
    places = digits()
    chunk, other = places[3] ^ flip, 1 - places[3 - bit]

    def emit(row, value):
        total[row] = (near[row] + value).astype(jnp.bfloat16).astype(jnp.float32)

    multiply(wide, state_rows(partner, present_of(pattern, level, other, chunk)), total.shape[0], emit)
    return [total[index] for index in range(total.shape[0])]


def first_image_kernel(level, bit, pattern, wide, image_wide, partner, near, out, total):
    rows = image_rows(level, bit, 0, pattern, wide, partner, near, total)

    def emit(row, value):
        out[row] = value.astype(jnp.bfloat16)

    multiply(image_wide, rows, out.shape[0], emit)


def last_kernel(level, bit, pattern, wide, image_wide, partner, near, ready, image, held, total, sems):
    core = digits()[3]
    copies = [pltpu.make_async_copy(ready, image.at[:, :, lanes_of(core)], sems.at[0])]
    copies[0].start()
    rows = image_rows(level, bit, 1, pattern, wide, partner, near, total)
    rank, parts = total.shape[0], sems.shape[0] - 1
    size = held.shape[0] // parts
    for part in range(parts):

        def emit(row, value):
            held[part * size + row] = value.astype(jnp.bfloat16)

        multiply(image_wide.at[pl.ds(part * size * rank, size * rank), :], rows, size, emit)
        span = pl.ds(part * size, size)
        copies.append(pltpu.make_async_copy(held.at[span], image.at[span, :, lanes_of(1 - core)], sems.at[part + 1]))
        copies[-1].start()
    for copy in copies:
        copy.wait()


def run(kernel, outs, operands, scratch=(), products=1, in_specs=None, out_specs=None, aliases=None, limit=KERNEL_LIMIT):
    whole = pl.BlockSpec(memory_space=pltpu.VMEM)
    single = not isinstance(outs, list)
    shapes = [outs] if single else outs
    result = pl.pallas_call(
        kernel,
        out_shape=shapes,
        in_specs=in_specs or [whole] * len(operands),
        out_specs=out_specs or [whole] * len(shapes),
        scratch_shapes=list(scratch),
        input_output_aliases=aliases or {},
        compiler_params=pltpu.CompilerParams(vmem_limit_bytes=limit),
        cost_estimate=pl.CostEstimate(flops=products * KERNEL_COST, bytes_accessed=products * KERNEL_COST, transcendentals=0),
    )(*operands)
    return result[0] if single else result


def permuted(value, target_of):
    pairs = [(source, target_of(source)) for source in range(lax.axis_size("leaf"))]
    pairs = [pair for pair in pairs if pair[0] != pair[1]]
    return lax.ppermute(value, "leaf", pairs)


def swapped(value, bit):
    return permuted(value, lambda source: source ^ 2**bit)


def crossed(source, turn):
    high, mid, low, core = source // 8 % 2, source // 4 % 2, source // 2 % 2, source % 2
    return ((core * 2 + (mid ^ (turn // 2))) * 2 + (low ^ (turn % 2))) * 2 + high


def fast_local(samples, interp_in, top_blocks, top_pattern, bottom_blocks, bottom_pattern, interp_out):
    rank, depth = interp_in.shape[:2]
    rhs_count, box_count = samples.shape[1:]
    out_depth = interp_out.shape[0]
    slot = box_count // lax.axis_size("leaf")
    fold = LANES // slot
    state = jax.ShapeDtypeStruct((rank, rhs_count, LANES), jnp.bfloat16)
    partial = jax.ShapeDtypeStruct((rank, rhs_count, LANES), jnp.float32)
    spread_out = jax.ShapeDtypeStruct((rank * rank, LANES), jnp.float32)
    pair_spread = jax.ShapeDtypeStruct((2, rank * rank, LANES), jnp.float32)
    total = pltpu.VMEM((rank, rhs_count, LANES), jnp.float32)
    wide = pltpu.VMEM((rank * rank, LANES), jnp.float32)
    packed = pltpu.VMEM((2, fold, rank // fold, rhs_count, LANES), jnp.bfloat16)

    def level_wides(blocks, level, bit, *after):
        wides = run(functools.partial(ahead_kernel, level, bit), [spread_out] * 4, (blocks, *after), products=4)
        return wides[:2], wides[2:]

    def level_nears(pattern, level, bit, order, wides, extra=()):
        return {
            flip: run(
                functools.partial(near_kernel, level, bit, flip), partial,
                (pattern, current[flip], wides[0][flip]) + ((current[1 - flip], *extra) if place < len(order) - 1 else ()),
            )
            for place, flip in enumerate(order)
        }

    def level_fars(pattern, level, bit, order, wides, extra=()):
        return {
            flip: run(
                functools.partial(far_kernel, level, bit, flip), state,
                (pattern, partner[flip], near[flip], wides[1][flip], *extra),
            )
            for flip in order
        }

    coeff_scratch = (
        pltpu.VMEM((2, rank, depth // 2, LANES), jnp.bfloat16),
        pltpu.VMEM((2, depth // 2, rhs_count, LANES), jnp.bfloat16),
        pltpu.VMEM((rank * depth // 2, LANES), jnp.float32), total, pltpu.SemaphoreType.DMA((4,)),
    )
    share_rows = 2 * rank + rank * rhs_count // (2 * rank)
    shared_shape = jax.ShapeDtypeStruct((share_rows, 2 * rank, LANES), jnp.bfloat16)
    current = {1: run(
        functools.partial(coeff_kernel, 1), state, (interp_in, samples), coeff_scratch, 2,
        in_specs=[pl.BlockSpec(memory_space=pl.ANY)] * 2, limit=START_LIMIT,
    )}
    for level in range(3):
        bit = 3 - level
        if level == 0:
            partner = {1: swapped(current[1], bit)}
            current[0], *wides = run(
                functools.partial(second_kernel, 0, 3, 0), [state] + [spread_out] * 4,
                (top_blocks, interp_in, samples, current[1]),
                coeff_scratch + (pltpu.VMEM((1, *top_blocks.shape[1:]), jnp.bfloat16), pltpu.SemaphoreType.DMA), 4,
                in_specs=[pl.BlockSpec(memory_space=pl.ANY)] * 4, limit=FETCH_LIMIT,
            )
            wides = wides[:2], wides[2:]
            partner[0] = swapped(current[0], bit)
            near = level_nears(top_pattern, level, bit, (1,), wides)
            near.update(level_nears(top_pattern, level, bit, (0,), wides))
            later_wides = {later: level_wides(top_blocks, later, 3 - later, near[0]) for later in (1, 2)}
            shared = run(
                functools.partial(share_kernel, 3), shared_shape,
                (top_blocks, top_pattern, bottom_blocks, bottom_pattern),
            )
        else:
            partner = {flip: swapped(current[flip], bit) for flip in (1, 0)}
            wides = later_wides[level]
            near = level_nears(top_pattern, level, bit, (1, 0), wides)
        if level < 2:
            current = level_fars(top_pattern, level, bit, (1, 0), wides)

    shared = run(
        functools.partial(send_kernel, 2, 1, 1), shared_shape, (top_pattern, partner[1], near[1], wides[1][1], shared), aliases={4: 0},
    )
    shared = swapped(shared, 0)
    pair_far, near_wide = run(
        functools.partial(pair_far_kernel, 3),
        [jax.ShapeDtypeStruct((2, rank, rhs_count, LANES), jnp.float32), pair_spread],
        (top_blocks, top_pattern, shared), (wide,), 2,
    )
    current = level_fars(top_pattern, 2, 1, (0,), wides, (pair_far,))

    piece = jax.ShapeDtypeStruct((2, 2, rank // fold, rhs_count, LANES), jnp.bfloat16)
    pieces = run(
        functools.partial(pair_near_kernel, 3, slot), [piece] * 4,
        (top_pattern, near_wide, current[0], pair_far), (total, packed), 2,
    )
    kept = pieces[0]
    pieces = [permuted(value, functools.partial(crossed, turn=turn)) for turn, value in enumerate(pieces)]
    own_wide, other_wide = run(wide_kernel, [pair_spread] * 2, (bottom_blocks, shared))
    wides = {level: level_wides(bottom_blocks, level, level, kept) for level in (1, 2, 3)}
    image_spread = jax.ShapeDtypeStruct((out_depth * rank, LANES), jnp.float32)
    image_wide = run(interp_kernel, [image_spread] * 2, (interp_out,))
    spreads = [wide for level in (1, 2, 3) for group in wides[level] for wide in group]
    second, states = run(
        functools.partial(open_kernel, slot), [state, jax.ShapeDtypeStruct((2, rank, rhs_count, LANES), jnp.bfloat16)],
        (other_wide, kept, *pieces, *spreads, *image_wide), (total, packed), 2,
    )
    current = {1: swapped(second, 0), 0: run(own_kernel, state, (bottom_pattern, own_wide, states), (total,), 2)}
    partner = {0: swapped(current[0], 1)}
    partner[1] = swapped(current[1], 1)
    for level in (1, 2, 3):
        if level > 1:
            partner = {flip: swapped(current[flip], level) for flip in (0, 1)}
        near = level_nears(bottom_pattern, level, level, (0, 1), wides[level])
        if level < 3:
            current = level_fars(bottom_pattern, level, level, (0, 1), wides[level])

    ready = run(
        functools.partial(first_image_kernel, 3, 3), jax.ShapeDtypeStruct((out_depth, rhs_count, LANES), jnp.bfloat16),
        (bottom_pattern, wides[3][1][0], image_wide[0], partner[0], near[0]), (total,), 3,
    )
    return run(
        functools.partial(last_kernel, 3, 3), jax.ShapeDtypeStruct((out_depth, rhs_count, box_count), jnp.bfloat16),
        (bottom_pattern, wides[3][1][1], image_wide[1], partner[1], near[1], ready),
        (pltpu.VMEM((out_depth, rhs_count, LANES), jnp.bfloat16), total, pltpu.SemaphoreType.DMA((5,))), 3,
        out_specs=[pl.BlockSpec(memory_space=pl.ANY)],
    )


def contract(weights, state):
    product = weights[:, :, None].astype(jnp.float32) * state[None].astype(jnp.float32)
    return jnp.sum(product, axis=1)


def plain_level(current, blocks, pattern, bit):
    rank = blocks.shape[0]
    partner = swapped(current, bit)
    is_lower = lax.axis_index("leaf") // 2**bit % 2 == 0
    lower = jnp.where(is_lower, current, partner)
    upper = jnp.where(is_lower, partner, current)
    weights = blocks * jnp.repeat(pattern, rank, axis=0).astype(jnp.bfloat16)[None]
    return contract(weights, jnp.concatenate([lower, upper], axis=0)).astype(jnp.bfloat16)


def plain_local(samples, interp_in, top_blocks, top_pattern, bottom_blocks, bottom_pattern, interp_out):
    bit_count = lax.axis_size("leaf").bit_length() - 1
    current = contract(interp_in, samples).astype(jnp.bfloat16)
    for level in range(top_blocks.shape[0]):
        current = plain_level(current, top_blocks[level], top_pattern[level], bit_count - 1 - level)
    flat = current.reshape(-1, current.shape[2])
    current = lax.all_to_all(flat, "leaf", split_axis=1, concat_axis=1, tiled=True).reshape(current.shape)
    for level in range(bottom_blocks.shape[0]):
        current = plain_level(current, bottom_blocks[level], bottom_pattern[level], level)
    return contract(interp_out, current).astype(jnp.bfloat16)


def local(samples, interp_in, top_blocks, *rest):
    four_digits = lax.axis_size("leaf") == 16 and top_blocks.shape[0] == 4
    chosen = fast_local if four_digits and samples.shape[1:] == (8, 2 * LANES) else plain_local
    return chosen(samples, interp_in, top_blocks, *rest)


def solution(mesh):
    boxes = ("parts", "leaf")
    return jax.shard_map(
        local,
        mesh=mesh,
        in_specs=(
            P(None, None, boxes),
            P(None, None, boxes),
            P(None, None, None, boxes),
            P(None, None, boxes),
            P(None, None, None, boxes),
            P(None, None, boxes),
            P(None, None, boxes),
        ),
        out_specs=P(None, None, boxes),
        check_vma=False,
    )
```

```python
import functools

import jax
import jax.numpy as jnp
from jax import lax
from jax.experimental import pallas as pl
from jax.experimental.pallas import tpu as pltpu
from jax.sharding import PartitionSpec as P

LANES = 128
GROUP = 4
ROWS = 8
KERNEL_COST = 1024
KERNEL_LIMIT = 16 * 2**20
FETCH_LIMIT = 53_850_000
START_LIMIT = 56_250_000


def digits():
    place = lax.axis_index("leaf")
    return lax.rem(place // 8, 2), lax.rem(place // 4, 2), lax.rem(place // 2, 2), lax.rem(place, 2)


def lanes_of(chunk):
    return pl.ds(pl.multiple_of(chunk * LANES, LANES), LANES)


def rows_of(half, rank):
    return pl.ds(pl.multiple_of(half * rank, rank), rank)


def spread(wide, load, row_count, rank):
    def body(step, carry):
        rows = load(step * GROUP).astype(jnp.float32)
        wide[pl.ds(step * GROUP * rank, GROUP * rank), :] = rows.reshape(GROUP * rank, LANES)
        return carry

    lax.fori_loop(0, row_count // GROUP, body, 0)


def multiply(wide, state, row_count, emit):
    rank = len(state)

    def body(step, carry):
        for inner in range(ROWS):
            sums = [None, None]
            for index in range(rank):
                weight = wide[pl.ds(step * ROWS * rank + inner * rank + index, 8, stride=0), :]
                term = weight * state[index]
                old = sums[index % 2]
                sums[index % 2] = term if old is None else old + term
            emit(step * ROWS + inner, sums[0] + sums[1])
        return carry

    lax.fori_loop(0, row_count // ROWS, body, 0)


def state_rows(ref, present=None):
    rows = [ref[index].astype(jnp.float32) for index in range(ref.shape[0])]
    return rows if present is None else [row * present for row in rows]


def level_load(blocks, level, half, chunk):
    rank = blocks.shape[1]
    return lambda row: blocks[level, pl.ds(row, GROUP), rows_of(half, rank), lanes_of(chunk)]


def present_of(pattern, level, half, chunk):
    pair = [pattern[level, place:place + 1, lanes_of(chunk)].astype(jnp.float32) for place in range(2)]
    return jnp.where(half == 0, pair[0], pair[1])


def coeff_kernel(flip, interp, samples, *rest):
    out, held_interp, held_samples, wide, total, sems = rest[-6:]
    rank, depth = interp.shape[0], interp.shape[1] // 2
    lanes = lanes_of(digits()[3] ^ flip)
    copies = []
    for half in range(2):
        part = pl.ds(half * depth, depth)
        copies.append(pltpu.make_async_copy(interp.at[:, part, lanes], held_interp.at[half], sems.at[half]))
        copies.append(pltpu.make_async_copy(samples.at[part, :, lanes], held_samples.at[half], sems.at[half + 2]))
    for copy in copies:
        copy.start()
    for half in range(2):
        copies[2 * half].wait()
        copies[2 * half + 1].wait()
        spread(wide, lambda row: held_interp[half, pl.ds(row, GROUP)], rank, depth)
        state = [held_samples[half, index].astype(jnp.float32) for index in range(depth)]

        def emit(row, value):
            if half == 0:
                total[row] = value
            else:
                out[row] = (total[row] + value).astype(jnp.bfloat16)

        multiply(wide, state, rank, emit)


def second_kernel(level, bit, flip, blocks, interp, samples, after, *rest):
    held, sem = rest[-2:]
    copy = pltpu.make_async_copy(blocks.at[pl.ds(level, 1)], held, sem)
    copy.start()
    coeff_kernel(flip, interp, samples, rest[0], *rest[5:-2])
    copy.wait()
    ahead_kernel(0, bit, held, *rest[1:5])


def ahead_kernel(level, bit, blocks, *rest):
    near_wides, far_wides = rest[-4:-2], rest[-2:]
    rank = blocks.shape[1]
    places = digits()
    own = places[3 - bit]
    for flip in range(2):
        chunk = places[3] ^ flip
        spread(near_wides[flip], level_load(blocks, level, own, chunk), rank, rank)
        spread(far_wides[flip], level_load(blocks, level, 1 - own, chunk), rank, rank)


def near_kernel(level, bit, flip, pattern, state, wide, *rest):
    out = rest[-1]
    places = digits()
    chunk, own = places[3] ^ flip, places[3 - bit]

    def emit(row, value):
        out[row] = value

    multiply(wide, state_rows(state, present_of(pattern, level, own, chunk)), out.shape[0], emit)


def far_kernel(level, bit, flip, pattern, partner, near, wide, *rest):
    out = rest[-1]
    places = digits()
    chunk, other = places[3] ^ flip, 1 - places[3 - bit]

    def emit(row, value):
        out[row] = (near[row] + value).astype(jnp.bfloat16)

    multiply(wide, state_rows(partner, present_of(pattern, level, other, chunk)), out.shape[0], emit)


def share_kernel(top_level, top_blocks, top_pattern, bottom_blocks, bottom_pattern, out):
    rank = top_blocks.shape[1]
    chunk = 1 - digits()[3]
    for place, (blocks, pattern, level) in enumerate(((top_blocks, top_pattern, top_level), (bottom_blocks, bottom_pattern, 0))):
        for half in range(2):
            present = present_of(pattern, level, half, chunk)[None]

            def body(step, carry):
                rows = blocks[level, pl.ds(step * 8, 8), half * rank:(half + 1) * rank, lanes_of(chunk)]
                span = pl.ds(place * rank + step * 8, 8)
                out[span, half * rank:(half + 1) * rank, :] = (rows.astype(jnp.float32) * present).astype(jnp.bfloat16)
                return carry

            lax.fori_loop(0, rank // 8, body, 0)


def shared_load(shared, place, half):
    rank = shared.shape[1] // 2
    return lambda row: shared[pl.ds(place * rank + row, GROUP), rows_of(half, rank), :]


def send_kernel(level, bit, flip, pattern, partner, near, wide, shared, *rest):
    out = rest[-1]
    rank, per = partner.shape[0], shared.shape[1] // partner.shape[1]
    places = digits()
    chunk, other = places[3] ^ flip, 1 - places[3 - bit]

    def emit(row, value):
        place = pl.ds(pl.multiple_of(lax.rem(row, per) * 8, 8), 8)
        out[2 * rank + row // per, place, :] = (near[row] + value).astype(jnp.bfloat16)

    multiply(wide, state_rows(partner, present_of(pattern, level, other, chunk)), rank, emit)


def sent_rows(shared):
    rank = shared.shape[1] // 2
    per = shared.shape[1] // 8
    return [
        shared[2 * rank + row // per, row % per * 8:(row % per + 1) * 8, :].astype(jnp.float32) for row in range(rank)
    ]


def swap_groups(tile, slot):
    lane_group = lax.broadcasted_iota(jnp.int32, tile[0].shape, 2) // slot
    step = 1
    while step < len(tile):
        low = (lane_group // step) % 2 == 0
        fresh = list(tile)
        for place in range(len(tile)):
            if place & step == 0:
                first, second = tile[place], tile[place + step]
                fresh[place] = jnp.where(low, first, pltpu.roll(second, step * slot, 2))
                fresh[place + step] = jnp.where(low, pltpu.roll(first, LANES - step * slot, 2), second)
        tile = fresh
        step *= 2
    return tile


def pair_far_kernel(level, blocks, pattern, shared, out, near_wide, wide):
    rank = blocks.shape[1]
    core = digits()[3]
    rows = sent_rows(shared)
    present = present_of(pattern, level, 1 - core, core)
    for box in range(2):
        for target, half in ((wide, 1 - core), (near_wide.at[box], core)):
            spread(target, level_load(blocks, level, half, core) if box == 0 else shared_load(shared, 0, half), rank, rank)

        def emit(row, value):
            out[box, row] = value

        multiply(wide, [row * present for row in rows] if box == 0 else rows, rank, emit)


def pair_near_kernel(level, slot, pattern, wide, state, far, *rest):
    outs, (total, packed) = rest[:4], rest[4:]
    rank = state.shape[0]
    _, mid, low, core = digits()
    rows = state_rows(state)
    present = present_of(pattern, level, core, core)
    fold = LANES // slot
    for box in range(2):

        def emit(row, value):
            total[row] = far[box, row] + value

        multiply(wide.at[box], [row * present for row in rows] if box == 0 else rows, rank, emit)
        depth = rank // fold
        pieces = swap_groups([total[place * depth:(place + 1) * depth].astype(jnp.bfloat16) for place in range(fold)], slot)
        for place, piece in enumerate(pieces):
            packed[core ^ box, place] = piece
    for turn, out in enumerate(outs):
        first = ((mid ^ (turn // 2)) * 2 + (low ^ (turn % 2))) * 2
        for box in range(2):
            for last in range(2):
                out[box, last] = packed[box, first + last]


def wide_kernel(blocks, shared, own_wide, other_wide):
    rank = blocks.shape[1]
    core = digits()[3]
    for half in range(2):
        spread(own_wide.at[half], level_load(blocks, 0, half, core), rank, rank)
        spread(other_wide.at[half], shared_load(shared, 1, half), rank, rank)


def pair_box(wide, total, states, presents, out):
    for half in range(2):
        present = presents[half]
        rows = [states[half, index].astype(jnp.float32) for index in range(out.shape[0])]
        if present is not None:
            rows = [row * present for row in rows]

        def emit(row, value):
            if half == 0:
                total[row] = value
            else:
                out[row] = (total[row] + value).astype(jnp.bfloat16)

        multiply(wide.at[half], rows, out.shape[0], emit)


def open_kernel(slot, wide, kept, *rest):
    pieces, (out, states, total, packed) = rest[:4], rest[-4:]
    high, mid, low, core = digits()
    fold = LANES // slot
    depth = out.shape[0] // fold
    for turn, piece in enumerate(pieces):
        first = ((mid ^ (turn // 2)) * 2 + (low ^ (turn % 2))) * 2
        for box in range(2):
            for last in range(2):
                value = piece[box, last]
                if turn == 0:
                    value = jnp.where(high == core, kept[box, last], value)
                packed[last, first + box] = value
    for last in range(2):
        tile = swap_groups([packed[last, place] for place in range(fold)], slot)
        for place, rows in enumerate(tile):
            states[last, place * depth:(place + 1) * depth] = rows
    pair_box(wide, total, states, (None, None), out)


def own_kernel(pattern, wide, states, out, total):
    core = digits()[3]
    pair_box(wide, total, states, [present_of(pattern, 0, half, core) for half in range(2)], out)


def interp_kernel(interp, first_wide, second_wide):
    core = digits()[3]
    for wide, chunk in ((first_wide, core), (second_wide, 1 - core)):
        spread(wide, lambda row: interp[pl.ds(row, GROUP), :, lanes_of(chunk)], interp.shape[0], interp.shape[1])


def image_rows(level, bit, flip, pattern, wide, partner, near, total):
    places = digits()
    chunk, other = places[3] ^ flip, 1 - places[3 - bit]

    def emit(row, value):
        total[row] = (near[row] + value).astype(jnp.bfloat16).astype(jnp.float32)

    multiply(wide, state_rows(partner, present_of(pattern, level, other, chunk)), total.shape[0], emit)
    return [total[index] for index in range(total.shape[0])]


def first_image_kernel(level, bit, pattern, wide, image_wide, partner, near, out, total):
    rows = image_rows(level, bit, 0, pattern, wide, partner, near, total)

    def emit(row, value):
        out[row] = value.astype(jnp.bfloat16)

    multiply(image_wide, rows, out.shape[0], emit)


def last_kernel(level, bit, pattern, wide, image_wide, partner, near, ready, image, held, total, sems):
    core = digits()[3]
    copies = [pltpu.make_async_copy(ready, image.at[:, :, lanes_of(core)], sems.at[0])]
    copies[0].start()
    rows = image_rows(level, bit, 1, pattern, wide, partner, near, total)
    rank, parts = total.shape[0], sems.shape[0] - 1
    size = held.shape[0] // parts
    for part in range(parts):

        def emit(row, value):
            held[part * size + row] = value.astype(jnp.bfloat16)

        multiply(image_wide.at[pl.ds(part * size * rank, size * rank), :], rows, size, emit)
        span = pl.ds(part * size, size)
        copies.append(pltpu.make_async_copy(held.at[span], image.at[span, :, lanes_of(1 - core)], sems.at[part + 1]))
        copies[-1].start()
    for copy in copies:
        copy.wait()


def run(kernel, outs, operands, scratch=(), products=1, in_specs=None, out_specs=None, aliases=None, limit=KERNEL_LIMIT):
    whole = pl.BlockSpec(memory_space=pltpu.VMEM)
    single = not isinstance(outs, list)
    shapes = [outs] if single else outs
    result = pl.pallas_call(
        kernel,
        out_shape=shapes,
        in_specs=in_specs or [whole] * len(operands),
        out_specs=out_specs or [whole] * len(shapes),
        scratch_shapes=list(scratch),
        input_output_aliases=aliases or {},
        compiler_params=pltpu.CompilerParams(vmem_limit_bytes=limit),
        cost_estimate=pl.CostEstimate(flops=products * KERNEL_COST, bytes_accessed=products * KERNEL_COST, transcendentals=0),
    )(*operands)
    return result[0] if single else result


def permuted(value, target_of):
    pairs = [(source, target_of(source)) for source in range(lax.axis_size("leaf"))]
    pairs = [pair for pair in pairs if pair[0] != pair[1]]
    return lax.ppermute(value, "leaf", pairs)


def swapped(value, bit):
    return permuted(value, lambda source: source ^ 2**bit)


def crossed(source, turn):
    high, mid, low, core = source // 8 % 2, source // 4 % 2, source // 2 % 2, source % 2
    return ((core * 2 + (mid ^ (turn // 2))) * 2 + (low ^ (turn % 2))) * 2 + high


def fast_local(samples, interp_in, top_blocks, top_pattern, bottom_blocks, bottom_pattern, interp_out):
    rank, depth = interp_in.shape[:2]
    rhs_count, box_count = samples.shape[1:]
    out_depth = interp_out.shape[0]
    slot = box_count // lax.axis_size("leaf")
    fold = LANES // slot
    state = jax.ShapeDtypeStruct((rank, rhs_count, LANES), jnp.bfloat16)
    partial = jax.ShapeDtypeStruct((rank, rhs_count, LANES), jnp.float32)
    spread_out = jax.ShapeDtypeStruct((rank * rank, LANES), jnp.float32)
    pair_spread = jax.ShapeDtypeStruct((2, rank * rank, LANES), jnp.float32)
    total = pltpu.VMEM((rank, rhs_count, LANES), jnp.float32)
    wide = pltpu.VMEM((rank * rank, LANES), jnp.float32)
    packed = pltpu.VMEM((2, fold, rank // fold, rhs_count, LANES), jnp.bfloat16)

    def level_wides(blocks, level, bit, *after):
        wides = run(functools.partial(ahead_kernel, level, bit), [spread_out] * 4, (blocks, *after), products=4)
        return wides[:2], wides[2:]

    def level_nears(pattern, level, bit, order, wides, extra=()):
        return {
            flip: run(
                functools.partial(near_kernel, level, bit, flip), partial,
                (pattern, current[flip], wides[0][flip]) + ((current[1 - flip], *extra) if place < len(order) - 1 else ()),
            )
            for place, flip in enumerate(order)
        }

    def level_fars(pattern, level, bit, order, wides, extra=()):
        return {
            flip: run(
                functools.partial(far_kernel, level, bit, flip), state,
                (pattern, partner[flip], near[flip], wides[1][flip]) + (tuple(extra) if place == len(order) - 1 else ()),
            )
            for place, flip in enumerate(order)
        }

    coeff_scratch = (
        pltpu.VMEM((2, rank, depth // 2, LANES), jnp.bfloat16),
        pltpu.VMEM((2, depth // 2, rhs_count, LANES), jnp.bfloat16),
        pltpu.VMEM((rank * depth // 2, LANES), jnp.float32), total, pltpu.SemaphoreType.DMA((4,)),
    )
    share_rows = 2 * rank + rank * rhs_count // (2 * rank)
    shared_shape = jax.ShapeDtypeStruct((share_rows, 2 * rank, LANES), jnp.bfloat16)
    current = {1: run(
        functools.partial(coeff_kernel, 1), state, (interp_in, samples), coeff_scratch, 2,
        in_specs=[pl.BlockSpec(memory_space=pl.ANY)] * 2, limit=START_LIMIT,
    )}
    for level in range(3):
        bit = 3 - level
        if level == 0:
            partner = {1: swapped(current[1], bit)}
            current[0], *wides = run(
                functools.partial(second_kernel, 0, 3, 0), [state] + [spread_out] * 4,
                (top_blocks, interp_in, samples, current[1]),
                coeff_scratch + (pltpu.VMEM((1, *top_blocks.shape[1:]), jnp.bfloat16), pltpu.SemaphoreType.DMA), 4,
                in_specs=[pl.BlockSpec(memory_space=pl.ANY)] * 4, limit=FETCH_LIMIT,
            )
            wides = wides[:2], wides[2:]
            partner[0] = swapped(current[0], bit)
            near = level_nears(top_pattern, level, bit, (1,), wides)
            near.update(level_nears(top_pattern, level, bit, (0,), wides))
            later_wides = {later: level_wides(top_blocks, later, 3 - later, near[0]) for later in (1, 2)}
            shared = run(
                functools.partial(share_kernel, 3), shared_shape,
                (top_blocks, top_pattern, bottom_blocks, bottom_pattern),
            )
        else:
            partner = {flip: swapped(current[flip], bit) for flip in (1, 0)}
            wides = later_wides[level]
            near = level_nears(top_pattern, level, bit, (1, 0), wides)
        if level < 2:
            current = level_fars(top_pattern, level, bit, (1, 0), wides, later_wides[2][0] if level == 0 else ())

    shared = run(
        functools.partial(send_kernel, 2, 1, 1), shared_shape, (top_pattern, partner[1], near[1], wides[1][1], shared), aliases={4: 0},
    )
    shared = swapped(shared, 0)
    pair_far, near_wide = run(
        functools.partial(pair_far_kernel, 3),
        [jax.ShapeDtypeStruct((2, rank, rhs_count, LANES), jnp.float32), pair_spread],
        (top_blocks, top_pattern, shared), (wide,), 2,
    )
    current = level_fars(top_pattern, 2, 1, (0,), wides, (pair_far,))

    piece = jax.ShapeDtypeStruct((2, 2, rank // fold, rhs_count, LANES), jnp.bfloat16)
    pieces = run(
        functools.partial(pair_near_kernel, 3, slot), [piece] * 4,
        (top_pattern, near_wide, current[0], pair_far), (total, packed), 2,
    )
    kept = pieces[0]
    pieces = [permuted(value, functools.partial(crossed, turn=turn)) for turn, value in enumerate(pieces)]
    own_wide, other_wide = run(wide_kernel, [pair_spread] * 2, (bottom_blocks, shared))
    wides = {level: level_wides(bottom_blocks, level, level, kept) for level in (1, 2, 3)}
    image_spread = jax.ShapeDtypeStruct((out_depth * rank, LANES), jnp.float32)
    image_wide = run(interp_kernel, [image_spread] * 2, (interp_out,))
    spreads = [wide for level in (1, 2, 3) for group in wides[level] for wide in group]
    second, states = run(
        functools.partial(open_kernel, slot), [state, jax.ShapeDtypeStruct((2, rank, rhs_count, LANES), jnp.bfloat16)],
        (other_wide, kept, *pieces, *spreads, *image_wide), (total, packed), 2,
    )
    current = {1: swapped(second, 0), 0: run(own_kernel, state, (bottom_pattern, own_wide, states), (total,), 2)}
    partner = {0: swapped(current[0], 1)}
    partner[1] = swapped(current[1], 1)
    for level in (1, 2, 3):
        if level > 1:
            partner = {flip: swapped(current[flip], level) for flip in (0, 1)}
        near = level_nears(bottom_pattern, level, level, (0, 1), wides[level])
        if level < 3:
            current = level_fars(bottom_pattern, level, level, (0, 1), wides[level])

    ready = run(
        functools.partial(first_image_kernel, 3, 3), jax.ShapeDtypeStruct((out_depth, rhs_count, LANES), jnp.bfloat16),
        (bottom_pattern, wides[3][1][0], image_wide[0], partner[0], near[0]), (total,), 3,
    )
    return run(
        functools.partial(last_kernel, 3, 3), jax.ShapeDtypeStruct((out_depth, rhs_count, box_count), jnp.bfloat16),
        (bottom_pattern, wides[3][1][1], image_wide[1], partner[1], near[1], ready),
        (pltpu.VMEM((out_depth, rhs_count, LANES), jnp.bfloat16), total, pltpu.SemaphoreType.DMA((5,))), 3,
        out_specs=[pl.BlockSpec(memory_space=pl.ANY)],
    )


def contract(weights, state):
    product = weights[:, :, None].astype(jnp.float32) * state[None].astype(jnp.float32)
    return jnp.sum(product, axis=1)


def plain_level(current, blocks, pattern, bit):
    rank = blocks.shape[0]
    partner = swapped(current, bit)
    is_lower = lax.axis_index("leaf") // 2**bit % 2 == 0
    lower = jnp.where(is_lower, current, partner)
    upper = jnp.where(is_lower, partner, current)
    weights = blocks * jnp.repeat(pattern, rank, axis=0).astype(jnp.bfloat16)[None]
    return contract(weights, jnp.concatenate([lower, upper], axis=0)).astype(jnp.bfloat16)


def plain_local(samples, interp_in, top_blocks, top_pattern, bottom_blocks, bottom_pattern, interp_out):
    bit_count = lax.axis_size("leaf").bit_length() - 1
    current = contract(interp_in, samples).astype(jnp.bfloat16)
    for level in range(top_blocks.shape[0]):
        current = plain_level(current, top_blocks[level], top_pattern[level], bit_count - 1 - level)
    flat = current.reshape(-1, current.shape[2])
    current = lax.all_to_all(flat, "leaf", split_axis=1, concat_axis=1, tiled=True).reshape(current.shape)
    for level in range(bottom_blocks.shape[0]):
        current = plain_level(current, bottom_blocks[level], bottom_pattern[level], level)
    return contract(interp_out, current).astype(jnp.bfloat16)


def local(samples, interp_in, top_blocks, *rest):
    four_digits = lax.axis_size("leaf") == 16 and top_blocks.shape[0] == 4
    chosen = fast_local if four_digits and samples.shape[1:] == (8, 2 * LANES) else plain_local
    return chosen(samples, interp_in, top_blocks, *rest)


def solution(mesh):
    boxes = ("parts", "leaf")
    return jax.shard_map(
        local,
        mesh=mesh,
        in_specs=(
            P(None, None, boxes),
            P(None, None, boxes),
            P(None, None, None, boxes),
            P(None, None, boxes),
            P(None, None, None, boxes),
            P(None, None, boxes),
            P(None, None, boxes),
        ),
        out_specs=P(None, None, boxes),
        check_vma=False,
    )
```

```python
import functools

import jax
import jax.numpy as jnp
from jax import lax
from jax.experimental import pallas as pl
from jax.experimental.pallas import tpu as pltpu
from jax.sharding import PartitionSpec as P

LANES = 128
GROUP = 4
ROWS = 8
KERNEL_COST = 2**19
KERNEL_LIMIT = 16 * 2**20
FETCH_LIMIT = 53_850_000
START_LIMIT = 56_250_000


def digits():
    place = lax.axis_index("leaf")
    return lax.rem(place // 8, 2), lax.rem(place // 4, 2), lax.rem(place // 2, 2), lax.rem(place, 2)


def lanes_of(chunk):
    return pl.ds(pl.multiple_of(chunk * LANES, LANES), LANES)


def rows_of(half, rank):
    return pl.ds(pl.multiple_of(half * rank, rank), rank)


def spread(wide, load, row_count, rank):
    def body(step, carry):
        rows = load(step * GROUP).astype(jnp.float32)
        wide[pl.ds(step * GROUP * rank, GROUP * rank), :] = rows.reshape(GROUP * rank, LANES)
        return carry

    lax.fori_loop(0, row_count // GROUP, body, 0)


def multiply(wide, state, row_count, emit):
    rank = len(state)

    def body(step, carry):
        for inner in range(ROWS):
            sums = [None, None]
            for index in range(rank):
                weight = wide[pl.ds(step * ROWS * rank + inner * rank + index, 8, stride=0), :]
                term = weight * state[index]
                old = sums[index % 2]
                sums[index % 2] = term if old is None else old + term
            emit(step * ROWS + inner, sums[0] + sums[1])
        return carry

    lax.fori_loop(0, row_count // ROWS, body, 0)


def state_rows(ref, present=None):
    rows = [ref[index].astype(jnp.float32) for index in range(ref.shape[0])]
    return rows if present is None else [row * present for row in rows]


def level_load(blocks, level, half, chunk):
    rank = blocks.shape[1]
    return lambda row: blocks[level, pl.ds(row, GROUP), rows_of(half, rank), lanes_of(chunk)]


def present_of(pattern, level, half, chunk):
    pair = [pattern[level, place:place + 1, lanes_of(chunk)].astype(jnp.float32) for place in range(2)]
    return jnp.where(half == 0, pair[0], pair[1])


def coeff_kernel(flip, interp, samples, *rest):
    out, held_interp, held_samples, wide, total, sems = rest[-6:]
    rank, depth = interp.shape[0], interp.shape[1] // 2
    lanes = lanes_of(digits()[3] ^ flip)
    copies = []
    for half in range(2):
        part = pl.ds(half * depth, depth)
        copies.append(pltpu.make_async_copy(interp.at[:, part, lanes], held_interp.at[half], sems.at[half]))
        copies.append(pltpu.make_async_copy(samples.at[part, :, lanes], held_samples.at[half], sems.at[half + 2]))
    for copy in copies:
        copy.start()
    for half in range(2):
        copies[2 * half].wait()
        copies[2 * half + 1].wait()
        spread(wide, lambda row: held_interp[half, pl.ds(row, GROUP)], rank, depth)
        state = [held_samples[half, index].astype(jnp.float32) for index in range(depth)]

        def emit(row, value):
            if half == 0:
                total[row] = value
            else:
                out[row] = (total[row] + value).astype(jnp.bfloat16)

        multiply(wide, state, rank, emit)


def second_kernel(flip, blocks, interp, samples, after, out, held, *rest):
    sem = rest[-1]
    copy = pltpu.make_async_copy(blocks.at[pl.ds(0, 1)], held, sem)
    copy.start()
    coeff_kernel(flip, interp, samples, out, *rest[:-1])
    copy.wait()


def ahead_kernel(level, bit, blocks, *rest):
    near_wides, far_wides = rest[-4:-2], rest[-2:]
    rank = blocks.shape[1]
    places = digits()
    own = places[3 - bit]
    for flip in range(2):
        chunk = places[3] ^ flip
        spread(near_wides[flip], level_load(blocks, level, own, chunk), rank, rank)
        spread(far_wides[flip], level_load(blocks, level, 1 - own, chunk), rank, rank)


def near_kernel(level, bit, flip, pattern, state, wide, *rest):
    out = rest[-1]
    places = digits()
    chunk, own = places[3] ^ flip, places[3 - bit]

    def emit(row, value):
        out[row] = value

    multiply(wide, state_rows(state, present_of(pattern, level, own, chunk)), out.shape[0], emit)


def far_kernel(level, bit, flip, pattern, partner, near, wide, *rest):
    out = rest[-1]
    places = digits()
    chunk, other = places[3] ^ flip, 1 - places[3 - bit]

    def emit(row, value):
        out[row] = (near[row] + value).astype(jnp.bfloat16)

    multiply(wide, state_rows(partner, present_of(pattern, level, other, chunk)), out.shape[0], emit)


def share_kernel(top_level, top_blocks, top_pattern, bottom_blocks, bottom_pattern, out):
    rank = top_blocks.shape[1]
    chunk = 1 - digits()[3]
    for place, (blocks, pattern, level) in enumerate(((top_blocks, top_pattern, top_level), (bottom_blocks, bottom_pattern, 0))):
        for half in range(2):
            present = present_of(pattern, level, half, chunk)[None]

            def body(step, carry):
                rows = blocks[level, pl.ds(step * 8, 8), half * rank:(half + 1) * rank, lanes_of(chunk)]
                span = pl.ds(place * rank + step * 8, 8)
                out[span, half * rank:(half + 1) * rank, :] = (rows.astype(jnp.float32) * present).astype(jnp.bfloat16)
                return carry

            lax.fori_loop(0, rank // 8, body, 0)


def shared_load(shared, place, half):
    rank = shared.shape[1] // 2
    return lambda row: shared[pl.ds(place * rank + row, GROUP), rows_of(half, rank), :]


def send_kernel(level, bit, flip, pattern, partner, near, wide, shared, *rest):
    out = rest[-1]
    rank, per = partner.shape[0], shared.shape[1] // partner.shape[1]
    places = digits()
    chunk, other = places[3] ^ flip, 1 - places[3 - bit]

    def emit(row, value):
        place = pl.ds(pl.multiple_of(lax.rem(row, per) * 8, 8), 8)
        out[2 * rank + row // per, place, :] = (near[row] + value).astype(jnp.bfloat16)

    multiply(wide, state_rows(partner, present_of(pattern, level, other, chunk)), rank, emit)


def sent_rows(shared):
    rank = shared.shape[1] // 2
    per = shared.shape[1] // 8
    return [
        shared[2 * rank + row // per, row % per * 8:(row % per + 1) * 8, :].astype(jnp.float32) for row in range(rank)
    ]


def swap_groups(tile, slot):
    axis = tile[0].ndim - 1
    lane_group = lax.broadcasted_iota(jnp.int32, tile[0].shape, axis) // slot
    step = 1
    while step < len(tile):
        low = (lane_group // step) % 2 == 0
        fresh = list(tile)
        for place in range(len(tile)):
            if place & step == 0:
                first, second = tile[place], tile[place + step]
                fresh[place] = jnp.where(low, first, pltpu.roll(second, step * slot, axis))
                fresh[place + step] = jnp.where(low, pltpu.roll(first, LANES - step * slot, axis), second)
        tile = fresh
        step *= 2
    return tile


def pair_far_kernel(level, blocks, pattern, shared, out, near_wide, wide):
    rank = blocks.shape[1]
    core = digits()[3]
    rows = sent_rows(shared)
    present = present_of(pattern, level, 1 - core, core)
    for box in range(2):
        for target, half in ((wide, 1 - core), (near_wide.at[box], core)):
            spread(target, level_load(blocks, level, half, core) if box == 0 else shared_load(shared, 0, half), rank, rank)

        def emit(row, value):
            out[box, row] = value

        multiply(wide, [row * present for row in rows] if box == 0 else rows, rank, emit)


def pair_near_kernel(level, slot, pattern, wide, state, far, *rest):
    outs, (total, packed) = rest[:4], rest[4:]
    rank = state.shape[0]
    _, mid, low, core = digits()
    rows = state_rows(state)
    present = present_of(pattern, level, core, core)
    fold = LANES // slot
    for box in range(2):

        def emit(row, value):
            total[row] = far[box, row] + value

        multiply(wide.at[box], [row * present for row in rows] if box == 0 else rows, rank, emit)
        depth = rank // fold
        rows_of_piece = depth * total.shape[1]
        flat = total[...].reshape(fold, rows_of_piece, LANES).astype(jnp.bfloat16)
        pieces = swap_groups([flat[place] for place in range(fold)], slot)
        for place, piece in enumerate(pieces):
            packed[core ^ box, place] = piece
    for turn, out in enumerate(outs):
        first = ((mid ^ (turn // 2)) * 2 + (low ^ (turn % 2))) * 2
        for box in range(2):
            for last in range(2):
                out[box, last] = packed[box, first + last]


def wide_kernel(blocks, shared, own_wide, other_wide):
    rank = blocks.shape[1]
    core = digits()[3]
    for half in range(2):
        spread(own_wide.at[half], level_load(blocks, 0, half, core), rank, rank)
        spread(other_wide.at[half], shared_load(shared, 1, half), rank, rank)


def pair_box(wide, total, states, presents, out):
    for half in range(2):
        present = presents[half]
        rows = [states[half, index].astype(jnp.float32) for index in range(out.shape[0])]
        if present is not None:
            rows = [row * present for row in rows]

        def emit(row, value):
            if half == 0:
                total[row] = value
            else:
                out[row] = (total[row] + value).astype(jnp.bfloat16)

        multiply(wide.at[half], rows, out.shape[0], emit)


def open_kernel(slot, wide, kept, *rest):
    pieces, (out, states, total, packed) = rest[:4], rest[-4:]
    high, mid, low, core = digits()
    fold = LANES // slot
    depth = out.shape[0] // fold
    for turn, piece in enumerate(pieces):
        first = ((mid ^ (turn // 2)) * 2 + (low ^ (turn % 2))) * 2
        for box in range(2):
            for last in range(2):
                value = piece[box, last]
                if turn == 0:
                    value = jnp.where(high == core, kept[box, last], value)
                packed[last, first + box] = value
    for last in range(2):
        tile = swap_groups([packed[last, place] for place in range(fold)], slot)
        for place, rows in enumerate(tile):
            rows = rows.astype(jnp.float32).reshape(depth, states.shape[2], LANES)
            states[last, place * depth:(place + 1) * depth] = rows.astype(jnp.bfloat16)
    pair_box(wide, total, states, (None, None), out)


def own_kernel(pattern, wide, states, out, total):
    core = digits()[3]
    pair_box(wide, total, states, [present_of(pattern, 0, half, core) for half in range(2)], out)


def interp_kernel(interp, first_wide, second_wide):
    core = digits()[3]
    for wide, chunk in ((first_wide, core), (second_wide, 1 - core)):
        spread(wide, lambda row: interp[pl.ds(row, GROUP), :, lanes_of(chunk)], interp.shape[0], interp.shape[1])


def image_rows(level, bit, flip, pattern, wide, partner, near, total):
    places = digits()
    chunk, other = places[3] ^ flip, 1 - places[3 - bit]

    def emit(row, value):
        total[row] = (near[row] + value).astype(jnp.bfloat16).astype(jnp.float32)

    multiply(wide, state_rows(partner, present_of(pattern, level, other, chunk)), total.shape[0], emit)
    return [total[index] for index in range(total.shape[0])]


def first_image_kernel(level, bit, pattern, wide, image_wide, partner, near, out, total):
    rows = image_rows(level, bit, 0, pattern, wide, partner, near, total)

    def emit(row, value):
        out[row] = value.astype(jnp.bfloat16)

    multiply(image_wide, rows, out.shape[0], emit)


def last_kernel(level, bit, pattern, wide, image_wide, partner, near, ready, image, held, total, sems):
    core = digits()[3]
    copies = [pltpu.make_async_copy(ready, image.at[:, :, lanes_of(core)], sems.at[0])]
    copies[0].start()
    rows = image_rows(level, bit, 1, pattern, wide, partner, near, total)
    rank, parts = total.shape[0], sems.shape[0] - 1
    size = held.shape[0] // parts
    for part in range(parts):

        def emit(row, value):
            held[part * size + row] = value.astype(jnp.bfloat16)

        multiply(image_wide.at[pl.ds(part * size * rank, size * rank), :], rows, size, emit)
        span = pl.ds(part * size, size)
        copies.append(pltpu.make_async_copy(held.at[span], image.at[span, :, lanes_of(1 - core)], sems.at[part + 1]))
        copies[-1].start()
    for copy in copies:
        copy.wait()


def run(kernel, outs, operands, scratch=(), products=1, in_specs=None, out_specs=None, aliases=None, limit=KERNEL_LIMIT):
    whole = pl.BlockSpec(memory_space=pltpu.VMEM)
    single = not isinstance(outs, list)
    shapes = [outs] if single else outs
    result = pl.pallas_call(
        kernel,
        out_shape=shapes,
        in_specs=in_specs or [whole] * len(operands),
        out_specs=out_specs or [whole] * len(shapes),
        scratch_shapes=list(scratch),
        input_output_aliases=aliases or {},
        compiler_params=pltpu.CompilerParams(vmem_limit_bytes=limit),
        cost_estimate=pl.CostEstimate(flops=products * KERNEL_COST, bytes_accessed=products * KERNEL_COST, transcendentals=0),
    )(*operands)
    return result[0] if single else result


def permuted(value, target_of):
    pairs = [(source, target_of(source)) for source in range(lax.axis_size("leaf"))]
    pairs = [pair for pair in pairs if pair[0] != pair[1]]
    return lax.ppermute(value, "leaf", pairs)


def swapped(value, bit):
    return permuted(value, lambda source: source ^ 2**bit)


def crossed(source, turn):
    high, mid, low, core = source // 8 % 2, source // 4 % 2, source // 2 % 2, source % 2
    return ((core * 2 + (mid ^ (turn // 2))) * 2 + (low ^ (turn % 2))) * 2 + high


def fast_local(samples, interp_in, top_blocks, top_pattern, bottom_blocks, bottom_pattern, interp_out):
    rank, depth = interp_in.shape[:2]
    rhs_count, box_count = samples.shape[1:]
    out_depth = interp_out.shape[0]
    slot = box_count // lax.axis_size("leaf")
    fold = LANES // slot
    state = jax.ShapeDtypeStruct((rank, rhs_count, LANES), jnp.bfloat16)
    partial = jax.ShapeDtypeStruct((rank, rhs_count, LANES), jnp.float32)
    spread_out = jax.ShapeDtypeStruct((rank * rank, LANES), jnp.float32)
    pair_spread = jax.ShapeDtypeStruct((2, rank * rank, LANES), jnp.float32)
    total = pltpu.VMEM((rank, rhs_count, LANES), jnp.float32)
    wide = pltpu.VMEM((rank * rank, LANES), jnp.float32)
    packed = pltpu.VMEM((2, fold, rank // fold * rhs_count, LANES), jnp.bfloat16)

    def level_wides(blocks, level, bit, *after):
        wides = run(functools.partial(ahead_kernel, level, bit), [spread_out] * 4, (blocks, *after), products=4)
        return wides[:2], wides[2:]

    def level_nears(pattern, level, bit, order, wides, extra=()):
        return {
            flip: run(
                functools.partial(near_kernel, level, bit, flip), partial,
                (pattern, current[flip], wides[0][flip]) + ((current[1 - flip], *extra) if place < len(order) - 1 else ()),
            )
            for place, flip in enumerate(order)
        }

    def level_fars(pattern, level, bit, order, wides, extra=()):
        return {
            flip: run(
                functools.partial(far_kernel, level, bit, flip), state,
                (pattern, partner[flip], near[flip], wides[1][flip]) + (tuple(extra) if place == len(order) - 1 else ()),
            )
            for place, flip in enumerate(order)
        }

    coeff_scratch = (
        pltpu.VMEM((2, rank, depth // 2, LANES), jnp.bfloat16),
        pltpu.VMEM((2, depth // 2, rhs_count, LANES), jnp.bfloat16),
        pltpu.VMEM((rank * depth // 2, LANES), jnp.float32), total, pltpu.SemaphoreType.DMA((4,)),
    )
    share_rows = 2 * rank + rank * rhs_count // (2 * rank)
    shared_shape = jax.ShapeDtypeStruct((share_rows, 2 * rank, LANES), jnp.bfloat16)
    current = {1: run(
        functools.partial(coeff_kernel, 1), state, (interp_in, samples), coeff_scratch, 2,
        in_specs=[pl.BlockSpec(memory_space=pl.ANY)] * 2, limit=START_LIMIT,
    )}
    for level in range(3):
        bit = 3 - level
        if level == 0:
            partner = {1: swapped(current[1], bit)}
            current[0], first_blocks = run(
                functools.partial(second_kernel, 0),
                [state, jax.ShapeDtypeStruct((1, *top_blocks.shape[1:]), jnp.bfloat16)],
                (top_blocks, interp_in, samples, current[1]), coeff_scratch + (pltpu.SemaphoreType.DMA,), 4,
                in_specs=[pl.BlockSpec(memory_space=pl.ANY)] * 4, limit=FETCH_LIMIT,
            )
            wides = level_wides(first_blocks, 0, bit)
            partner[0] = swapped(current[0], bit)
            near = level_nears(top_pattern, level, bit, (1,), wides)
            near.update(level_nears(top_pattern, level, bit, (0,), wides))
            later_wides = {later: level_wides(top_blocks, later, 3 - later, near[0]) for later in (1, 2)}
            shared = run(
                functools.partial(share_kernel, 3), shared_shape,
                (top_blocks, top_pattern, bottom_blocks, bottom_pattern),
            )
        else:
            partner = {flip: swapped(current[flip], bit) for flip in (1, 0)}
            wides = later_wides[level]
            near = level_nears(top_pattern, level, bit, (1, 0), wides)
        if level < 2:
            current = level_fars(top_pattern, level, bit, (1, 0), wides, later_wides[2][0] if level == 0 else ())

    shared = run(
        functools.partial(send_kernel, 2, 1, 1), shared_shape, (top_pattern, partner[1], near[1], wides[1][1], shared), aliases={4: 0},
    )
    shared = swapped(shared, 0)
    pair_far, near_wide = run(
        functools.partial(pair_far_kernel, 3),
        [jax.ShapeDtypeStruct((2, rank, rhs_count, LANES), jnp.float32), pair_spread],
        (top_blocks, top_pattern, shared), (wide,), 2,
    )
    current = level_fars(top_pattern, 2, 1, (0,), wides, (pair_far,))

    piece = jax.ShapeDtypeStruct((2, 2, rank // fold * rhs_count, LANES), jnp.bfloat16)
    pieces = run(
        functools.partial(pair_near_kernel, 3, slot), [piece] * 4,
        (top_pattern, near_wide, current[0], pair_far), (total, packed), 2,
    )
    kept = pieces[0]
    pieces = [permuted(value, functools.partial(crossed, turn=turn)) for turn, value in enumerate(pieces)]
    own_wide, other_wide = run(wide_kernel, [pair_spread] * 2, (bottom_blocks, shared))
    wides = {level: level_wides(bottom_blocks, level, level, kept) for level in (1, 2, 3)}
    image_spread = jax.ShapeDtypeStruct((out_depth * rank, LANES), jnp.float32)
    image_wide = run(interp_kernel, [image_spread] * 2, (interp_out,))
    spreads = [wide for level in (1, 2, 3) for group in wides[level] for wide in group]
    second, states = run(
        functools.partial(open_kernel, slot), [state, jax.ShapeDtypeStruct((2, rank, rhs_count, LANES), jnp.bfloat16)],
        (other_wide, kept, *pieces, *spreads, *image_wide), (total, packed), 2,
    )
    current = {1: swapped(second, 0), 0: run(own_kernel, state, (bottom_pattern, own_wide, states), (total,), 2)}
    partner = {0: swapped(current[0], 1)}
    partner[1] = swapped(current[1], 1)
    for level in (1, 2, 3):
        if level > 1:
            partner = {flip: swapped(current[flip], level) for flip in (0, 1)}
        near = level_nears(bottom_pattern, level, level, (0, 1), wides[level])
        if level < 3:
            current = level_fars(bottom_pattern, level, level, (0, 1), wides[level])

    ready = run(
        functools.partial(first_image_kernel, 3, 3), jax.ShapeDtypeStruct((out_depth, rhs_count, LANES), jnp.bfloat16),
        (bottom_pattern, wides[3][1][0], image_wide[0], partner[0], near[0]), (total,), 3,
    )
    return run(
        functools.partial(last_kernel, 3, 3), jax.ShapeDtypeStruct((out_depth, rhs_count, box_count), jnp.bfloat16),
        (bottom_pattern, wides[3][1][1], image_wide[1], partner[1], near[1], ready),
        (pltpu.VMEM((out_depth, rhs_count, LANES), jnp.bfloat16), total, pltpu.SemaphoreType.DMA((5,))), 3,
        out_specs=[pl.BlockSpec(memory_space=pl.ANY)],
    )


def contract(weights, state):
    product = weights[:, :, None].astype(jnp.float32) * state[None].astype(jnp.float32)
    return jnp.sum(product, axis=1)


def plain_level(current, blocks, pattern, bit):
    rank = blocks.shape[0]
    partner = swapped(current, bit)
    is_lower = lax.axis_index("leaf") // 2**bit % 2 == 0
    lower = jnp.where(is_lower, current, partner)
    upper = jnp.where(is_lower, partner, current)
    weights = blocks * jnp.repeat(pattern, rank, axis=0).astype(jnp.bfloat16)[None]
    return contract(weights, jnp.concatenate([lower, upper], axis=0)).astype(jnp.bfloat16)


def plain_local(samples, interp_in, top_blocks, top_pattern, bottom_blocks, bottom_pattern, interp_out):
    bit_count = lax.axis_size("leaf").bit_length() - 1
    current = contract(interp_in, samples).astype(jnp.bfloat16)
    for level in range(top_blocks.shape[0]):
        current = plain_level(current, top_blocks[level], top_pattern[level], bit_count - 1 - level)
    flat = current.reshape(-1, current.shape[2])
    current = lax.all_to_all(flat, "leaf", split_axis=1, concat_axis=1, tiled=True).reshape(current.shape)
    for level in range(bottom_blocks.shape[0]):
        current = plain_level(current, bottom_blocks[level], bottom_pattern[level], level)
    return contract(interp_out, current).astype(jnp.bfloat16)


def local(samples, interp_in, top_blocks, *rest):
    four_digits = lax.axis_size("leaf") == 16 and top_blocks.shape[0] == 4
    chosen = fast_local if four_digits and samples.shape[1:] == (8, 2 * LANES) else plain_local
    return chosen(samples, interp_in, top_blocks, *rest)


def solution(mesh):
    boxes = ("parts", "leaf")
    return jax.shard_map(
        local,
        mesh=mesh,
        in_specs=(
            P(None, None, boxes),
            P(None, None, boxes),
            P(None, None, None, boxes),
            P(None, None, boxes),
            P(None, None, None, boxes),
            P(None, None, boxes),
            P(None, None, boxes),
        ),
        out_specs=P(None, None, boxes),
        check_vma=False,
    )
```

```python
import functools

import jax
import jax.numpy as jnp
from jax import lax
from jax.experimental import pallas as pl
from jax.experimental.pallas import tpu as pltpu
from jax.sharding import PartitionSpec as P

LANES = 128
GROUP = 4
ROWS = 8
KERNEL_COST = 2**19
KERNEL_LIMIT = 16 * 2**20
FETCH_LIMIT = 53_850_000
START_LIMIT = 56_250_000


def digits():
    place = lax.axis_index("leaf")
    return lax.rem(place // 8, 2), lax.rem(place // 4, 2), lax.rem(place // 2, 2), lax.rem(place, 2)


def lanes_of(chunk):
    return pl.ds(pl.multiple_of(chunk * LANES, LANES), LANES)


def rows_of(half, rank):
    return pl.ds(pl.multiple_of(half * rank, rank), rank)


def spread(wide, load, row_count, rank):
    def body(step, carry):
        rows = load(step * GROUP).astype(jnp.float32)
        wide[pl.ds(step * GROUP * rank, GROUP * rank), :] = rows.reshape(GROUP * rank, LANES)
        return carry

    lax.fori_loop(0, row_count // GROUP, body, 0)


def multiply(wide, state, row_count, emit):
    rank = len(state)

    def body(step, carry):
        for inner in range(ROWS):
            sums = [None, None]
            for index in range(rank):
                weight = wide[pl.ds(step * ROWS * rank + inner * rank + index, 8, stride=0), :]
                term = weight * state[index]
                old = sums[index % 2]
                sums[index % 2] = term if old is None else old + term
            emit(step * ROWS + inner, sums[0] + sums[1])
        return carry

    lax.fori_loop(0, row_count // ROWS, body, 0)


def state_rows(ref, present=None):
    rows = [ref[index].astype(jnp.float32) for index in range(ref.shape[0])]
    return rows if present is None else [row * present for row in rows]


def level_load(blocks, level, half, chunk):
    rank = blocks.shape[1]
    return lambda row: blocks[level, pl.ds(row, GROUP), rows_of(half, rank), lanes_of(chunk)]


def present_of(pattern, level, half, chunk):
    pair = [pattern[level, place:place + 1, lanes_of(chunk)].astype(jnp.float32) for place in range(2)]
    return jnp.where(half == 0, pair[0], pair[1])


def coeff_kernel(flip, interp, samples, *rest):
    out, held_interp, held_samples, wide, total, sems = rest[-6:]
    rank, depth = interp.shape[0], interp.shape[1] // 2
    lanes = lanes_of(digits()[3] ^ flip)
    copies = []
    for half in range(2):
        part = pl.ds(half * depth, depth)
        copies.append(pltpu.make_async_copy(interp.at[:, part, lanes], held_interp.at[half], sems.at[half]))
        copies.append(pltpu.make_async_copy(samples.at[part, :, lanes], held_samples.at[half], sems.at[half + 2]))
    for copy in copies:
        copy.start()
    for half in range(2):
        copies[2 * half].wait()
        copies[2 * half + 1].wait()
        spread(wide, lambda row: held_interp[half, pl.ds(row, GROUP)], rank, depth)
        state = [held_samples[half, index].astype(jnp.float32) for index in range(depth)]

        def emit(row, value):
            if half == 0:
                total[row] = value
            else:
                out[row] = (total[row] + value).astype(jnp.bfloat16)

        multiply(wide, state, rank, emit)


def second_kernel(level, bit, flip, blocks, interp, samples, after, *rest):
    held, sem = rest[-2:]
    copy = pltpu.make_async_copy(blocks.at[pl.ds(level, 1)], held, sem)
    copy.start()
    coeff_kernel(flip, interp, samples, rest[0], *rest[5:-2])
    copy.wait()
    ahead_kernel(0, bit, held, *rest[1:5])


def ahead_kernel(level, bit, blocks, *rest):
    near_wides, far_wides = rest[-4:-2], rest[-2:]
    rank = blocks.shape[1]
    places = digits()
    own = places[3 - bit]
    for flip in range(2):
        chunk = places[3] ^ flip
        spread(near_wides[flip], level_load(blocks, level, own, chunk), rank, rank)
        spread(far_wides[flip], level_load(blocks, level, 1 - own, chunk), rank, rank)


def near_kernel(level, bit, flip, pattern, state, wide, *rest):
    out = rest[-1]
    places = digits()
    chunk, own = places[3] ^ flip, places[3 - bit]

    def emit(row, value):
        out[row] = value

    multiply(wide, state_rows(state, present_of(pattern, level, own, chunk)), out.shape[0], emit)


def far_kernel(level, bit, flip, pattern, partner, near, wide, *rest):
    out = rest[-1]
    places = digits()
    chunk, other = places[3] ^ flip, 1 - places[3 - bit]

    def emit(row, value):
        out[row] = (near[row] + value).astype(jnp.bfloat16)

    multiply(wide, state_rows(partner, present_of(pattern, level, other, chunk)), out.shape[0], emit)


def share_kernel(top_level, top_blocks, top_pattern, bottom_blocks, bottom_pattern, out):
    rank = top_blocks.shape[1]
    chunk = 1 - digits()[3]
    for place, (blocks, pattern, level) in enumerate(((top_blocks, top_pattern, top_level), (bottom_blocks, bottom_pattern, 0))):
        for half in range(2):
            present = present_of(pattern, level, half, chunk)[None]

            def body(step, carry):
                rows = blocks[level, pl.ds(step * 8, 8), half * rank:(half + 1) * rank, lanes_of(chunk)]
                span = pl.ds(place * rank + step * 8, 8)
                out[span, half * rank:(half + 1) * rank, :] = (rows.astype(jnp.float32) * present).astype(jnp.bfloat16)
                return carry

            lax.fori_loop(0, rank // 8, body, 0)


def shared_load(shared, place, half):
    rank = shared.shape[1] // 2
    return lambda row: shared[pl.ds(place * rank + row, GROUP), rows_of(half, rank), :]


def send_kernel(level, bit, flip, pattern, partner, near, wide, shared, *rest):
    out = rest[-1]
    rank, per = partner.shape[0], shared.shape[1] // partner.shape[1]
    places = digits()
    chunk, other = places[3] ^ flip, 1 - places[3 - bit]

    def emit(row, value):
        place = pl.ds(pl.multiple_of(lax.rem(row, per) * 8, 8), 8)
        out[2 * rank + row // per, place, :] = (near[row] + value).astype(jnp.bfloat16)

    multiply(wide, state_rows(partner, present_of(pattern, level, other, chunk)), rank, emit)


def sent_rows(shared):
    rank = shared.shape[1] // 2
    per = shared.shape[1] // 8
    return [
        shared[2 * rank + row // per, row % per * 8:(row % per + 1) * 8, :].astype(jnp.float32) for row in range(rank)
    ]


def swap_groups(tile, slot):
    axis = tile[0].ndim - 1
    lane_group = lax.broadcasted_iota(jnp.int32, tile[0].shape, axis) // slot
    step = 1
    while step < len(tile):
        low = (lane_group // step) % 2 == 0
        fresh = list(tile)
        for place in range(len(tile)):
            if place & step == 0:
                first, second = tile[place], tile[place + step]
                fresh[place] = jnp.where(low, first, pltpu.roll(second, step * slot, axis))
                fresh[place + step] = jnp.where(low, pltpu.roll(first, LANES - step * slot, axis), second)
        tile = fresh
        step *= 2
    return tile


def pair_far_kernel(level, blocks, pattern, shared, out, near_wide, wide):
    rank = blocks.shape[1]
    core = digits()[3]
    rows = sent_rows(shared)
    present = present_of(pattern, level, 1 - core, core)
    for box in range(2):
        for target, half in ((wide, 1 - core), (near_wide.at[box], core)):
            spread(target, level_load(blocks, level, half, core) if box == 0 else shared_load(shared, 0, half), rank, rank)

        def emit(row, value):
            out[box, row] = value

        multiply(wide, [row * present for row in rows] if box == 0 else rows, rank, emit)


def pair_near_kernel(level, slot, pattern, wide, state, far, *rest):
    outs, (total, packed) = rest[:4], rest[4:]
    rank = state.shape[0]
    _, mid, low, core = digits()
    rows = state_rows(state)
    present = present_of(pattern, level, core, core)
    fold = LANES // slot
    for box in range(2):

        def emit(row, value):
            total[row] = far[box, row] + value

        multiply(wide.at[box], [row * present for row in rows] if box == 0 else rows, rank, emit)
        depth = rank // fold
        rows_of_piece = depth * total.shape[1]
        flat = total[...].reshape(fold, rows_of_piece, LANES).astype(jnp.bfloat16)
        pieces = swap_groups([flat[place] for place in range(fold)], slot)
        for place, piece in enumerate(pieces):
            packed[core ^ box, place] = piece
    for turn, out in enumerate(outs):
        first = ((mid ^ (turn // 2)) * 2 + (low ^ (turn % 2))) * 2
        for box in range(2):
            for last in range(2):
                out[box, last] = packed[box, first + last]


def wide_kernel(blocks, shared, own_wide, other_wide):
    rank = blocks.shape[1]
    core = digits()[3]
    for half in range(2):
        spread(own_wide.at[half], level_load(blocks, 0, half, core), rank, rank)
        spread(other_wide.at[half], shared_load(shared, 1, half), rank, rank)


def pair_box(wide, total, states, presents, out):
    for half in range(2):
        present = presents[half]
        rows = [states[half, index].astype(jnp.float32) for index in range(out.shape[0])]
        if present is not None:
            rows = [row * present for row in rows]

        def emit(row, value):
            if half == 0:
                total[row] = value
            else:
                out[row] = (total[row] + value).astype(jnp.bfloat16)

        multiply(wide.at[half], rows, out.shape[0], emit)


def open_kernel(slot, wide, kept, *rest):
    pieces, (out, states, total, packed) = rest[:4], rest[-4:]
    high, mid, low, core = digits()
    fold = LANES // slot
    depth = out.shape[0] // fold
    for turn, piece in enumerate(pieces):
        first = ((mid ^ (turn // 2)) * 2 + (low ^ (turn % 2))) * 2
        for box in range(2):
            for last in range(2):
                value = piece[box, last]
                if turn == 0:
                    value = jnp.where(high == core, kept[box, last], value)
                packed[last, first + box] = value
    for last in range(2):
        tile = swap_groups([packed[last, place] for place in range(fold)], slot)
        for place, rows in enumerate(tile):
            rows = rows.astype(jnp.float32).reshape(depth, states.shape[2], LANES)
            states[last, place * depth:(place + 1) * depth] = rows.astype(jnp.bfloat16)
    pair_box(wide, total, states, (None, None), out)


def own_kernel(pattern, wide, states, out, total):
    core = digits()[3]
    pair_box(wide, total, states, [present_of(pattern, 0, half, core) for half in range(2)], out)


def interp_kernel(interp, first_wide, second_wide):
    core = digits()[3]
    for wide, chunk in ((first_wide, core), (second_wide, 1 - core)):
        spread(wide, lambda row: interp[pl.ds(row, GROUP), :, lanes_of(chunk)], interp.shape[0], interp.shape[1])


def image_rows(level, bit, flip, pattern, wide, partner, near, total):
    places = digits()
    chunk, other = places[3] ^ flip, 1 - places[3 - bit]

    def emit(row, value):
        total[row] = (near[row] + value).astype(jnp.bfloat16).astype(jnp.float32)

    multiply(wide, state_rows(partner, present_of(pattern, level, other, chunk)), total.shape[0], emit)
    return [total[index] for index in range(total.shape[0])]


def first_image_kernel(level, bit, pattern, wide, image_wide, partner, near, out, total):
    rows = image_rows(level, bit, 0, pattern, wide, partner, near, total)

    def emit(row, value):
        out[row] = value.astype(jnp.bfloat16)

    multiply(image_wide, rows, out.shape[0], emit)


def last_kernel(level, bit, pattern, wide, image_wide, partner, near, ready, image, held, total, sems):
    core = digits()[3]
    copies = [pltpu.make_async_copy(ready, image.at[:, :, lanes_of(core)], sems.at[0])]
    copies[0].start()
    rows = image_rows(level, bit, 1, pattern, wide, partner, near, total)
    rank, parts = total.shape[0], sems.shape[0] - 1
    size = held.shape[0] // parts
    for part in range(parts):

        def emit(row, value):
            held[part * size + row] = value.astype(jnp.bfloat16)

        multiply(image_wide.at[pl.ds(part * size * rank, size * rank), :], rows, size, emit)
        span = pl.ds(part * size, size)
        copies.append(pltpu.make_async_copy(held.at[span], image.at[span, :, lanes_of(1 - core)], sems.at[part + 1]))
        copies[-1].start()
    for copy in copies:
        copy.wait()


def run(kernel, outs, operands, scratch=(), products=1, in_specs=None, out_specs=None, aliases=None, limit=KERNEL_LIMIT):
    whole = pl.BlockSpec(memory_space=pltpu.VMEM)
    single = not isinstance(outs, list)
    shapes = [outs] if single else outs
    result = pl.pallas_call(
        kernel,
        out_shape=shapes,
        in_specs=in_specs or [whole] * len(operands),
        out_specs=out_specs or [whole] * len(shapes),
        scratch_shapes=list(scratch),
        input_output_aliases=aliases or {},
        compiler_params=pltpu.CompilerParams(vmem_limit_bytes=limit),
        cost_estimate=pl.CostEstimate(flops=products * KERNEL_COST, bytes_accessed=products * KERNEL_COST, transcendentals=0),
    )(*operands)
    return result[0] if single else result


def permuted(value, target_of):
    pairs = [(source, target_of(source)) for source in range(lax.axis_size("leaf"))]
    pairs = [pair for pair in pairs if pair[0] != pair[1]]
    return lax.ppermute(value, "leaf", pairs)


def swapped(value, bit):
    return permuted(value, lambda source: source ^ 2**bit)


def crossed(source, turn):
    high, mid, low, core = source // 8 % 2, source // 4 % 2, source // 2 % 2, source % 2
    return ((core * 2 + (mid ^ (turn // 2))) * 2 + (low ^ (turn % 2))) * 2 + high


def fast_local(samples, interp_in, top_blocks, top_pattern, bottom_blocks, bottom_pattern, interp_out):
    rank, depth = interp_in.shape[:2]
    rhs_count, box_count = samples.shape[1:]
    out_depth = interp_out.shape[0]
    slot = box_count // lax.axis_size("leaf")
    fold = LANES // slot
    state = jax.ShapeDtypeStruct((rank, rhs_count, LANES), jnp.bfloat16)
    partial = jax.ShapeDtypeStruct((rank, rhs_count, LANES), jnp.float32)
    spread_out = jax.ShapeDtypeStruct((rank * rank, LANES), jnp.float32)
    pair_spread = jax.ShapeDtypeStruct((2, rank * rank, LANES), jnp.float32)
    total = pltpu.VMEM((rank, rhs_count, LANES), jnp.float32)
    wide = pltpu.VMEM((rank * rank, LANES), jnp.float32)
    packed = pltpu.VMEM((2, fold, rank // fold * rhs_count, LANES), jnp.bfloat16)

    def level_wides(blocks, level, bit, *after):
        wides = run(functools.partial(ahead_kernel, level, bit), [spread_out] * 4, (blocks, *after), products=4)
        return wides[:2], wides[2:]

    def level_nears(pattern, level, bit, order, wides, extra=()):
        return {
            flip: run(
                functools.partial(near_kernel, level, bit, flip), partial,
                (pattern, current[flip], wides[0][flip]) + ((current[1 - flip], *extra) if place < len(order) - 1 else ()),
            )
            for place, flip in enumerate(order)
        }

    def level_fars(pattern, level, bit, order, wides, extra=()):
        return {
            flip: run(
                functools.partial(far_kernel, level, bit, flip), state,
                (pattern, partner[flip], near[flip], wides[1][flip]) + (tuple(extra) if place == len(order) - 1 else ()),
            )
            for place, flip in enumerate(order)
        }

    coeff_scratch = (
        pltpu.VMEM((2, rank, depth // 2, LANES), jnp.bfloat16),
        pltpu.VMEM((2, depth // 2, rhs_count, LANES), jnp.bfloat16),
        pltpu.VMEM((rank * depth // 2, LANES), jnp.float32), total, pltpu.SemaphoreType.DMA((4,)),
    )
    share_rows = 2 * rank + rank * rhs_count // (2 * rank)
    shared_shape = jax.ShapeDtypeStruct((share_rows, 2 * rank, LANES), jnp.bfloat16)
    current = {1: run(
        functools.partial(coeff_kernel, 1), state, (interp_in, samples), coeff_scratch, 2,
        in_specs=[pl.BlockSpec(memory_space=pl.ANY)] * 2, limit=START_LIMIT,
    )}
    for level in range(3):
        bit = 3 - level
        if level == 0:
            partner = {1: swapped(current[1], bit)}
            current[0], *wides = run(
                functools.partial(second_kernel, 0, 3, 0), [state] + [spread_out] * 4,
                (top_blocks, interp_in, samples, current[1]),
                coeff_scratch + (pltpu.VMEM((1, *top_blocks.shape[1:]), jnp.bfloat16), pltpu.SemaphoreType.DMA), 4,
                in_specs=[pl.BlockSpec(memory_space=pl.ANY)] * 4, limit=FETCH_LIMIT,
            )
            wides = wides[:2], wides[2:]
            partner[0] = swapped(current[0], bit)
            near = level_nears(top_pattern, level, bit, (1,), wides)
            near.update(level_nears(top_pattern, level, bit, (0,), wides))
            later_wides = {later: level_wides(top_blocks, later, 3 - later, near[0]) for later in (1, 2)}
            shared = run(
                functools.partial(share_kernel, 3), shared_shape,
                (top_blocks, top_pattern, bottom_blocks, bottom_pattern),
            )
        else:
            partner = {flip: swapped(current[flip], bit) for flip in (1, 0)}
            wides = later_wides[level]
            near = level_nears(top_pattern, level, bit, (1, 0), wides)
        if level < 2:
            current = level_fars(top_pattern, level, bit, (1, 0), wides, later_wides[2][0] if level == 0 else ())

    shared = run(
        functools.partial(send_kernel, 2, 1, 1), shared_shape, (top_pattern, partner[1], near[1], wides[1][1], shared), aliases={4: 0},
    )
    shared = swapped(shared, 0)
    pair_far, near_wide = run(
        functools.partial(pair_far_kernel, 3),
        [jax.ShapeDtypeStruct((2, rank, rhs_count, LANES), jnp.float32), pair_spread],
        (top_blocks, top_pattern, shared), (wide,), 2,
    )
    current = level_fars(top_pattern, 2, 1, (0,), wides, (pair_far,))

    piece = jax.ShapeDtypeStruct((2, 2, rank // fold * rhs_count, LANES), jnp.bfloat16)
    pieces = run(
        functools.partial(pair_near_kernel, 3, slot), [piece] * 4,
        (top_pattern, near_wide, current[0], pair_far), (total, packed), 2,
    )
    kept = pieces[0]
    pieces = [permuted(value, functools.partial(crossed, turn=turn)) for turn, value in enumerate(pieces)]
    own_wide, other_wide = run(wide_kernel, [pair_spread] * 2, (bottom_blocks, shared))
    wides = {level: level_wides(bottom_blocks, level, level, kept) for level in (1, 2, 3)}
    image_spread = jax.ShapeDtypeStruct((out_depth * rank, LANES), jnp.float32)
    image_wide = run(interp_kernel, [image_spread] * 2, (interp_out,))
    spreads = [wide for level in (1, 2, 3) for group in wides[level] for wide in group]
    second, states = run(
        functools.partial(open_kernel, slot), [state, jax.ShapeDtypeStruct((2, rank, rhs_count, LANES), jnp.bfloat16)],
        (other_wide, kept, *pieces, *spreads, *image_wide), (total, packed), 2,
    )
    current = {1: swapped(second, 0), 0: run(own_kernel, state, (bottom_pattern, own_wide, states), (total,), 2)}
    partner = {0: swapped(current[0], 1)}
    partner[1] = swapped(current[1], 1)
    for level in (1, 2, 3):
        if level > 1:
            partner = {flip: swapped(current[flip], level) for flip in (0, 1)}
        near = level_nears(bottom_pattern, level, level, (0, 1), wides[level])
        if level < 3:
            current = level_fars(bottom_pattern, level, level, (0, 1), wides[level])

    ready = run(
        functools.partial(first_image_kernel, 3, 3), jax.ShapeDtypeStruct((out_depth, rhs_count, LANES), jnp.bfloat16),
        (bottom_pattern, wides[3][1][0], image_wide[0], partner[0], near[0]), (total,), 3,
    )
    return run(
        functools.partial(last_kernel, 3, 3), jax.ShapeDtypeStruct((out_depth, rhs_count, box_count), jnp.bfloat16),
        (bottom_pattern, wides[3][1][1], image_wide[1], partner[1], near[1], ready),
        (pltpu.VMEM((out_depth, rhs_count, LANES), jnp.bfloat16), total, pltpu.SemaphoreType.DMA((5,))), 3,
        out_specs=[pl.BlockSpec(memory_space=pl.ANY)],
    )


def contract(weights, state):
    product = weights[:, :, None].astype(jnp.float32) * state[None].astype(jnp.float32)
    return jnp.sum(product, axis=1)


def plain_level(current, blocks, pattern, bit):
    rank = blocks.shape[0]
    partner = swapped(current, bit)
    is_lower = lax.axis_index("leaf") // 2**bit % 2 == 0
    lower = jnp.where(is_lower, current, partner)
    upper = jnp.where(is_lower, partner, current)
    weights = blocks * jnp.repeat(pattern, rank, axis=0).astype(jnp.bfloat16)[None]
    return contract(weights, jnp.concatenate([lower, upper], axis=0)).astype(jnp.bfloat16)


def plain_local(samples, interp_in, top_blocks, top_pattern, bottom_blocks, bottom_pattern, interp_out):
    bit_count = lax.axis_size("leaf").bit_length() - 1
    current = contract(interp_in, samples).astype(jnp.bfloat16)
    for level in range(top_blocks.shape[0]):
        current = plain_level(current, top_blocks[level], top_pattern[level], bit_count - 1 - level)
    flat = current.reshape(-1, current.shape[2])
    current = lax.all_to_all(flat, "leaf", split_axis=1, concat_axis=1, tiled=True).reshape(current.shape)
    for level in range(bottom_blocks.shape[0]):
        current = plain_level(current, bottom_blocks[level], bottom_pattern[level], level)
    return contract(interp_out, current).astype(jnp.bfloat16)


def local(samples, interp_in, top_blocks, *rest):
    four_digits = lax.axis_size("leaf") == 16 and top_blocks.shape[0] == 4
    chosen = fast_local if four_digits and samples.shape[1:] == (8, 2 * LANES) else plain_local
    return chosen(samples, interp_in, top_blocks, *rest)


def solution(mesh):
    boxes = ("parts", "leaf")
    return jax.shard_map(
        local,
        mesh=mesh,
        in_specs=(
            P(None, None, boxes),
            P(None, None, boxes),
            P(None, None, None, boxes),
            P(None, None, boxes),
            P(None, None, None, boxes),
            P(None, None, boxes),
            P(None, None, boxes),
        ),
        out_specs=P(None, None, boxes),
        check_vma=False,
    )
```

```python
import functools

import jax
import jax.numpy as jnp
from jax import lax
from jax.experimental import pallas as pl
from jax.experimental.pallas import tpu as pltpu
from jax.sharding import PartitionSpec as P

LANES = 128
GROUP = 4
TURNS = (1, 3, 2, 0)
ROWS = 8
KERNEL_COST = 2**19
KERNEL_LIMIT = 16 * 2**20
FETCH_LIMIT = 53_850_000
START_LIMIT = 56_250_000


def digits():
    place = lax.axis_index("leaf")
    return lax.rem(place // 8, 2), lax.rem(place // 4, 2), lax.rem(place // 2, 2), lax.rem(place, 2)


def lanes_of(chunk):
    return pl.ds(pl.multiple_of(chunk * LANES, LANES), LANES)


def rows_of(half, rank):
    return pl.ds(pl.multiple_of(half * rank, rank), rank)


def spread(wide, load, row_count, rank):
    def body(step, carry):
        rows = load(step * GROUP).astype(jnp.float32)
        wide[pl.ds(step * GROUP * rank, GROUP * rank), :] = rows.reshape(GROUP * rank, LANES)
        return carry

    lax.fori_loop(0, row_count // GROUP, body, 0)


def multiply(wide, state, row_count, emit):
    rank = len(state)

    def body(step, carry):
        for inner in range(ROWS):
            sums = [None, None]
            for index in range(rank):
                weight = wide[pl.ds(step * ROWS * rank + inner * rank + index, 8, stride=0), :]
                term = weight * state[index]
                old = sums[index % 2]
                sums[index % 2] = term if old is None else old + term
            emit(step * ROWS + inner, sums[0] + sums[1])
        return carry

    lax.fori_loop(0, row_count // ROWS, body, 0)


def state_rows(ref, present=None):
    rows = [ref[index].astype(jnp.float32) for index in range(ref.shape[0])]
    return rows if present is None else [row * present for row in rows]


def level_load(blocks, level, half, chunk):
    rank = blocks.shape[1]
    return lambda row: blocks[level, pl.ds(row, GROUP), rows_of(half, rank), lanes_of(chunk)]


def present_of(pattern, level, half, chunk):
    pair = [pattern[level, place:place + 1, lanes_of(chunk)].astype(jnp.float32) for place in range(2)]
    return jnp.where(half == 0, pair[0], pair[1])


def coeff_kernel(flip, interp, samples, *rest):
    out, held_interp, held_samples, wide, total, sems = rest[-6:]
    rank, depth = interp.shape[0], interp.shape[1] // 2
    lanes = lanes_of(digits()[3] ^ flip)
    copies = []
    for half in range(2):
        part = pl.ds(half * depth, depth)
        copies.append(pltpu.make_async_copy(interp.at[:, part, lanes], held_interp.at[half], sems.at[half]))
        copies.append(pltpu.make_async_copy(samples.at[part, :, lanes], held_samples.at[half], sems.at[half + 2]))
    for copy in copies:
        copy.start()
    for half in range(2):
        copies[2 * half].wait()
        copies[2 * half + 1].wait()
        spread(wide, lambda row: held_interp[half, pl.ds(row, GROUP)], rank, depth)
        state = [held_samples[half, index].astype(jnp.float32) for index in range(depth)]

        def emit(row, value):
            if half == 0:
                total[row] = value
            else:
                out[row] = (total[row] + value).astype(jnp.bfloat16)

        multiply(wide, state, rank, emit)


def second_kernel(level, bit, flip, blocks, interp, samples, after, *rest):
    held, sem = rest[-2:]
    copy = pltpu.make_async_copy(blocks.at[pl.ds(level, 1)], held, sem)
    copy.start()
    coeff_kernel(flip, interp, samples, rest[0], *rest[5:-2])
    copy.wait()
    ahead_kernel(0, bit, held, *rest[1:5])


def ahead_kernel(level, bit, blocks, *rest):
    near_wides, far_wides = rest[-4:-2], rest[-2:]
    rank = blocks.shape[1]
    places = digits()
    own = places[3 - bit]
    for flip in range(2):
        chunk = places[3] ^ flip
        spread(near_wides[flip], level_load(blocks, level, own, chunk), rank, rank)
        spread(far_wides[flip], level_load(blocks, level, 1 - own, chunk), rank, rank)


def near_kernel(level, bit, flip, pattern, state, wide, *rest):
    out = rest[-1]
    places = digits()
    chunk, own = places[3] ^ flip, places[3 - bit]

    def emit(row, value):
        out[row] = value

    multiply(wide, state_rows(state, present_of(pattern, level, own, chunk)), out.shape[0], emit)


def far_kernel(level, bit, flip, pattern, partner, near, wide, *rest):
    out = rest[-1]
    places = digits()
    chunk, other = places[3] ^ flip, 1 - places[3 - bit]

    def emit(row, value):
        out[row] = (near[row] + value).astype(jnp.bfloat16)

    multiply(wide, state_rows(partner, present_of(pattern, level, other, chunk)), out.shape[0], emit)


def share_kernel(top_level, top_blocks, top_pattern, bottom_blocks, bottom_pattern, out):
    rank = top_blocks.shape[1]
    chunk = 1 - digits()[3]
    for place, (blocks, pattern, level) in enumerate(((top_blocks, top_pattern, top_level), (bottom_blocks, bottom_pattern, 0))):
        for half in range(2):
            present = present_of(pattern, level, half, chunk)[None]

            def body(step, carry):
                rows = blocks[level, pl.ds(step * 8, 8), half * rank:(half + 1) * rank, lanes_of(chunk)]
                span = pl.ds(place * rank + step * 8, 8)
                out[span, half * rank:(half + 1) * rank, :] = (rows.astype(jnp.float32) * present).astype(jnp.bfloat16)
                return carry

            lax.fori_loop(0, rank // 8, body, 0)


def shared_load(shared, place, half):
    rank = shared.shape[1] // 2
    return lambda row: shared[pl.ds(place * rank + row, GROUP), rows_of(half, rank), :]


def send_kernel(level, bit, flip, pattern, partner, near, wide, shared, *rest):
    out = rest[-1]
    rank, per = partner.shape[0], shared.shape[1] // partner.shape[1]
    places = digits()
    chunk, other = places[3] ^ flip, 1 - places[3 - bit]

    def emit(row, value):
        place = pl.ds(pl.multiple_of(lax.rem(row, per) * 8, 8), 8)
        out[2 * rank + row // per, place, :] = (near[row] + value).astype(jnp.bfloat16)

    multiply(wide, state_rows(partner, present_of(pattern, level, other, chunk)), rank, emit)


def sent_rows(shared):
    rank = shared.shape[1] // 2
    per = shared.shape[1] // 8
    return [
        shared[2 * rank + row // per, row % per * 8:(row % per + 1) * 8, :].astype(jnp.float32) for row in range(rank)
    ]


def swap_groups(tile, slot):
    axis = tile[0].ndim - 1
    lane_group = lax.broadcasted_iota(jnp.int32, tile[0].shape, axis) // slot
    step = 1
    while step < len(tile):
        low = (lane_group // step) % 2 == 0
        fresh = list(tile)
        for place in range(len(tile)):
            if place & step == 0:
                first, second = tile[place], tile[place + step]
                fresh[place] = jnp.where(low, first, pltpu.roll(second, step * slot, axis))
                fresh[place + step] = jnp.where(low, pltpu.roll(first, LANES - step * slot, axis), second)
        tile = fresh
        step *= 2
    return tile


def pair_far_kernel(level, blocks, pattern, shared, out, near_wide, wide):
    rank = blocks.shape[1]
    core = digits()[3]
    rows = sent_rows(shared)
    present = present_of(pattern, level, 1 - core, core)
    for box in range(2):
        for target, half in ((wide, 1 - core), (near_wide.at[box], core)):
            spread(target, level_load(blocks, level, half, core) if box == 0 else shared_load(shared, 0, half), rank, rank)

        def emit(row, value):
            out[box, row] = value

        multiply(wide, [row * present for row in rows] if box == 0 else rows, rank, emit)


def pair_near_kernel(level, slot, pattern, wide, state, far, *rest):
    outs, (total, packed) = rest[:4], rest[4:]
    rank = state.shape[0]
    _, mid, low, core = digits()
    rows = state_rows(state)
    present = present_of(pattern, level, core, core)
    fold = LANES // slot
    for box in range(2):

        def emit(row, value):
            total[row] = far[box, row] + value

        multiply(wide.at[box], [row * present for row in rows] if box == 0 else rows, rank, emit)
        depth = rank // fold
        rows_of_piece = depth * total.shape[1]
        flat = total[...].reshape(fold, rows_of_piece, LANES).astype(jnp.bfloat16)
        pieces = swap_groups([flat[place] for place in range(fold)], slot)
        for place, piece in enumerate(pieces):
            packed[core ^ box, place] = piece
    for turn, out in enumerate(outs):
        first = ((mid ^ (TURNS[turn] // 2)) * 2 + (low ^ (TURNS[turn] % 2))) * 2
        for box in range(2):
            for last in range(2):
                out[box, last] = packed[box, first + last]


def wide_kernel(blocks, shared, own_wide, other_wide):
    rank = blocks.shape[1]
    core = digits()[3]
    for half in range(2):
        spread(own_wide.at[half], level_load(blocks, 0, half, core), rank, rank)
        spread(other_wide.at[half], shared_load(shared, 1, half), rank, rank)


def pair_box(wide, total, states, presents, out):
    for half in range(2):
        present = presents[half]
        rows = [states[half, index].astype(jnp.float32) for index in range(out.shape[0])]
        if present is not None:
            rows = [row * present for row in rows]

        def emit(row, value):
            if half == 0:
                total[row] = value
            else:
                out[row] = (total[row] + value).astype(jnp.bfloat16)

        multiply(wide.at[half], rows, out.shape[0], emit)


def open_kernel(slot, wide, kept, *rest):
    pieces, (out, states, total, packed) = rest[:4], rest[-4:]
    high, mid, low, core = digits()
    fold = LANES // slot
    depth = out.shape[0] // fold
    for turn, piece in enumerate(pieces):
        first = ((mid ^ (TURNS[turn] // 2)) * 2 + (low ^ (TURNS[turn] % 2))) * 2
        for box in range(2):
            for last in range(2):
                value = piece[box, last]
                if TURNS[turn] == 0:
                    value = jnp.where(high == core, kept[box, last], value)
                packed[last, first + box] = value
    for last in range(2):
        tile = swap_groups([packed[last, place] for place in range(fold)], slot)
        for place, rows in enumerate(tile):
            rows = rows.astype(jnp.float32).reshape(depth, states.shape[2], LANES)
            states[last, place * depth:(place + 1) * depth] = rows.astype(jnp.bfloat16)
    pair_box(wide, total, states, (None, None), out)


def own_kernel(pattern, wide, states, out, total):
    core = digits()[3]
    pair_box(wide, total, states, [present_of(pattern, 0, half, core) for half in range(2)], out)


def interp_kernel(interp, first_wide, second_wide):
    core = digits()[3]
    for wide, chunk in ((first_wide, core), (second_wide, 1 - core)):
        spread(wide, lambda row: interp[pl.ds(row, GROUP), :, lanes_of(chunk)], interp.shape[0], interp.shape[1])


def image_rows(level, bit, flip, pattern, wide, partner, near, total):
    places = digits()
    chunk, other = places[3] ^ flip, 1 - places[3 - bit]

    def emit(row, value):
        total[row] = (near[row] + value).astype(jnp.bfloat16).astype(jnp.float32)

    multiply(wide, state_rows(partner, present_of(pattern, level, other, chunk)), total.shape[0], emit)
    return [total[index] for index in range(total.shape[0])]


def first_image_kernel(level, bit, pattern, wide, image_wide, partner, near, out, total):
    rows = image_rows(level, bit, 0, pattern, wide, partner, near, total)

    def emit(row, value):
        out[row] = value.astype(jnp.bfloat16)

    multiply(image_wide, rows, out.shape[0], emit)


def last_kernel(level, bit, pattern, wide, image_wide, partner, near, ready, image, held, total, sems):
    core = digits()[3]
    copies = [pltpu.make_async_copy(ready, image.at[:, :, lanes_of(core)], sems.at[0])]
    copies[0].start()
    rows = image_rows(level, bit, 1, pattern, wide, partner, near, total)
    rank, parts = total.shape[0], sems.shape[0] - 1
    size = held.shape[0] // parts
    for part in range(parts):

        def emit(row, value):
            held[part * size + row] = value.astype(jnp.bfloat16)

        multiply(image_wide.at[pl.ds(part * size * rank, size * rank), :], rows, size, emit)
        span = pl.ds(part * size, size)
        copies.append(pltpu.make_async_copy(held.at[span], image.at[span, :, lanes_of(1 - core)], sems.at[part + 1]))
        copies[-1].start()
    for copy in copies:
        copy.wait()


def run(kernel, outs, operands, scratch=(), products=1, in_specs=None, out_specs=None, aliases=None, limit=KERNEL_LIMIT):
    whole = pl.BlockSpec(memory_space=pltpu.VMEM)
    single = not isinstance(outs, list)
    shapes = [outs] if single else outs
    result = pl.pallas_call(
        kernel,
        out_shape=shapes,
        in_specs=in_specs or [whole] * len(operands),
        out_specs=out_specs or [whole] * len(shapes),
        scratch_shapes=list(scratch),
        input_output_aliases=aliases or {},
        compiler_params=pltpu.CompilerParams(vmem_limit_bytes=limit),
        cost_estimate=pl.CostEstimate(flops=products * KERNEL_COST, bytes_accessed=products * KERNEL_COST, transcendentals=0),
    )(*operands)
    return result[0] if single else result


def permuted(value, target_of):
    pairs = [(source, target_of(source)) for source in range(lax.axis_size("leaf"))]
    pairs = [pair for pair in pairs if pair[0] != pair[1]]
    return lax.ppermute(value, "leaf", pairs)


def swapped(value, bit):
    return permuted(value, lambda source: source ^ 2**bit)


def crossed(source, turn):
    high, mid, low, core = source // 8 % 2, source // 4 % 2, source // 2 % 2, source % 2
    return ((core * 2 + (mid ^ (TURNS[turn] // 2))) * 2 + (low ^ (TURNS[turn] % 2))) * 2 + high


def fast_local(samples, interp_in, top_blocks, top_pattern, bottom_blocks, bottom_pattern, interp_out):
    rank, depth = interp_in.shape[:2]
    rhs_count, box_count = samples.shape[1:]
    out_depth = interp_out.shape[0]
    slot = box_count // lax.axis_size("leaf")
    fold = LANES // slot
    state = jax.ShapeDtypeStruct((rank, rhs_count, LANES), jnp.bfloat16)
    partial = jax.ShapeDtypeStruct((rank, rhs_count, LANES), jnp.float32)
    spread_out = jax.ShapeDtypeStruct((rank * rank, LANES), jnp.float32)
    pair_spread = jax.ShapeDtypeStruct((2, rank * rank, LANES), jnp.float32)
    total = pltpu.VMEM((rank, rhs_count, LANES), jnp.float32)
    wide = pltpu.VMEM((rank * rank, LANES), jnp.float32)
    packed = pltpu.VMEM((2, fold, rank // fold * rhs_count, LANES), jnp.bfloat16)

    def level_wides(blocks, level, bit, *after):
        wides = run(functools.partial(ahead_kernel, level, bit), [spread_out] * 4, (blocks, *after), products=4)
        return wides[:2], wides[2:]

    def level_nears(pattern, level, bit, order, wides, extra=()):
        return {
            flip: run(
                functools.partial(near_kernel, level, bit, flip), partial,
                (pattern, current[flip], wides[0][flip]) + ((current[1 - flip], *extra) if place < len(order) - 1 else ()),
            )
            for place, flip in enumerate(order)
        }

    def level_fars(pattern, level, bit, order, wides, extra=()):
        return {
            flip: run(
                functools.partial(far_kernel, level, bit, flip), state,
                (pattern, partner[flip], near[flip], wides[1][flip]) + (tuple(extra) if place == len(order) - 1 else ()),
            )
            for place, flip in enumerate(order)
        }

    coeff_scratch = (
        pltpu.VMEM((2, rank, depth // 2, LANES), jnp.bfloat16),
        pltpu.VMEM((2, depth // 2, rhs_count, LANES), jnp.bfloat16),
        pltpu.VMEM((rank * depth // 2, LANES), jnp.float32), total, pltpu.SemaphoreType.DMA((4,)),
    )
    share_rows = 2 * rank + rank * rhs_count // (2 * rank)
    shared_shape = jax.ShapeDtypeStruct((share_rows, 2 * rank, LANES), jnp.bfloat16)
    current = {1: run(
        functools.partial(coeff_kernel, 1), state, (interp_in, samples), coeff_scratch, 2,
        in_specs=[pl.BlockSpec(memory_space=pl.ANY)] * 2, limit=START_LIMIT,
    )}
    for level in range(3):
        bit = 3 - level
        if level == 0:
            partner = {1: swapped(current[1], bit)}
            current[0], *wides = run(
                functools.partial(second_kernel, 0, 3, 0), [state] + [spread_out] * 4,
                (top_blocks, interp_in, samples, current[1]),
                coeff_scratch + (pltpu.VMEM((1, *top_blocks.shape[1:]), jnp.bfloat16), pltpu.SemaphoreType.DMA), 4,
                in_specs=[pl.BlockSpec(memory_space=pl.ANY)] * 4, limit=FETCH_LIMIT,
            )
            wides = wides[:2], wides[2:]
            partner[0] = swapped(current[0], bit)
            near = level_nears(top_pattern, level, bit, (1,), wides)
            near.update(level_nears(top_pattern, level, bit, (0,), wides))
            later_wides = {later: level_wides(top_blocks, later, 3 - later, near[0]) for later in (1, 2)}
            shared = run(
                functools.partial(share_kernel, 3), shared_shape,
                (top_blocks, top_pattern, bottom_blocks, bottom_pattern),
            )
        else:
            partner = {flip: swapped(current[flip], bit) for flip in (1, 0)}
            wides = later_wides[level]
            near = level_nears(top_pattern, level, bit, (1, 0), wides)
        if level < 2:
            current = level_fars(top_pattern, level, bit, (1, 0), wides, later_wides[2][0] if level == 0 else ())

    shared = run(
        functools.partial(send_kernel, 2, 1, 1), shared_shape, (top_pattern, partner[1], near[1], wides[1][1], shared), aliases={4: 0},
    )
    shared = swapped(shared, 0)
    pair_far, near_wide = run(
        functools.partial(pair_far_kernel, 3),
        [jax.ShapeDtypeStruct((2, rank, rhs_count, LANES), jnp.float32), pair_spread],
        (top_blocks, top_pattern, shared), (wide,), 2,
    )
    current = level_fars(top_pattern, 2, 1, (0,), wides, (pair_far,))

    piece = jax.ShapeDtypeStruct((2, 2, rank // fold * rhs_count, LANES), jnp.bfloat16)
    pieces = run(
        functools.partial(pair_near_kernel, 3, slot), [piece] * 4,
        (top_pattern, near_wide, current[0], pair_far), (total, packed), 2,
    )
    kept = pieces[TURNS.index(0)]
    pieces = [permuted(value, functools.partial(crossed, turn=turn)) for turn, value in enumerate(pieces)]
    own_wide, other_wide = run(wide_kernel, [pair_spread] * 2, (bottom_blocks, shared))
    wides = {level: level_wides(bottom_blocks, level, level, kept) for level in (1, 2, 3)}
    image_spread = jax.ShapeDtypeStruct((out_depth * rank, LANES), jnp.float32)
    image_wide = run(interp_kernel, [image_spread] * 2, (interp_out,))
    spreads = [wide for level in (1, 2, 3) for group in wides[level] for wide in group]
    second, states = run(
        functools.partial(open_kernel, slot), [state, jax.ShapeDtypeStruct((2, rank, rhs_count, LANES), jnp.bfloat16)],
        (other_wide, kept, *pieces, *spreads, *image_wide), (total, packed), 2,
    )
    current = {1: swapped(second, 0), 0: run(own_kernel, state, (bottom_pattern, own_wide, states), (total,), 2)}
    partner = {0: swapped(current[0], 1)}
    partner[1] = swapped(current[1], 1)
    for level in (1, 2, 3):
        if level > 1:
            partner = {flip: swapped(current[flip], level) for flip in (0, 1)}
        near = level_nears(bottom_pattern, level, level, (0, 1), wides[level])
        if level < 3:
            current = level_fars(bottom_pattern, level, level, (0, 1), wides[level])

    ready = run(
        functools.partial(first_image_kernel, 3, 3), jax.ShapeDtypeStruct((out_depth, rhs_count, LANES), jnp.bfloat16),
        (bottom_pattern, wides[3][1][0], image_wide[0], partner[0], near[0]), (total,), 3,
    )
    return run(
        functools.partial(last_kernel, 3, 3), jax.ShapeDtypeStruct((out_depth, rhs_count, box_count), jnp.bfloat16),
        (bottom_pattern, wides[3][1][1], image_wide[1], partner[1], near[1], ready),
        (pltpu.VMEM((out_depth, rhs_count, LANES), jnp.bfloat16), total, pltpu.SemaphoreType.DMA((5,))), 3,
        out_specs=[pl.BlockSpec(memory_space=pl.ANY)],
    )


def contract(weights, state):
    product = weights[:, :, None].astype(jnp.float32) * state[None].astype(jnp.float32)
    return jnp.sum(product, axis=1)


def plain_level(current, blocks, pattern, bit):
    rank = blocks.shape[0]
    partner = swapped(current, bit)
    is_lower = lax.axis_index("leaf") // 2**bit % 2 == 0
    lower = jnp.where(is_lower, current, partner)
    upper = jnp.where(is_lower, partner, current)
    weights = blocks * jnp.repeat(pattern, rank, axis=0).astype(jnp.bfloat16)[None]
    return contract(weights, jnp.concatenate([lower, upper], axis=0)).astype(jnp.bfloat16)


def plain_local(samples, interp_in, top_blocks, top_pattern, bottom_blocks, bottom_pattern, interp_out):
    bit_count = lax.axis_size("leaf").bit_length() - 1
    current = contract(interp_in, samples).astype(jnp.bfloat16)
    for level in range(top_blocks.shape[0]):
        current = plain_level(current, top_blocks[level], top_pattern[level], bit_count - 1 - level)
    flat = current.reshape(-1, current.shape[2])
    current = lax.all_to_all(flat, "leaf", split_axis=1, concat_axis=1, tiled=True).reshape(current.shape)
    for level in range(bottom_blocks.shape[0]):
        current = plain_level(current, bottom_blocks[level], bottom_pattern[level], level)
    return contract(interp_out, current).astype(jnp.bfloat16)


def local(samples, interp_in, top_blocks, *rest):
    four_digits = lax.axis_size("leaf") == 16 and top_blocks.shape[0] == 4
    chosen = fast_local if four_digits and samples.shape[1:] == (8, 2 * LANES) else plain_local
    return chosen(samples, interp_in, top_blocks, *rest)


def solution(mesh):
    boxes = ("parts", "leaf")
    return jax.shard_map(
        local,
        mesh=mesh,
        in_specs=(
            P(None, None, boxes),
            P(None, None, boxes),
            P(None, None, None, boxes),
            P(None, None, boxes),
            P(None, None, None, boxes),
            P(None, None, boxes),
            P(None, None, boxes),
        ),
        out_specs=P(None, None, boxes),
        check_vma=False,
    )
```

```python
import functools

import jax
import jax.numpy as jnp
from jax import lax
from jax.experimental import pallas as pl
from jax.experimental.pallas import tpu as pltpu
from jax.sharding import PartitionSpec as P

LANES = 128
GROUP = 4
ROWS = 16
KERNEL_COST = 2**19
KERNEL_LIMIT = 16 * 2**20
FETCH_LIMIT = 53_850_000
START_LIMIT = 56_250_000


def digits():
    place = lax.axis_index("leaf")
    return lax.rem(place // 8, 2), lax.rem(place // 4, 2), lax.rem(place // 2, 2), lax.rem(place, 2)


def lanes_of(chunk):
    return pl.ds(pl.multiple_of(chunk * LANES, LANES), LANES)


def rows_of(half, rank):
    return pl.ds(pl.multiple_of(half * rank, rank), rank)


def spread(wide, load, row_count, rank):
    def body(step, carry):
        rows = load(step * GROUP).astype(jnp.float32)
        wide[pl.ds(step * GROUP * rank, GROUP * rank), :] = rows.reshape(GROUP * rank, LANES)
        return carry

    lax.fori_loop(0, row_count // GROUP, body, 0)


def multiply(wide, state, row_count, emit):
    rank = len(state)

    def body(step, carry):
        for inner in range(ROWS):
            sums = [None, None]
            for index in range(rank):
                weight = wide[pl.ds(step * ROWS * rank + inner * rank + index, 8, stride=0), :]
                term = weight * state[index]
                old = sums[index % 2]
                sums[index % 2] = term if old is None else old + term
            emit(step * ROWS + inner, sums[0] + sums[1])
        return carry

    lax.fori_loop(0, row_count // ROWS, body, 0)


def state_rows(ref, present=None):
    rows = [ref[index].astype(jnp.float32) for index in range(ref.shape[0])]
    return rows if present is None else [row * present for row in rows]


def level_load(blocks, level, half, chunk):
    rank = blocks.shape[1]
    return lambda row: blocks[level, pl.ds(row, GROUP), rows_of(half, rank), lanes_of(chunk)]


def present_of(pattern, level, half, chunk):
    pair = [pattern[level, place:place + 1, lanes_of(chunk)].astype(jnp.float32) for place in range(2)]
    return jnp.where(half == 0, pair[0], pair[1])


def coeff_kernel(flip, interp, samples, *rest):
    out, held_interp, held_samples, wide, total, sems = rest[-6:]
    rank, depth = interp.shape[0], interp.shape[1] // 2
    lanes = lanes_of(digits()[3] ^ flip)
    copies = []
    for half in range(2):
        part = pl.ds(half * depth, depth)
        copies.append(pltpu.make_async_copy(interp.at[:, part, lanes], held_interp.at[half], sems.at[half]))
        copies.append(pltpu.make_async_copy(samples.at[part, :, lanes], held_samples.at[half], sems.at[half + 2]))
    for copy in copies:
        copy.start()
    for half in range(2):
        copies[2 * half].wait()
        copies[2 * half + 1].wait()
        spread(wide, lambda row: held_interp[half, pl.ds(row, GROUP)], rank, depth)
        state = [held_samples[half, index].astype(jnp.float32) for index in range(depth)]

        def emit(row, value):
            if half == 0:
                total[row] = value
            else:
                out[row] = (total[row] + value).astype(jnp.bfloat16)

        multiply(wide, state, rank, emit)


def second_kernel(level, bit, flip, blocks, interp, samples, after, *rest):
    held, sem = rest[-2:]
    copy = pltpu.make_async_copy(blocks.at[pl.ds(level, 1)], held, sem)
    copy.start()
    coeff_kernel(flip, interp, samples, rest[0], *rest[5:-2])
    copy.wait()
    ahead_kernel(0, bit, held, *rest[1:5])


def ahead_kernel(level, bit, blocks, *rest):
    near_wides, far_wides = rest[-4:-2], rest[-2:]
    rank = blocks.shape[1]
    places = digits()
    own = places[3 - bit]
    for flip in range(2):
        chunk = places[3] ^ flip
        spread(near_wides[flip], level_load(blocks, level, own, chunk), rank, rank)
        spread(far_wides[flip], level_load(blocks, level, 1 - own, chunk), rank, rank)


def near_kernel(level, bit, flip, pattern, state, wide, *rest):
    out = rest[-1]
    places = digits()
    chunk, own = places[3] ^ flip, places[3 - bit]

    def emit(row, value):
        out[row] = value

    multiply(wide, state_rows(state, present_of(pattern, level, own, chunk)), out.shape[0], emit)


def far_kernel(level, bit, flip, pattern, partner, near, wide, *rest):
    out = rest[-1]
    places = digits()
    chunk, other = places[3] ^ flip, 1 - places[3 - bit]

    def emit(row, value):
        out[row] = (near[row] + value).astype(jnp.bfloat16)

    multiply(wide, state_rows(partner, present_of(pattern, level, other, chunk)), out.shape[0], emit)


def share_kernel(top_level, top_blocks, top_pattern, bottom_blocks, bottom_pattern, out):
    rank = top_blocks.shape[1]
    chunk = 1 - digits()[3]
    for place, (blocks, pattern, level) in enumerate(((top_blocks, top_pattern, top_level), (bottom_blocks, bottom_pattern, 0))):
        for half in range(2):
            present = present_of(pattern, level, half, chunk)[None]

            def body(step, carry):
                rows = blocks[level, pl.ds(step * 8, 8), half * rank:(half + 1) * rank, lanes_of(chunk)]
                span = pl.ds(place * rank + step * 8, 8)
                out[span, half * rank:(half + 1) * rank, :] = (rows.astype(jnp.float32) * present).astype(jnp.bfloat16)
                return carry

            lax.fori_loop(0, rank // 8, body, 0)


def shared_load(shared, place, half):
    rank = shared.shape[1] // 2
    return lambda row: shared[pl.ds(place * rank + row, GROUP), rows_of(half, rank), :]


def send_kernel(level, bit, flip, pattern, partner, near, wide, shared, *rest):
    out = rest[-1]
    rank, per = partner.shape[0], shared.shape[1] // partner.shape[1]
    places = digits()
    chunk, other = places[3] ^ flip, 1 - places[3 - bit]

    def emit(row, value):
        place = pl.ds(pl.multiple_of(lax.rem(row, per) * 8, 8), 8)
        out[2 * rank + row // per, place, :] = (near[row] + value).astype(jnp.bfloat16)

    multiply(wide, state_rows(partner, present_of(pattern, level, other, chunk)), rank, emit)


def sent_rows(shared):
    rank = shared.shape[1] // 2
    per = shared.shape[1] // 8
    return [
        shared[2 * rank + row // per, row % per * 8:(row % per + 1) * 8, :].astype(jnp.float32) for row in range(rank)
    ]


def swap_groups(tile, slot):
    axis = tile[0].ndim - 1
    lane_group = lax.broadcasted_iota(jnp.int32, tile[0].shape, axis) // slot
    step = 1
    while step < len(tile):
        low = (lane_group // step) % 2 == 0
        fresh = list(tile)
        for place in range(len(tile)):
            if place & step == 0:
                first, second = tile[place], tile[place + step]
                fresh[place] = jnp.where(low, first, pltpu.roll(second, step * slot, axis))
                fresh[place + step] = jnp.where(low, pltpu.roll(first, LANES - step * slot, axis), second)
        tile = fresh
        step *= 2
    return tile


def pair_far_kernel(level, blocks, pattern, shared, out, near_wide, wide):
    rank = blocks.shape[1]
    core = digits()[3]
    rows = sent_rows(shared)
    present = present_of(pattern, level, 1 - core, core)
    for box in range(2):
        for target, half in ((wide, 1 - core), (near_wide.at[box], core)):
            spread(target, level_load(blocks, level, half, core) if box == 0 else shared_load(shared, 0, half), rank, rank)

        def emit(row, value):
            out[box, row] = value

        multiply(wide, [row * present for row in rows] if box == 0 else rows, rank, emit)


def pair_near_kernel(level, slot, pattern, wide, state, far, *rest):
    outs, (total, packed) = rest[:4], rest[4:]
    rank = state.shape[0]
    _, mid, low, core = digits()
    rows = state_rows(state)
    present = present_of(pattern, level, core, core)
    fold = LANES // slot
    for box in range(2):

        def emit(row, value):
            total[row] = far[box, row] + value

        multiply(wide.at[box], [row * present for row in rows] if box == 0 else rows, rank, emit)
        depth = rank // fold
        rows_of_piece = depth * total.shape[1]
        flat = total[...].reshape(fold, rows_of_piece, LANES).astype(jnp.bfloat16)
        pieces = swap_groups([flat[place] for place in range(fold)], slot)
        for place, piece in enumerate(pieces):
            packed[core ^ box, place] = piece
    for turn, out in enumerate(outs):
        first = ((mid ^ (turn // 2)) * 2 + (low ^ (turn % 2))) * 2
        for box in range(2):
            for last in range(2):
                out[box, last] = packed[box, first + last]


def wide_kernel(blocks, shared, own_wide, other_wide):
    rank = blocks.shape[1]
    core = digits()[3]
    for half in range(2):
        spread(own_wide.at[half], level_load(blocks, 0, half, core), rank, rank)
        spread(other_wide.at[half], shared_load(shared, 1, half), rank, rank)


def pair_box(wide, total, states, presents, out):
    for half in range(2):
        present = presents[half]
        rows = [states[half, index].astype(jnp.float32) for index in range(out.shape[0])]
        if present is not None:
            rows = [row * present for row in rows]

        def emit(row, value):
            if half == 0:
                total[row] = value
            else:
                out[row] = (total[row] + value).astype(jnp.bfloat16)

        multiply(wide.at[half], rows, out.shape[0], emit)


def open_kernel(slot, wide, kept, *rest):
    pieces, (out, states, total, packed) = rest[:4], rest[-4:]
    high, mid, low, core = digits()
    fold = LANES // slot
    depth = out.shape[0] // fold
    for turn, piece in enumerate(pieces):
        first = ((mid ^ (turn // 2)) * 2 + (low ^ (turn % 2))) * 2
        for box in range(2):
            for last in range(2):
                value = piece[box, last]
                if turn == 0:
                    value = jnp.where(high == core, kept[box, last], value)
                packed[last, first + box] = value
    for last in range(2):
        tile = swap_groups([packed[last, place] for place in range(fold)], slot)
        for place, rows in enumerate(tile):
            rows = rows.astype(jnp.float32).reshape(depth, states.shape[2], LANES)
            states[last, place * depth:(place + 1) * depth] = rows.astype(jnp.bfloat16)
    pair_box(wide, total, states, (None, None), out)


def own_kernel(pattern, wide, states, out, total):
    core = digits()[3]
    pair_box(wide, total, states, [present_of(pattern, 0, half, core) for half in range(2)], out)


def interp_kernel(interp, first_wide, second_wide):
    core = digits()[3]
    for wide, chunk in ((first_wide, core), (second_wide, 1 - core)):
        spread(wide, lambda row: interp[pl.ds(row, GROUP), :, lanes_of(chunk)], interp.shape[0], interp.shape[1])


def image_rows(level, bit, flip, pattern, wide, partner, near, total):
    places = digits()
    chunk, other = places[3] ^ flip, 1 - places[3 - bit]

    def emit(row, value):
        total[row] = (near[row] + value).astype(jnp.bfloat16).astype(jnp.float32)

    multiply(wide, state_rows(partner, present_of(pattern, level, other, chunk)), total.shape[0], emit)
    return [total[index] for index in range(total.shape[0])]


def first_image_kernel(level, bit, pattern, wide, image_wide, partner, near, out, total):
    rows = image_rows(level, bit, 0, pattern, wide, partner, near, total)

    def emit(row, value):
        out[row] = value.astype(jnp.bfloat16)

    multiply(image_wide, rows, out.shape[0], emit)


def last_kernel(level, bit, pattern, wide, image_wide, partner, near, ready, image, held, total, sems):
    core = digits()[3]
    copies = [pltpu.make_async_copy(ready, image.at[:, :, lanes_of(core)], sems.at[0])]
    copies[0].start()
    rows = image_rows(level, bit, 1, pattern, wide, partner, near, total)
    rank, parts = total.shape[0], sems.shape[0] - 1
    size = held.shape[0] // parts
    for part in range(parts):

        def emit(row, value):
            held[part * size + row] = value.astype(jnp.bfloat16)

        multiply(image_wide.at[pl.ds(part * size * rank, size * rank), :], rows, size, emit)
        span = pl.ds(part * size, size)
        copies.append(pltpu.make_async_copy(held.at[span], image.at[span, :, lanes_of(1 - core)], sems.at[part + 1]))
        copies[-1].start()
    for copy in copies:
        copy.wait()


def run(kernel, outs, operands, scratch=(), products=1, in_specs=None, out_specs=None, aliases=None, limit=KERNEL_LIMIT):
    whole = pl.BlockSpec(memory_space=pltpu.VMEM)
    single = not isinstance(outs, list)
    shapes = [outs] if single else outs
    result = pl.pallas_call(
        kernel,
        out_shape=shapes,
        in_specs=in_specs or [whole] * len(operands),
        out_specs=out_specs or [whole] * len(shapes),
        scratch_shapes=list(scratch),
        input_output_aliases=aliases or {},
        compiler_params=pltpu.CompilerParams(vmem_limit_bytes=limit),
        cost_estimate=pl.CostEstimate(flops=products * KERNEL_COST, bytes_accessed=products * KERNEL_COST, transcendentals=0),
    )(*operands)
    return result[0] if single else result


def permuted(value, target_of):
    pairs = [(source, target_of(source)) for source in range(lax.axis_size("leaf"))]
    pairs = [pair for pair in pairs if pair[0] != pair[1]]
    return lax.ppermute(value, "leaf", pairs)


def swapped(value, bit):
    return permuted(value, lambda source: source ^ 2**bit)


def crossed(source, turn):
    high, mid, low, core = source // 8 % 2, source // 4 % 2, source // 2 % 2, source % 2
    return ((core * 2 + (mid ^ (turn // 2))) * 2 + (low ^ (turn % 2))) * 2 + high


def fast_local(samples, interp_in, top_blocks, top_pattern, bottom_blocks, bottom_pattern, interp_out):
    rank, depth = interp_in.shape[:2]
    rhs_count, box_count = samples.shape[1:]
    out_depth = interp_out.shape[0]
    slot = box_count // lax.axis_size("leaf")
    fold = LANES // slot
    state = jax.ShapeDtypeStruct((rank, rhs_count, LANES), jnp.bfloat16)
    partial = jax.ShapeDtypeStruct((rank, rhs_count, LANES), jnp.float32)
    spread_out = jax.ShapeDtypeStruct((rank * rank, LANES), jnp.float32)
    pair_spread = jax.ShapeDtypeStruct((2, rank * rank, LANES), jnp.float32)
    total = pltpu.VMEM((rank, rhs_count, LANES), jnp.float32)
    wide = pltpu.VMEM((rank * rank, LANES), jnp.float32)
    packed = pltpu.VMEM((2, fold, rank // fold * rhs_count, LANES), jnp.bfloat16)

    def level_wides(blocks, level, bit, *after):
        wides = run(functools.partial(ahead_kernel, level, bit), [spread_out] * 4, (blocks, *after), products=4)
        return wides[:2], wides[2:]

    def level_nears(pattern, level, bit, order, wides, extra=()):
        return {
            flip: run(
                functools.partial(near_kernel, level, bit, flip), partial,
                (pattern, current[flip], wides[0][flip]) + ((current[1 - flip], *extra) if place < len(order) - 1 else ()),
            )
            for place, flip in enumerate(order)
        }

    def level_fars(pattern, level, bit, order, wides, extra=()):
        return {
            flip: run(
                functools.partial(far_kernel, level, bit, flip), state,
                (pattern, partner[flip], near[flip], wides[1][flip]) + (tuple(extra) if place == len(order) - 1 else ()),
            )
            for place, flip in enumerate(order)
        }

    coeff_scratch = (
        pltpu.VMEM((2, rank, depth // 2, LANES), jnp.bfloat16),
        pltpu.VMEM((2, depth // 2, rhs_count, LANES), jnp.bfloat16),
        pltpu.VMEM((rank * depth // 2, LANES), jnp.float32), total, pltpu.SemaphoreType.DMA((4,)),
    )
    share_rows = 2 * rank + rank * rhs_count // (2 * rank)
    shared_shape = jax.ShapeDtypeStruct((share_rows, 2 * rank, LANES), jnp.bfloat16)
    current = {1: run(
        functools.partial(coeff_kernel, 1), state, (interp_in, samples), coeff_scratch, 2,
        in_specs=[pl.BlockSpec(memory_space=pl.ANY)] * 2, limit=START_LIMIT,
    )}
    for level in range(3):
        bit = 3 - level
        if level == 0:
            partner = {1: swapped(current[1], bit)}
            current[0], *wides = run(
                functools.partial(second_kernel, 0, 3, 0), [state] + [spread_out] * 4,
                (top_blocks, interp_in, samples, current[1]),
                coeff_scratch + (pltpu.VMEM((1, *top_blocks.shape[1:]), jnp.bfloat16), pltpu.SemaphoreType.DMA), 4,
                in_specs=[pl.BlockSpec(memory_space=pl.ANY)] * 4, limit=FETCH_LIMIT,
            )
            wides = wides[:2], wides[2:]
            partner[0] = swapped(current[0], bit)
            near = level_nears(top_pattern, level, bit, (1,), wides)
            near.update(level_nears(top_pattern, level, bit, (0,), wides))
            later_wides = {later: level_wides(top_blocks, later, 3 - later, near[0]) for later in (1, 2)}
            shared = run(
                functools.partial(share_kernel, 3), shared_shape,
                (top_blocks, top_pattern, bottom_blocks, bottom_pattern),
            )
        else:
            partner = {flip: swapped(current[flip], bit) for flip in (1, 0)}
            wides = later_wides[level]
            near = level_nears(top_pattern, level, bit, (1, 0), wides)
        if level < 2:
            current = level_fars(top_pattern, level, bit, (1, 0), wides, later_wides[2][0] if level == 0 else ())

    shared = run(
        functools.partial(send_kernel, 2, 1, 1), shared_shape, (top_pattern, partner[1], near[1], wides[1][1], shared), aliases={4: 0},
    )
    shared = swapped(shared, 0)
    pair_far, near_wide = run(
        functools.partial(pair_far_kernel, 3),
        [jax.ShapeDtypeStruct((2, rank, rhs_count, LANES), jnp.float32), pair_spread],
        (top_blocks, top_pattern, shared), (wide,), 2,
    )
    current = level_fars(top_pattern, 2, 1, (0,), wides, (pair_far,))

    piece = jax.ShapeDtypeStruct((2, 2, rank // fold * rhs_count, LANES), jnp.bfloat16)
    pieces = run(
        functools.partial(pair_near_kernel, 3, slot), [piece] * 4,
        (top_pattern, near_wide, current[0], pair_far), (total, packed), 2,
    )
    kept = pieces[0]
    pieces = [permuted(value, functools.partial(crossed, turn=turn)) for turn, value in enumerate(pieces)]
    own_wide, other_wide = run(wide_kernel, [pair_spread] * 2, (bottom_blocks, shared))
    wides = {level: level_wides(bottom_blocks, level, level, kept) for level in (1, 2, 3)}
    image_spread = jax.ShapeDtypeStruct((out_depth * rank, LANES), jnp.float32)
    image_wide = run(interp_kernel, [image_spread] * 2, (interp_out,))
    spreads = [wide for level in (1, 2, 3) for group in wides[level] for wide in group]
    second, states = run(
        functools.partial(open_kernel, slot), [state, jax.ShapeDtypeStruct((2, rank, rhs_count, LANES), jnp.bfloat16)],
        (other_wide, kept, *pieces, *spreads, *image_wide), (total, packed), 2,
    )
    current = {1: swapped(second, 0), 0: run(own_kernel, state, (bottom_pattern, own_wide, states), (total,), 2)}
    partner = {0: swapped(current[0], 1)}
    partner[1] = swapped(current[1], 1)
    for level in (1, 2, 3):
        if level > 1:
            partner = {flip: swapped(current[flip], level) for flip in (0, 1)}
        near = level_nears(bottom_pattern, level, level, (0, 1), wides[level])
        if level < 3:
            current = level_fars(bottom_pattern, level, level, (0, 1), wides[level])

    ready = run(
        functools.partial(first_image_kernel, 3, 3), jax.ShapeDtypeStruct((out_depth, rhs_count, LANES), jnp.bfloat16),
        (bottom_pattern, wides[3][1][0], image_wide[0], partner[0], near[0]), (total,), 3,
    )
    return run(
        functools.partial(last_kernel, 3, 3), jax.ShapeDtypeStruct((out_depth, rhs_count, box_count), jnp.bfloat16),
        (bottom_pattern, wides[3][1][1], image_wide[1], partner[1], near[1], ready),
        (pltpu.VMEM((out_depth, rhs_count, LANES), jnp.bfloat16), total, pltpu.SemaphoreType.DMA((5,))), 3,
        out_specs=[pl.BlockSpec(memory_space=pl.ANY)],
    )


def contract(weights, state):
    product = weights[:, :, None].astype(jnp.float32) * state[None].astype(jnp.float32)
    return jnp.sum(product, axis=1)


def plain_level(current, blocks, pattern, bit):
    rank = blocks.shape[0]
    partner = swapped(current, bit)
    is_lower = lax.axis_index("leaf") // 2**bit % 2 == 0
    lower = jnp.where(is_lower, current, partner)
    upper = jnp.where(is_lower, partner, current)
    weights = blocks * jnp.repeat(pattern, rank, axis=0).astype(jnp.bfloat16)[None]
    return contract(weights, jnp.concatenate([lower, upper], axis=0)).astype(jnp.bfloat16)


def plain_local(samples, interp_in, top_blocks, top_pattern, bottom_blocks, bottom_pattern, interp_out):
    bit_count = lax.axis_size("leaf").bit_length() - 1
    current = contract(interp_in, samples).astype(jnp.bfloat16)
    for level in range(top_blocks.shape[0]):
        current = plain_level(current, top_blocks[level], top_pattern[level], bit_count - 1 - level)
    flat = current.reshape(-1, current.shape[2])
    current = lax.all_to_all(flat, "leaf", split_axis=1, concat_axis=1, tiled=True).reshape(current.shape)
    for level in range(bottom_blocks.shape[0]):
        current = plain_level(current, bottom_blocks[level], bottom_pattern[level], level)
    return contract(interp_out, current).astype(jnp.bfloat16)


def local(samples, interp_in, top_blocks, *rest):
    four_digits = lax.axis_size("leaf") == 16 and top_blocks.shape[0] == 4
    chosen = fast_local if four_digits and samples.shape[1:] == (8, 2 * LANES) else plain_local
    return chosen(samples, interp_in, top_blocks, *rest)


def solution(mesh):
    boxes = ("parts", "leaf")
    return jax.shard_map(
        local,
        mesh=mesh,
        in_specs=(
            P(None, None, boxes),
            P(None, None, boxes),
            P(None, None, None, boxes),
            P(None, None, boxes),
            P(None, None, None, boxes),
            P(None, None, boxes),
            P(None, None, boxes),
        ),
        out_specs=P(None, None, boxes),
        check_vma=False,
    )
```

```python
import functools

import jax
import jax.numpy as jnp
from jax import lax
from jax.experimental import pallas as pl
from jax.experimental.pallas import tpu as pltpu
from jax.sharding import PartitionSpec as P

LANES = 128
GROUP = 4
ROWS = 32
KERNEL_COST = 2**19
KERNEL_LIMIT = 16 * 2**20
FETCH_LIMIT = 53_850_000
START_LIMIT = 56_250_000


def digits():
    place = lax.axis_index("leaf")
    return lax.rem(place // 8, 2), lax.rem(place // 4, 2), lax.rem(place // 2, 2), lax.rem(place, 2)


def lanes_of(chunk):
    return pl.ds(pl.multiple_of(chunk * LANES, LANES), LANES)


def rows_of(half, rank):
    return pl.ds(pl.multiple_of(half * rank, rank), rank)


def spread(wide, load, row_count, rank):
    def body(step, carry):
        rows = load(step * GROUP).astype(jnp.float32)
        wide[pl.ds(step * GROUP * rank, GROUP * rank), :] = rows.reshape(GROUP * rank, LANES)
        return carry

    lax.fori_loop(0, row_count // GROUP, body, 0)


def multiply(wide, state, row_count, emit):
    rank, rows = len(state), min(ROWS, row_count)

    def body(step, carry):
        for inner in range(rows):
            sums = [None, None]
            for index in range(rank):
                weight = wide[pl.ds(step * rows * rank + inner * rank + index, 8, stride=0), :]
                term = weight * state[index]
                old = sums[index % 2]
                sums[index % 2] = term if old is None else old + term
            emit(step * rows + inner, sums[0] + sums[1])
        return carry

    lax.fori_loop(0, row_count // rows, body, 0)


def state_rows(ref, present=None):
    rows = [ref[index].astype(jnp.float32) for index in range(ref.shape[0])]
    return rows if present is None else [row * present for row in rows]


def level_load(blocks, level, half, chunk):
    rank = blocks.shape[1]
    return lambda row: blocks[level, pl.ds(row, GROUP), rows_of(half, rank), lanes_of(chunk)]


def present_of(pattern, level, half, chunk):
    pair = [pattern[level, place:place + 1, lanes_of(chunk)].astype(jnp.float32) for place in range(2)]
    return jnp.where(half == 0, pair[0], pair[1])


def coeff_kernel(flip, interp, samples, *rest):
    out, held_interp, held_samples, wide, total, sems = rest[-6:]
    rank, depth = interp.shape[0], interp.shape[1] // 2
    lanes = lanes_of(digits()[3] ^ flip)
    copies = []
    for half in range(2):
        part = pl.ds(half * depth, depth)
        copies.append(pltpu.make_async_copy(interp.at[:, part, lanes], held_interp.at[half], sems.at[half]))
        copies.append(pltpu.make_async_copy(samples.at[part, :, lanes], held_samples.at[half], sems.at[half + 2]))
    for copy in copies:
        copy.start()
    for half in range(2):
        copies[2 * half].wait()
        copies[2 * half + 1].wait()
        spread(wide, lambda row: held_interp[half, pl.ds(row, GROUP)], rank, depth)
        state = [held_samples[half, index].astype(jnp.float32) for index in range(depth)]

        def emit(row, value):
            if half == 0:
                total[row] = value
            else:
                out[row] = (total[row] + value).astype(jnp.bfloat16)

        multiply(wide, state, rank, emit)


def second_kernel(level, bit, flip, blocks, interp, samples, after, *rest):
    held, sem = rest[-2:]
    copy = pltpu.make_async_copy(blocks.at[pl.ds(level, 1)], held, sem)
    copy.start()
    coeff_kernel(flip, interp, samples, rest[0], *rest[5:-2])
    copy.wait()
    ahead_kernel(0, bit, held, *rest[1:5])


def ahead_kernel(level, bit, blocks, *rest):
    near_wides, far_wides = rest[-4:-2], rest[-2:]
    rank = blocks.shape[1]
    places = digits()
    own = places[3 - bit]
    for flip in range(2):
        chunk = places[3] ^ flip
        spread(near_wides[flip], level_load(blocks, level, own, chunk), rank, rank)
        spread(far_wides[flip], level_load(blocks, level, 1 - own, chunk), rank, rank)


def near_kernel(level, bit, flip, pattern, state, wide, *rest):
    out = rest[-1]
    places = digits()
    chunk, own = places[3] ^ flip, places[3 - bit]

    def emit(row, value):
        out[row] = value

    multiply(wide, state_rows(state, present_of(pattern, level, own, chunk)), out.shape[0], emit)


def far_kernel(level, bit, flip, pattern, partner, near, wide, *rest):
    out = rest[-1]
    places = digits()
    chunk, other = places[3] ^ flip, 1 - places[3 - bit]

    def emit(row, value):
        out[row] = (near[row] + value).astype(jnp.bfloat16)

    multiply(wide, state_rows(partner, present_of(pattern, level, other, chunk)), out.shape[0], emit)


def share_kernel(top_level, top_blocks, top_pattern, bottom_blocks, bottom_pattern, out):
    rank = top_blocks.shape[1]
    chunk = 1 - digits()[3]
    for place, (blocks, pattern, level) in enumerate(((top_blocks, top_pattern, top_level), (bottom_blocks, bottom_pattern, 0))):
        for half in range(2):
            present = present_of(pattern, level, half, chunk)[None]

            def body(step, carry):
                rows = blocks[level, pl.ds(step * 8, 8), half * rank:(half + 1) * rank, lanes_of(chunk)]
                span = pl.ds(place * rank + step * 8, 8)
                out[span, half * rank:(half + 1) * rank, :] = (rows.astype(jnp.float32) * present).astype(jnp.bfloat16)
                return carry

            lax.fori_loop(0, rank // 8, body, 0)


def shared_load(shared, place, half):
    rank = shared.shape[1] // 2
    return lambda row: shared[pl.ds(place * rank + row, GROUP), rows_of(half, rank), :]


def send_kernel(level, bit, flip, pattern, partner, near, wide, shared, *rest):
    out = rest[-1]
    rank, per = partner.shape[0], shared.shape[1] // partner.shape[1]
    places = digits()
    chunk, other = places[3] ^ flip, 1 - places[3 - bit]

    def emit(row, value):
        place = pl.ds(pl.multiple_of(lax.rem(row, per) * 8, 8), 8)
        out[2 * rank + row // per, place, :] = (near[row] + value).astype(jnp.bfloat16)

    multiply(wide, state_rows(partner, present_of(pattern, level, other, chunk)), rank, emit)


def sent_rows(shared):
    rank = shared.shape[1] // 2
    per = shared.shape[1] // 8
    return [
        shared[2 * rank + row // per, row % per * 8:(row % per + 1) * 8, :].astype(jnp.float32) for row in range(rank)
    ]


def swap_groups(tile, slot):
    axis = tile[0].ndim - 1
    lane_group = lax.broadcasted_iota(jnp.int32, tile[0].shape, axis) // slot
    step = 1
    while step < len(tile):
        low = (lane_group // step) % 2 == 0
        fresh = list(tile)
        for place in range(len(tile)):
            if place & step == 0:
                first, second = tile[place], tile[place + step]
                fresh[place] = jnp.where(low, first, pltpu.roll(second, step * slot, axis))
                fresh[place + step] = jnp.where(low, pltpu.roll(first, LANES - step * slot, axis), second)
        tile = fresh
        step *= 2
    return tile


def pair_far_kernel(level, blocks, pattern, shared, out, near_wide, wide):
    rank = blocks.shape[1]
    core = digits()[3]
    rows = sent_rows(shared)
    present = present_of(pattern, level, 1 - core, core)
    for box in range(2):
        for target, half in ((wide, 1 - core), (near_wide.at[box], core)):
            spread(target, level_load(blocks, level, half, core) if box == 0 else shared_load(shared, 0, half), rank, rank)

        def emit(row, value):
            out[box, row] = value

        multiply(wide, [row * present for row in rows] if box == 0 else rows, rank, emit)


def pair_near_kernel(level, slot, pattern, wide, state, far, *rest):
    outs, (total, packed) = rest[:4], rest[4:]
    rank = state.shape[0]
    _, mid, low, core = digits()
    rows = state_rows(state)
    present = present_of(pattern, level, core, core)
    fold = LANES // slot
    for box in range(2):

        def emit(row, value):
            total[row] = far[box, row] + value

        multiply(wide.at[box], [row * present for row in rows] if box == 0 else rows, rank, emit)
        depth = rank // fold
        rows_of_piece = depth * total.shape[1]
        flat = total[...].reshape(fold, rows_of_piece, LANES).astype(jnp.bfloat16)
        pieces = swap_groups([flat[place] for place in range(fold)], slot)
        for place, piece in enumerate(pieces):
            packed[core ^ box, place] = piece
    for turn, out in enumerate(outs):
        first = ((mid ^ (turn // 2)) * 2 + (low ^ (turn % 2))) * 2
        for box in range(2):
            for last in range(2):
                out[box, last] = packed[box, first + last]


def wide_kernel(blocks, shared, own_wide, other_wide):
    rank = blocks.shape[1]
    core = digits()[3]
    for half in range(2):
        spread(own_wide.at[half], level_load(blocks, 0, half, core), rank, rank)
        spread(other_wide.at[half], shared_load(shared, 1, half), rank, rank)


def pair_box(wide, total, states, presents, out):
    for half in range(2):
        present = presents[half]
        rows = [states[half, index].astype(jnp.float32) for index in range(out.shape[0])]
        if present is not None:
            rows = [row * present for row in rows]

        def emit(row, value):
            if half == 0:
                total[row] = value
            else:
                out[row] = (total[row] + value).astype(jnp.bfloat16)

        multiply(wide.at[half], rows, out.shape[0], emit)


def open_kernel(slot, wide, kept, *rest):
    pieces, (out, states, total, packed) = rest[:4], rest[-4:]
    high, mid, low, core = digits()
    fold = LANES // slot
    depth = out.shape[0] // fold
    for turn, piece in enumerate(pieces):
        first = ((mid ^ (turn // 2)) * 2 + (low ^ (turn % 2))) * 2
        for box in range(2):
            for last in range(2):
                value = piece[box, last]
                if turn == 0:
                    value = jnp.where(high == core, kept[box, last], value)
                packed[last, first + box] = value
    for last in range(2):
        tile = swap_groups([packed[last, place] for place in range(fold)], slot)
        for place, rows in enumerate(tile):
            rows = rows.astype(jnp.float32).reshape(depth, states.shape[2], LANES)
            states[last, place * depth:(place + 1) * depth] = rows.astype(jnp.bfloat16)
    pair_box(wide, total, states, (None, None), out)


def own_kernel(pattern, wide, states, out, total):
    core = digits()[3]
    pair_box(wide, total, states, [present_of(pattern, 0, half, core) for half in range(2)], out)


def interp_kernel(interp, first_wide, second_wide):
    core = digits()[3]
    for wide, chunk in ((first_wide, core), (second_wide, 1 - core)):
        spread(wide, lambda row: interp[pl.ds(row, GROUP), :, lanes_of(chunk)], interp.shape[0], interp.shape[1])


def image_rows(level, bit, flip, pattern, wide, partner, near, total):
    places = digits()
    chunk, other = places[3] ^ flip, 1 - places[3 - bit]

    def emit(row, value):
        total[row] = (near[row] + value).astype(jnp.bfloat16).astype(jnp.float32)

    multiply(wide, state_rows(partner, present_of(pattern, level, other, chunk)), total.shape[0], emit)
    return [total[index] for index in range(total.shape[0])]


def first_image_kernel(level, bit, pattern, wide, image_wide, partner, near, out, total):
    rows = image_rows(level, bit, 0, pattern, wide, partner, near, total)

    def emit(row, value):
        out[row] = value.astype(jnp.bfloat16)

    multiply(image_wide, rows, out.shape[0], emit)


def last_kernel(level, bit, pattern, wide, image_wide, partner, near, ready, image, held, total, sems):
    core = digits()[3]
    copies = [pltpu.make_async_copy(ready, image.at[:, :, lanes_of(core)], sems.at[0])]
    copies[0].start()
    rows = image_rows(level, bit, 1, pattern, wide, partner, near, total)
    rank, parts = total.shape[0], sems.shape[0] - 1
    size = held.shape[0] // parts
    for part in range(parts):

        def emit(row, value):
            held[part * size + row] = value.astype(jnp.bfloat16)

        multiply(image_wide.at[pl.ds(part * size * rank, size * rank), :], rows, size, emit)
        span = pl.ds(part * size, size)
        copies.append(pltpu.make_async_copy(held.at[span], image.at[span, :, lanes_of(1 - core)], sems.at[part + 1]))
        copies[-1].start()
    for copy in copies:
        copy.wait()


def run(kernel, outs, operands, scratch=(), products=1, in_specs=None, out_specs=None, aliases=None, limit=KERNEL_LIMIT):
    whole = pl.BlockSpec(memory_space=pltpu.VMEM)
    single = not isinstance(outs, list)
    shapes = [outs] if single else outs
    result = pl.pallas_call(
        kernel,
        out_shape=shapes,
        in_specs=in_specs or [whole] * len(operands),
        out_specs=out_specs or [whole] * len(shapes),
        scratch_shapes=list(scratch),
        input_output_aliases=aliases or {},
        compiler_params=pltpu.CompilerParams(vmem_limit_bytes=limit),
        cost_estimate=pl.CostEstimate(flops=products * KERNEL_COST, bytes_accessed=products * KERNEL_COST, transcendentals=0),
    )(*operands)
    return result[0] if single else result


def permuted(value, target_of):
    pairs = [(source, target_of(source)) for source in range(lax.axis_size("leaf"))]
    pairs = [pair for pair in pairs if pair[0] != pair[1]]
    return lax.ppermute(value, "leaf", pairs)


def swapped(value, bit):
    return permuted(value, lambda source: source ^ 2**bit)


def crossed(source, turn):
    high, mid, low, core = source // 8 % 2, source // 4 % 2, source // 2 % 2, source % 2
    return ((core * 2 + (mid ^ (turn // 2))) * 2 + (low ^ (turn % 2))) * 2 + high


def fast_local(samples, interp_in, top_blocks, top_pattern, bottom_blocks, bottom_pattern, interp_out):
    rank, depth = interp_in.shape[:2]
    rhs_count, box_count = samples.shape[1:]
    out_depth = interp_out.shape[0]
    slot = box_count // lax.axis_size("leaf")
    fold = LANES // slot
    state = jax.ShapeDtypeStruct((rank, rhs_count, LANES), jnp.bfloat16)
    partial = jax.ShapeDtypeStruct((rank, rhs_count, LANES), jnp.float32)
    spread_out = jax.ShapeDtypeStruct((rank * rank, LANES), jnp.float32)
    pair_spread = jax.ShapeDtypeStruct((2, rank * rank, LANES), jnp.float32)
    total = pltpu.VMEM((rank, rhs_count, LANES), jnp.float32)
    wide = pltpu.VMEM((rank * rank, LANES), jnp.float32)
    packed = pltpu.VMEM((2, fold, rank // fold * rhs_count, LANES), jnp.bfloat16)

    def level_wides(blocks, level, bit, *after):
        wides = run(functools.partial(ahead_kernel, level, bit), [spread_out] * 4, (blocks, *after), products=4)
        return wides[:2], wides[2:]

    def level_nears(pattern, level, bit, order, wides, extra=()):
        return {
            flip: run(
                functools.partial(near_kernel, level, bit, flip), partial,
                (pattern, current[flip], wides[0][flip]) + ((current[1 - flip], *extra) if place < len(order) - 1 else ()),
            )
            for place, flip in enumerate(order)
        }

    def level_fars(pattern, level, bit, order, wides, extra=()):
        return {
            flip: run(
                functools.partial(far_kernel, level, bit, flip), state,
                (pattern, partner[flip], near[flip], wides[1][flip]) + (tuple(extra) if place == len(order) - 1 else ()),
            )
            for place, flip in enumerate(order)
        }

    coeff_scratch = (
        pltpu.VMEM((2, rank, depth // 2, LANES), jnp.bfloat16),
        pltpu.VMEM((2, depth // 2, rhs_count, LANES), jnp.bfloat16),
        pltpu.VMEM((rank * depth // 2, LANES), jnp.float32), total, pltpu.SemaphoreType.DMA((4,)),
    )
    share_rows = 2 * rank + rank * rhs_count // (2 * rank)
    shared_shape = jax.ShapeDtypeStruct((share_rows, 2 * rank, LANES), jnp.bfloat16)
    current = {1: run(
        functools.partial(coeff_kernel, 1), state, (interp_in, samples), coeff_scratch, 2,
        in_specs=[pl.BlockSpec(memory_space=pl.ANY)] * 2, limit=START_LIMIT,
    )}
    for level in range(3):
        bit = 3 - level
        if level == 0:
            partner = {1: swapped(current[1], bit)}
            current[0], *wides = run(
                functools.partial(second_kernel, 0, 3, 0), [state] + [spread_out] * 4,
                (top_blocks, interp_in, samples, current[1]),
                coeff_scratch + (pltpu.VMEM((1, *top_blocks.shape[1:]), jnp.bfloat16), pltpu.SemaphoreType.DMA), 4,
                in_specs=[pl.BlockSpec(memory_space=pl.ANY)] * 4, limit=FETCH_LIMIT,
            )
            wides = wides[:2], wides[2:]
            partner[0] = swapped(current[0], bit)
            near = level_nears(top_pattern, level, bit, (1,), wides)
            near.update(level_nears(top_pattern, level, bit, (0,), wides))
            later_wides = {later: level_wides(top_blocks, later, 3 - later, near[0]) for later in (1, 2)}
            shared = run(
                functools.partial(share_kernel, 3), shared_shape,
                (top_blocks, top_pattern, bottom_blocks, bottom_pattern),
            )
        else:
            partner = {flip: swapped(current[flip], bit) for flip in (1, 0)}
            wides = later_wides[level]
            near = level_nears(top_pattern, level, bit, (1, 0), wides)
        if level < 2:
            current = level_fars(top_pattern, level, bit, (1, 0), wides, later_wides[2][0] if level == 0 else ())

    shared = run(
        functools.partial(send_kernel, 2, 1, 1), shared_shape, (top_pattern, partner[1], near[1], wides[1][1], shared), aliases={4: 0},
    )
    shared = swapped(shared, 0)
    pair_far, near_wide = run(
        functools.partial(pair_far_kernel, 3),
        [jax.ShapeDtypeStruct((2, rank, rhs_count, LANES), jnp.float32), pair_spread],
        (top_blocks, top_pattern, shared), (wide,), 2,
    )
    current = level_fars(top_pattern, 2, 1, (0,), wides, (pair_far,))

    piece = jax.ShapeDtypeStruct((2, 2, rank // fold * rhs_count, LANES), jnp.bfloat16)
    pieces = run(
        functools.partial(pair_near_kernel, 3, slot), [piece] * 4,
        (top_pattern, near_wide, current[0], pair_far), (total, packed), 2,
    )
    kept = pieces[0]
    pieces = [permuted(value, functools.partial(crossed, turn=turn)) for turn, value in enumerate(pieces)]
    own_wide, other_wide = run(wide_kernel, [pair_spread] * 2, (bottom_blocks, shared))
    wides = {level: level_wides(bottom_blocks, level, level, kept) for level in (1, 2, 3)}
    image_spread = jax.ShapeDtypeStruct((out_depth * rank, LANES), jnp.float32)
    image_wide = run(interp_kernel, [image_spread] * 2, (interp_out,))
    spreads = [wide for level in (1, 2, 3) for group in wides[level] for wide in group]
    second, states = run(
        functools.partial(open_kernel, slot), [state, jax.ShapeDtypeStruct((2, rank, rhs_count, LANES), jnp.bfloat16)],
        (other_wide, kept, *pieces, *spreads, *image_wide), (total, packed), 2,
    )
    current = {1: swapped(second, 0), 0: run(own_kernel, state, (bottom_pattern, own_wide, states), (total,), 2)}
    partner = {0: swapped(current[0], 1)}
    partner[1] = swapped(current[1], 1)
    for level in (1, 2, 3):
        if level > 1:
            partner = {flip: swapped(current[flip], level) for flip in (0, 1)}
        near = level_nears(bottom_pattern, level, level, (0, 1), wides[level])
        if level < 3:
            current = level_fars(bottom_pattern, level, level, (0, 1), wides[level])

    ready = run(
        functools.partial(first_image_kernel, 3, 3), jax.ShapeDtypeStruct((out_depth, rhs_count, LANES), jnp.bfloat16),
        (bottom_pattern, wides[3][1][0], image_wide[0], partner[0], near[0]), (total,), 3,
    )
    return run(
        functools.partial(last_kernel, 3, 3), jax.ShapeDtypeStruct((out_depth, rhs_count, box_count), jnp.bfloat16),
        (bottom_pattern, wides[3][1][1], image_wide[1], partner[1], near[1], ready),
        (pltpu.VMEM((out_depth, rhs_count, LANES), jnp.bfloat16), total, pltpu.SemaphoreType.DMA((5,))), 3,
        out_specs=[pl.BlockSpec(memory_space=pl.ANY)],
    )


def contract(weights, state):
    product = weights[:, :, None].astype(jnp.float32) * state[None].astype(jnp.float32)
    return jnp.sum(product, axis=1)


def plain_level(current, blocks, pattern, bit):
    rank = blocks.shape[0]
    partner = swapped(current, bit)
    is_lower = lax.axis_index("leaf") // 2**bit % 2 == 0
    lower = jnp.where(is_lower, current, partner)
    upper = jnp.where(is_lower, partner, current)
    weights = blocks * jnp.repeat(pattern, rank, axis=0).astype(jnp.bfloat16)[None]
    return contract(weights, jnp.concatenate([lower, upper], axis=0)).astype(jnp.bfloat16)


def plain_local(samples, interp_in, top_blocks, top_pattern, bottom_blocks, bottom_pattern, interp_out):
    bit_count = lax.axis_size("leaf").bit_length() - 1
    current = contract(interp_in, samples).astype(jnp.bfloat16)
    for level in range(top_blocks.shape[0]):
        current = plain_level(current, top_blocks[level], top_pattern[level], bit_count - 1 - level)
    flat = current.reshape(-1, current.shape[2])
    current = lax.all_to_all(flat, "leaf", split_axis=1, concat_axis=1, tiled=True).reshape(current.shape)
    for level in range(bottom_blocks.shape[0]):
        current = plain_level(current, bottom_blocks[level], bottom_pattern[level], level)
    return contract(interp_out, current).astype(jnp.bfloat16)


def local(samples, interp_in, top_blocks, *rest):
    four_digits = lax.axis_size("leaf") == 16 and top_blocks.shape[0] == 4
    chosen = fast_local if four_digits and samples.shape[1:] == (8, 2 * LANES) else plain_local
    return chosen(samples, interp_in, top_blocks, *rest)


def solution(mesh):
    boxes = ("parts", "leaf")
    return jax.shard_map(
        local,
        mesh=mesh,
        in_specs=(
            P(None, None, boxes),
            P(None, None, boxes),
            P(None, None, None, boxes),
            P(None, None, boxes),
            P(None, None, None, boxes),
            P(None, None, boxes),
            P(None, None, boxes),
        ),
        out_specs=P(None, None, boxes),
        check_vma=False,
    )
```
